32 devices in a mesh: tower: 2 (over y), dp: 16 (over z, x, core).
Axes of the slice: x: 2, y: 2, z: 4, core: 2. Of those that a mesh axis runs over, the one named last changes fastest.
Arguments:
- hidden: bfloat16 [2, 16, 2, 1024, 768], P('tower', 'dp'), may hold values from -6 to 6
- lengths: int32 [2, 16, 2, 16], P('tower', 'dp'), may hold values from 0 to 1024, as said below
- pairs: int32 [2, 16, 16], P(None, 'dp'), may hold values from 0 to 15
- out_grad: bfloat16 [2, 16, 2, 1024, 768], P('tower', 'dp'), may hold values from -6 to 6
- w_query: bfloat16 [768, 768], P(('tower', 'dp')), may hold values from -0.21875 to 0.21875
- w_key: bfloat16 [768, 768], P(('tower', 'dp')), may hold values from -0.21875 to 0.21875
- w_value: bfloat16 [768, 768], P(('tower', 'dp')), may hold values from -0.21875 to 0.21875
- w_attn_out: bfloat16 [768, 768], P(('tower', 'dp')), may hold values from -1.75 to 1.75
- w_in: bfloat16 [768, 3072], P(('tower', 'dp')), may hold values from -0.21875 to 0.21875
- w_out: bfloat16 [3072, 768], P(('tower', 'dp')), may hold values from -0.109375 to 0.109375
- w_proj: bfloat16 [768, 768], P(('tower', 'dp')), may hold values from -0.21875 to 0.21875
- gain_attn: float32 [768], replicated, may hold values from 0.5 to 1.5
- gain_ffn: float32 [768], replicated, may hold values from 0.5 to 1.5
- gain_final: float32 [768], replicated, may hold values from 0.5 to 1.5
- rel_bias: float32 [32, 12], replicated, may hold values from -4 to 4
Outputs:
- block_out: bfloat16 [2, 16, 2, 1024, 768], P('tower', 'dp')
- hidden_grad: float32 [2, 16, 2, 1024, 768], P('tower', 'dp')
- loss: float32 [], replicated
- grad_w_query: float32 [768, 768], P(('tower', 'dp'))
- grad_w_key: float32 [768, 768], P(('tower', 'dp'))
- grad_w_value: float32 [768, 768], P(('tower', 'dp'))
- grad_w_attn_out: float32 [768, 768], P(('tower', 'dp'))
- grad_w_in: float32 [768, 3072], P(('tower', 'dp'))
- grad_w_out: float32 [3072, 768], P(('tower', 'dp'))
- grad_w_proj: float32 [768, 768], P(('tower', 'dp'))
- grad_gain_attn: float32 [768], replicated
- grad_gain_ffn: float32 [768], replicated
- grad_gain_final: float32 [768], replicated
- grad_rel_bias: float32 [32, 12], replicated
The draws below stay inside these ranges and needn't reach their ends.
Inputs may be any that keep to these rules, and one draw needn't show every extreme that they name: lengths[0,r,m,s] is a query's length from 32 to 64 for every slot; lengths[1,r,m,0] is a document's length from 512 to 1024 and lengths[1,r,m,s] = 0 for s > 0; some query has 64 and some document 1024 rows in every draw.
All inputs are finite; a program needn't handle non-finite values.
Results may differ from the reference program's by a relative error of at most 0.015.
Values may be sent and summed in bfloat16 or wider, within the bound.
No kernel may reach another device: no remote copies, remote signals or barrier semaphores. Data moves between devices by JAX's collectives and lax.ppermute only.
A program may use at most 320 MiB of HBM per device.

```python
import jax
import jax.numpy as jnp
from jax import lax

D = 768
HEADS = 12
HEAD_DIM = 64
FF = 3072
BUCKETS = 32
DOC_LEN = 1024
SEGS = 16
MICRO = 2
N_DP = 16


def draw_lengths(key, part):
    key = jax.random.fold_in(key, 7)
    subkeys = jax.random.split(key, 4)
    query_most = DOC_LEN // SEGS
    query_count = N_DP * MICRO * SEGS
    query_len = jax.random.randint(subkeys[0], (query_count,), query_most // 2, query_most + 1)
    query_len = query_len.at[jax.random.randint(subkeys[1], (), 0, query_count)].set(query_most)
    doc_len = jax.random.randint(subkeys[2], (N_DP * MICRO,), DOC_LEN // 2, DOC_LEN + 1)
    doc_len = doc_len.at[jax.random.randint(subkeys[3], (), 0, N_DP * MICRO)].set(DOC_LEN)
    first_slot = jnp.arange(SEGS) == 0
    doc_slots = jnp.where(first_slot[None, :], doc_len[:, None], 0)
    return jnp.stack([query_len.reshape(N_DP, MICRO, SEGS), doc_slots.reshape(N_DP, MICRO, SEGS)]).astype(jnp.int32)


def plant(drawn, key, low, largest):
    place = [jax.random.randint(jax.random.fold_in(key, axis), (), 0, length) for axis, length in enumerate(drawn.shape)]
    main_axis = drawn.shape.index(max(drawn.shape))
    next_to = place[:main_axis] + [(place[main_axis] + 1) % drawn.shape[main_axis]] + place[main_axis + 1:]
    return drawn.at[tuple(place)].set(low).at[tuple(next_to)].set(largest)


def level_of(rng, extent, cuts, least, top_value):
    def one(axis_at, parts):
        heights = jax.random.uniform(jax.random.fold_in(jax.random.fold_in(rng, 6), axis_at), (parts,), jnp.float32, least / len(cuts), top_value / len(cuts))
        return jnp.repeat(jnp.exp(heights), extent[axis_at] // parts).reshape((-1,) + (1,) * (len(extent) - axis_at - 1))

    loudness = one(*cuts[0])
    for cut in cuts[1:]:
        loudness = loudness * one(*cut)
    return loudness


def gaussian(own_key, shape, spread, reach, shards=(), held_as=jnp.bfloat16):
    entries = spread * jax.random.normal(own_key, shape, jnp.float32)
    if shards:
        entries = entries * level_of(own_key, shape, shards, -0.22, 0.18)
    return jnp.clip(entries, -reach, reach).astype(held_as)


def setup_inputs(seed: int = 0) -> dict:
    keys = jax.random.split(jax.random.key(seed), 16)
    return {
        "hidden": gaussian(keys[0], (2, N_DP, MICRO, DOC_LEN, D), 1.0, 6.0, ((0, 2), (1, 16))),
        "lengths": draw_lengths(jax.random.fold_in(keys[15], 71), 0),
        "pairs": plant(jax.random.randint(keys[2], (MICRO, N_DP, SEGS), 0, N_DP), jax.random.fold_in(keys[2], 1), 0, N_DP - 1).astype(jnp.int32),
        "out_grad": gaussian(keys[3], (2, N_DP, MICRO, DOC_LEN, D), 1.0, 6.0, ((0, 2), (1, 16))),
        "w_query": gaussian(keys[4], (D, D), D ** -0.5, 0.21875, ((0, 32),)),
        "w_key": gaussian(keys[5], (D, D), D ** -0.5, 0.21875, ((0, 32),)),
        "w_value": gaussian(keys[6], (D, D), D ** -0.5, 0.21875, ((0, 32),)),
        "w_attn_out": gaussian(keys[7], (D, D), (D // 64) ** -0.5, 1.75, ((0, 32),)),
        "w_in": gaussian(keys[8], (D, FF), D ** -0.5, 0.21875, ((0, 32),)),
        "w_out": gaussian(keys[9], (FF, D), FF ** -0.5, 0.109375, ((0, 32),)),
        "w_proj": gaussian(keys[10], (D, D), D ** -0.5, 0.21875, ((0, 32),)),
        "gain_attn": jnp.clip(1.0 + 0.1 * jax.random.normal(keys[11], (D,), jnp.float32), 0.5, 1.5),
        "gain_ffn": jnp.clip(1.0 + 0.1 * jax.random.normal(keys[12], (D,), jnp.float32), 0.5, 1.5),
        "gain_final": jnp.clip(1.0 + 0.1 * jax.random.normal(keys[13], (D,), jnp.float32), 0.5, 1.5),
        "rel_bias": gaussian(keys[14], (BUCKETS, HEADS), 1.0, 4.0, (), jnp.float32),
    }


bucket_steps = (12, 16, 23, 32, 46, 64, 91)
score_scale = 0.125
logit_scale = 64.0
negative = -1e+30

@jax.custom_vjp
def low(v):
    return lax.optimization_barrier(v.astype(jnp.bfloat16)).astype(jnp.float32)

@jax.custom_vjp
def low_back(v):
    return v

def low_keep(v):
    return (low(v), None)

def low_pass(kept, grad):
    return (grad,)

def back_keep(v):
    return (v, None)

def back_low(kept, grad):
    return (low(grad),)
low.defvjp(low_keep, low_pass)
low_back.defvjp(back_keep, back_low)

def rms_norm(activation, gain_vec):
    return activation * lax.rsqrt(lax.optimization_barrier(jnp.mean(activation * activation, axis=-1, keepdims=True)) + 1e-06) * gain_vec

def unit_norm(vector):
    return vector * lax.rsqrt(lax.optimization_barrier(jnp.sum(vector * vector, axis=-1, keepdims=True)) + 1e-06)

def bucket_ids(offset):
    distance = jnp.abs(offset)
    far_bucket = jnp.full(offset.shape, 8, jnp.int32)
    for threshold in bucket_steps:
        far_bucket = far_bucket + (distance >= threshold).astype(jnp.int32)
    bucket = jnp.where(distance < 8, distance, far_bucket)
    return bucket + 16 * (offset > 0).astype(jnp.int32)

def layout(lengths_row, is_doc, row_count):
    slot_count = lengths_row.shape[0]
    spacing = row_count // slot_count
    positions = jnp.arange(row_count, dtype=jnp.int32)
    slot_starts = jnp.where(is_doc, 0, jnp.arange(slot_count, dtype=jnp.int32) * spacing)
    member = (positions[None, :] >= slot_starts[:, None]) & (positions[None, :] < (slot_starts + lengths_row)[:, None])
    segment = jnp.where(is_doc, 0, positions // spacing)
    usable = jnp.any(member, axis=0)
    return (member, segment, usable)

def slab_forward(stream, lengths_row, doc_flag, params):
    query_weight, key_weight, value_weight, attn_weight, inner_weight, outer_weight, proj_weight, gain_one, gain_two, gain_three, bias_table = params
    highest = lax.Precision.HIGHEST
    member, segment, usable = layout(lengths_row, doc_flag == 1, DOC_LEN)
    attn_in = low(rms_norm(stream, gain_one))
    queries = low(low_back(jnp.dot(attn_in, query_weight, precision=highest))).reshape(DOC_LEN, HEADS, HEAD_DIM)
    keys_all = low(low_back(jnp.dot(attn_in, key_weight, precision=highest))).reshape(DOC_LEN, HEADS, HEAD_DIM)
    values_all = low(low_back(jnp.dot(attn_in, value_weight, precision=highest))).reshape(DOC_LEN, HEADS, HEAD_DIM)
    positions = jnp.arange(DOC_LEN, dtype=jnp.int32)
    offset = positions[None, :] - positions[:, None]
    pos_bias = jnp.transpose(bias_table[bucket_ids(offset)], (2, 0, 1))
    scores = score_scale * jnp.einsum('ihd,jhd->hij', queries, keys_all, precision=highest) + pos_bias
    scores = low_back(scores)
    allowed = (segment[:, None] == segment[None, :]) & usable[None, :]
    attn_probs = low(jax.nn.softmax(jnp.where(allowed[None], scores, negative), axis=-1))
    mixed_out = jnp.einsum('hij,jhd->ihd', attn_probs, values_all, precision=highest).reshape(DOC_LEN, D)
    mixed_out = low(low_back(mixed_out))
    after_attn = stream + low_back(jnp.dot(mixed_out, attn_weight, precision=highest))
    ffn_in = low(rms_norm(after_attn, gain_two))
    pre_act = low_back(jnp.dot(ffn_in, inner_weight, precision=highest))
    activated = low(jax.nn.gelu(pre_act, approximate=True))
    block_value = after_attn + low_back(jnp.dot(activated, outer_weight, precision=highest))
    normed_three = rms_norm(block_value, gain_three)
    member_f = member.astype(jnp.float32)
    counts = jnp.maximum(lax.optimization_barrier(jnp.sum(member_f, axis=1)), 1.0)
    pooled = low(lax.optimization_barrier(jnp.sum(member_f[:, :, None] * normed_three[None], axis=1)) / counts[:, None])
    projected = low_back(jnp.dot(pooled, proj_weight, precision=highest))
    return (block_value, unit_norm(projected))

def reference(hidden, lengths, pairs, out_grad, w_query, w_key, w_value, w_attn_out, w_in, w_out, w_proj, gain_attn, gain_ffn, gain_final, rel_bias):
    params = (w_query.astype(jnp.float32), w_key.astype(jnp.float32), w_value.astype(jnp.float32), w_attn_out.astype(jnp.float32), w_in.astype(jnp.float32), w_out.astype(jnp.float32), w_proj.astype(jnp.float32), gain_attn.astype(jnp.float32), gain_ffn.astype(jnp.float32), gain_final.astype(jnp.float32), rel_bias.astype(jnp.float32))
    inputs = hidden.astype(jnp.float32)
    slab_total = 2 * N_DP * MICRO
    flat_lengths = lengths.reshape(slab_total, SEGS)
    doc_flags = jnp.repeat(jnp.array([0, 1], jnp.int32), N_DP * MICRO)

    def forward(inputs, params):
        flat = inputs.reshape(slab_total, DOC_LEN, D)

        def one_slab(running, slab_item):
            slab_rows, lengths_row, doc_flag = slab_item
            block_value, embed = jax.checkpoint(slab_forward)(slab_rows, lengths_row, doc_flag, params)
            return (running, (block_value, embed))
        _, (outputs, embeds) = lax.scan(one_slab, jnp.int32(0), (flat, flat_lengths, doc_flags))
        embeds = low(embeds).reshape(2, N_DP, MICRO, SEGS, D)
        loss_sum = jnp.zeros((), jnp.float32)
        for batch in range(MICRO):
            queries = embeds[0, :, batch].reshape(N_DP * SEGS, D)
            documents = embeds[1, :, batch, 0]
            logits = low_back(logit_scale * jnp.dot(queries, documents.T, precision=lax.Precision.HIGHEST))
            log_total = jax.nn.logsumexp(logits, axis=-1)
            chosen = jnp.take_along_axis(logits, pairs[batch].reshape(N_DP * SEGS, 1).astype(jnp.int32), axis=1)[:, 0]
            loss_sum = loss_sum + jnp.sum(log_total - chosen)
        return (outputs.reshape(2, N_DP, MICRO, DOC_LEN, D), loss_sum)
    (outputs, loss_sum), pullback = jax.vjp(forward, inputs, params)
    grad_in, grads = pullback((out_grad.astype(outputs.dtype), jnp.ones_like(loss_sum)))
    loss_mean = loss_sum / (N_DP * SEGS * MICRO)
    return (outputs.astype(jnp.bfloat16), grad_in, loss_mean, grads[0], grads[1], grads[2], grads[3], grads[4], grads[5], grads[6], grads[7], grads[8], grads[9], grads[10])
```

```python
import jax
import jax.numpy as jnp
from jax import lax
from jax.experimental import pallas as pl
from jax.experimental.pallas import tpu as pltpu
from jax.sharding import Mesh, PartitionSpec as P

bucket_steps = (12, 16, 23, 32, 46, 64, 91)
score_scale = 0.125
logit_scale = 64.0
negative = -1e30
MICRO = 2
TILE = 128
WIDE = 256
GROUP = 64

BF = jnp.bfloat16
F32 = jnp.float32
NN = (((1,), (0,)), ((), ()))
NT = (((1,), (1,)), ((), ()))
TN = (((0,), (0,)), ((), ()))
GELU_A = 0.7978845608028654
GELU_B = 0.044715


def mm(a, b, dims=NN):
    return lax.dot_general(a, b, dims, preferred_element_type=F32)


def params(megabytes):
    return pltpu.CompilerParams(vmem_limit_bytes=megabytes << 20)


def fixed(shape):
    zeros = (0,) * len(shape)
    return pl.BlockSpec(shape, lambda *_: zeros, pipeline_mode=pl.Buffered(1))


def cost(flops, data):
    return pl.CostEstimate(flops=int(flops), bytes_accessed=int(data), transcendentals=0)


def unit_norm(vector):
    return vector * lax.rsqrt(jnp.sum(vector * vector, axis=-1, keepdims=True) + 1e-06)


def bucket_ids(offset):
    distance = jnp.abs(offset)
    far_bucket = jnp.full(offset.shape, 8, jnp.int32)
    for threshold in bucket_steps:
        far_bucket = far_bucket + (distance >= threshold).astype(jnp.int32)
    bucket = jnp.where(distance < 8, distance, far_bucket)
    return bucket + 16 * (offset > 0).astype(jnp.int32)


def qkv_kernel(x_ref, gain_ref, w_ref, a1_ref, qkv_ref):
    x = x_ref[...].astype(F32)
    r = lax.rsqrt(jnp.mean(x * x, axis=-1, keepdims=True) + 1e-06)
    a1 = (x * r * gain_ref[...]).astype(BF)
    a1_ref[...] = a1
    width = a1.shape[1]
    for part in range(3):
        out = mm(a1, w_ref[:, part * width : (part + 1) * width]).astype(BF)
        if part == 0:
            out = out * BF(score_scale)
        qkv_ref[:, part * width : (part + 1) * width] = out


def project_qkv(x, gain, w):
    rows, width = x.shape
    block = 256
    return pl.pallas_call(
        qkv_kernel,
        grid=(rows // block,),
        in_specs=[
            pl.BlockSpec((block, width), lambda i: (i, 0)),
            fixed((1, width)),
            fixed(w.shape),
        ],
        out_specs=[
            pl.BlockSpec((block, width), lambda i: (i, 0)),
            pl.BlockSpec((block, 3 * width), lambda i: (i, 0)),
        ],
        out_shape=[
            jax.ShapeDtypeStruct((rows, width), BF),
            jax.ShapeDtypeStruct((rows, 3 * width), BF),
        ],
        compiler_params=params(40),
        cost_estimate=cost(6 * rows * width * width, rows * width * 10),
        name="norm_qkv",
    )(x, gain, w)


def lane_half(shape, head):
    lane = lax.broadcasted_iota(jnp.int32, shape, 1)
    return (lane // GROUP) == head


def key_extras(rows, length):
    row = lax.broadcasted_iota(jnp.int32, (rows, TILE), 0)
    col = lax.broadcasted_iota(jnp.int32, (rows, TILE), 1)
    block = row // TILE
    hit = (col - 1 == block) | (col - 1 - rows // TILE == block)
    ones = jnp.where(hit & (col > 0), 1.0, 0.0)
    return jnp.where(col == 0, jnp.where(row < length, 0.0, negative), ones).astype(BF)


def query_mask(info_ref, tile):
    row = lax.broadcasted_iota(jnp.int32, (TILE, TILE), 0)
    col = lax.broadcasted_iota(jnp.int32, (TILE, TILE), 1)
    per = TILE // GROUP
    good = jnp.zeros((TILE, TILE), jnp.bool_)
    for s in range(per):
        low = s * GROUP
        inside = (row >= low) & (row < low + info_ref[2 + tile * per + s])
        good = good | (inside & (col >= low) & (col < low + GROUP))
    return good


def attn_fwd_kernel(
    info_ref, q_ref, k_ref, v_ref, eq_ref, t_ref, o_ref, p_ref, linv_ref, s_scr, ot_scr
):
    rows = q_ref.shape[0]
    tiles = rows // TILE
    vt = v_ref[...].T

    def ones_below(head):
        return jnp.concatenate(
            [vt[head * GROUP : (head + 1) * GROUP, :], jnp.ones((16, rows), BF)], axis=0
        )

    @pl.when(info_ref[0] == 1)
    def _():
        keys = jnp.concatenate([k_ref[...], key_extras(rows, info_ref[1])], axis=1)
        for head in range(2):
            va = ones_below(head)
            masked = jnp.where(lane_half((rows, TILE), head), q_ref[...], BF(0))
            for wide in range(rows // WIDE):
                cols = slice(wide * WIDE, (wide + 1) * WIDE)
                tags = [
                    jnp.broadcast_to(eq_ref[head, qb : qb + 1, :], (TILE, TILE))
                    for qb in range(wide * WIDE // TILE, (wide + 1) * WIDE // TILE)
                ]
                qa = jnp.concatenate([masked[cols, :], jnp.concatenate(tags, axis=0)], axis=1)
                slot = (head * (rows // WIDE) + wide) % 2
                s_scr[slot] = mm(keys, qa, NT)
                for kb in range(tiles):
                    for sub in range(WIDE // TILE):
                        delta = kb - (wide * WIDE // TILE + sub)
                        if abs(delta) <= 1:
                            at = (
                                slot,
                                slice(kb * TILE, (kb + 1) * TILE),
                                slice(sub * TILE, (sub + 1) * TILE),
                            )
                            s_scr[at] = s_scr[at] + t_ref[head, delta + 1]
                top = s_scr[slot, 0:TILE, :]
                for kb in range(1, tiles):
                    top = jnp.maximum(top, s_scr[slot, kb * TILE : (kb + 1) * TILE, :])
                top = jnp.max(top, axis=0, keepdims=True)
                for kb in range(tiles):
                    at = slice(kb * TILE, (kb + 1) * TILE)
                    p_ref[head, at, cols] = jnp.exp(s_scr[slot, at, :] - top).astype(BF)
                out = mm(va, p_ref[head, :, cols])
                inv = 1.0 / out[GROUP : GROUP + 1, :]
                ot_scr[head * GROUP : (head + 1) * GROUP, cols] = out[:GROUP, :] * inv
                linv_ref[0, head : head + 1, cols] = inv

    @pl.when(info_ref[0] == 0)
    def _():
        for tile in range(tiles):
            at = slice(tile * TILE, (tile + 1) * TILE)
            good = query_mask(info_ref, tile)
            for head in range(2):
                va = ones_below(head)[:, at]
                masked = jnp.where(lane_half((TILE, TILE), head), q_ref[at, :], BF(0))
                s = mm(k_ref[at, :], masked, NT) + t_ref[head, 1]
                s = jnp.where(good, s, negative)
                top = jnp.max(s, axis=0, keepdims=True)
                p = jnp.exp(s - top).astype(BF)
                p_ref[head, at, at] = p
                out = mm(va, p)
                inv = 1.0 / out[GROUP : GROUP + 1, :]
                ot_scr[head * GROUP : (head + 1) * GROUP, at] = out[:GROUP, :] * inv
                linv_ref[0, head : head + 1, at] = inv

    o_ref[...] = ot_scr[...].T.astype(BF)


def attention(info, qkv, tags, near, heads):
    rows = qkv.shape[0]
    width = qkv.shape[1] // 3
    pairs = heads // 2
    return pl.pallas_call(
        attn_fwd_kernel,
        grid_spec=pltpu.PrefetchScalarGridSpec(
            num_scalar_prefetch=1,
            grid=(pairs,),
            in_specs=[
                pl.BlockSpec((rows, TILE), lambda i, _: (0, i)),
                pl.BlockSpec((rows, TILE), lambda i, _: (0, pairs + i)),
                pl.BlockSpec((rows, TILE), lambda i, _: (0, 2 * pairs + i)),
                pl.BlockSpec((2,) + tags.shape[1:], lambda i, _: (i, 0, 0)),
                pl.BlockSpec((2,) + near.shape[1:], lambda i, _: (i, 0, 0, 0)),
            ],
            out_specs=[
                pl.BlockSpec((rows, TILE), lambda i, _: (0, i)),
                pl.BlockSpec((2, rows, rows), lambda i, _: (i, 0, 0)),
                pl.BlockSpec((1, 2, rows), lambda i, _: (i, 0, 0)),
            ],
            scratch_shapes=[pltpu.VMEM((2, rows, WIDE), F32), pltpu.VMEM((TILE, rows), F32)],
        ),
        out_shape=[
            jax.ShapeDtypeStruct((rows, width), BF),
            jax.ShapeDtypeStruct((heads, rows, rows), BF),
            jax.ShapeDtypeStruct((pairs, 2, rows), F32),
        ],
        compiler_params=params(48),
        cost_estimate=cost(heads * rows * rows * 512, heads * rows * rows * 2),
        name="attention_forward",
    )(info, qkv, qkv, qkv, tags, near)


def attn_bwd_kernel(
    info_ref,
    q_ref,
    k_ref,
    v_ref,
    o_ref,
    do_ref,
    p_ref,
    linv_ref,
    dqkv_ref,
    near_ref,
    far_ref,
    ds_scr,
    dqt_scr,
):
    rows = q_ref.shape[0]
    tiles = rows // TILE
    col = lax.broadcasted_iota(jnp.int32, (rows, TILE), 1)
    kt = k_ref[...].T
    scale = jnp.concatenate([linv_ref[0], jnp.zeros((6, rows), F32)], axis=0).T
    d_out = do_ref[...].astype(F32)
    prod = d_out * o_ref[...].astype(F32)
    values = jnp.concatenate([v_ref[...], jnp.where(col < 2, 1.0, 0.0).astype(BF)], axis=1)

    def prepare(head):
        mine = lane_half((rows, TILE), head)
        inv = scale[:, head : head + 1]
        scaled = jnp.where(mine, d_out * inv, 0.0).astype(BF)
        shift = -jnp.sum(jnp.where(mine, prod, 0.0), axis=1, keepdims=True) * inv
        high = shift.astype(BF)
        rest = (shift - high.astype(F32)).astype(BF)
        extra = jnp.where(col == 0, high, jnp.where(col == 1, rest, BF(0)))
        masked = jnp.where(mine, q_ref[...], BF(0))
        return scaled, jnp.concatenate([scaled, extra], axis=1), masked

    @pl.when(info_ref[0] == 1)
    def _():
        block = lax.broadcasted_iota(jnp.int32, (16, rows), 1) // TILE
        place = lax.broadcasted_iota(jnp.int32, (16, rows), 0)
        marks = jnp.where(block == place, 1.0, 0.0).astype(BF)
        dk = jnp.zeros((rows, TILE), F32)
        dv = jnp.zeros((rows, TILE), F32)
        for head in range(2):
            scaled, outer, masked = prepare(head)
            ka = jnp.concatenate([kt[head * GROUP : (head + 1) * GROUP, :], marks], axis=0)
            for wide in range(rows // WIDE):
                cols = slice(wide * WIDE, (wide + 1) * WIDE)
                dp = mm(values, outer[cols, :], NT)
                ds = (p_ref[head, :, cols].astype(F32) * dp).astype(BF)
                ds_scr[head, :, cols] = ds
                out = mm(ka, ds)
                dqt_scr[head * GROUP : (head + 1) * GROUP, cols] = out[:GROUP, :] * score_scale
                far_ref[0, head, :, cols] = out[GROUP : GROUP + tiles, :]
            dv = dv + mm(p_ref[head], scaled)
            dk = dk + mm(ds_scr[head], masked)
            for delta in (-1, 0, 1):
                total = None
                for qb in range(tiles):
                    kb = qb + delta
                    if 0 <= kb < tiles:
                        part = ds_scr[
                            head, kb * TILE : (kb + 1) * TILE, qb * TILE : (qb + 1) * TILE
                        ].astype(F32)
                        total = part if total is None else total + part
                near_ref[head, delta + 1] = total
        dqkv_ref[1] = dk.astype(BF)
        dqkv_ref[2] = dv.astype(BF)

    @pl.when(info_ref[0] == 0)
    def _():
        far_ref[...] = jnp.zeros(far_ref.shape, F32)
        near_ref[...] = jnp.zeros(near_ref.shape, F32)
        for head in range(2):
            scaled, outer, masked = prepare(head)
            total = None
            for tile in range(tiles):
                at = slice(tile * TILE, (tile + 1) * TILE)
                p = p_ref[head, at, at]
                dp = mm(values[at, :], outer[at, :], NT)
                part = p.astype(F32) * dp
                ds = part.astype(BF)
                total = part if total is None else total + part
                out = mm(kt[head * GROUP : (head + 1) * GROUP, at], ds)
                dqt_scr[head * GROUP : (head + 1) * GROUP, at] = out * score_scale
                dk = mm(ds, masked[at, :])
                dv = mm(p, scaled[at, :])
                if head == 0:
                    ds_scr[0, at, 0:TILE] = dk.astype(BF)
                    ds_scr[1, at, 0:TILE] = dv.astype(BF)
                else:
                    dqkv_ref[1, at, :] = ds_scr[0, at, 0:TILE] + dk.astype(BF)
                    dqkv_ref[2, at, :] = ds_scr[1, at, 0:TILE] + dv.astype(BF)
            near_ref[head, 1] = total

    dqkv_ref[0] = dqt_scr[...].T.astype(BF)


def attention_back(info, qkv, mixed, d_mixed, probs, linv):
    rows = qkv.shape[0]
    width = qkv.shape[1] // 3
    pairs = linv.shape[0]
    heads = 2 * pairs
    tiles = rows // TILE
    return pl.pallas_call(
        attn_bwd_kernel,
        grid_spec=pltpu.PrefetchScalarGridSpec(
            num_scalar_prefetch=1,
            grid=(pairs,),
            in_specs=[
                pl.BlockSpec((rows, TILE), lambda i, _: (0, i)),
                pl.BlockSpec((rows, TILE), lambda i, _: (0, pairs + i)),
                pl.BlockSpec((rows, TILE), lambda i, _: (0, 2 * pairs + i)),
                pl.BlockSpec((rows, TILE), lambda i, _: (0, i)),
                pl.BlockSpec((rows, TILE), lambda i, _: (0, i)),
                pl.BlockSpec((2, rows, rows), lambda i, _: (i, 0, 0)),
                pl.BlockSpec((1, 2, rows), lambda i, _: (i, 0, 0)),
            ],
            out_specs=[
                pl.BlockSpec((3, rows, TILE), lambda i, _: (0, 0, i)),
                pl.BlockSpec((2, 3, TILE, TILE), lambda i, _: (i, 0, 0, 0)),
                pl.BlockSpec((1, 2, tiles, rows), lambda i, _: (i, 0, 0, 0)),
            ],
            scratch_shapes=[pltpu.VMEM((2, rows, rows), BF), pltpu.VMEM((TILE, rows), F32)],
        ),
        out_shape=[
            jax.ShapeDtypeStruct((3, rows, width), BF),
            jax.ShapeDtypeStruct((heads, 3, TILE, TILE), F32),
            jax.ShapeDtypeStruct((pairs, 2, tiles, rows), F32),
        ],
        compiler_params=params(56),
        cost_estimate=cost(heads * rows * rows * 1024, heads * rows * rows * 2),
        name="attention_backward",
    )(info, qkv, qkv, qkv, mixed, d_mixed, probs, linv)


def usable_rows(glen_ref, first, rows):
    row = lax.broadcasted_iota(jnp.int32, (rows, 1), 0)
    good = jnp.zeros((rows, 1), jnp.bool_)
    for g in range(rows // GROUP):
        low = g * GROUP
        good = good | ((row >= low) & (row < low + glen_ref[first + g]))
    return good


def ffn_fwd_kernel(
    glen_ref,
    x_ref,
    mixed_ref,
    w_ref,
    gain2_ref,
    gain3_ref,
    x1_ref,
    a2_ref,
    act_ref,
    slope_ref,
    x2_ref,
    out_ref,
    pool_ref,
):
    rows, width = x_ref.shape
    last = w_ref.shape[1] - 2 * width
    x1 = x_ref[...].astype(F32) + mm(mixed_ref[...], w_ref[:, last : last + width])
    x1_ref[...] = x1
    r = lax.rsqrt(jnp.mean(x1 * x1, axis=-1, keepdims=True) + 1e-06)
    a2 = (x1 * r * gain2_ref[...]).astype(BF)
    a2_ref[...] = a2
    total = x1
    for c in range(last // (2 * width)):
        at = slice(c * width, (c + 1) * width)
        into = 2 * c * width
        pre = mm(a2, w_ref[:, into : into + width])
        sq = pre * pre
        tanh = jnp.tanh(pre * (sq * (GELU_A * GELU_B) + GELU_A))
        half = 0.5 * tanh + 0.5
        act = pre * half
        slope = half + 2.0 * act * (1.0 - half) * (sq * (3 * GELU_A * GELU_B) + GELU_A)
        act = act.astype(BF)
        act_ref[:, at] = act
        slope_ref[:, at] = slope.astype(BF)
        total = total + mm(act, w_ref[:, into + width : into + 2 * width])
    x2_ref[...] = total
    out_ref[...] = total.astype(BF)
    r3 = lax.rsqrt(jnp.mean(total * total, axis=-1, keepdims=True) + 1e-06)
    a3 = total * r3 * gain3_ref[...]
    a3 = jnp.where(usable_rows(glen_ref, pl.program_id(0) * (rows // GROUP), rows), a3, 0.0)
    for g in range(rows // GROUP):
        pool_ref[0, g : g + 1, :] = jnp.sum(
            a3[g * GROUP : (g + 1) * GROUP, :], axis=0, keepdims=True
        )


def ffn_forward(glen, x, mixed, w_all, gain2, gain3):
    rows, width = x.shape
    ff = w_all.shape[1] // 2 - width
    block = 256
    groups = block // GROUP
    spec = pl.BlockSpec((block, width), lambda i, _: (i, 0))
    wide = pl.BlockSpec((block, ff), lambda i, _: (i, 0))
    out = pl.pallas_call(
        ffn_fwd_kernel,
        grid_spec=pltpu.PrefetchScalarGridSpec(
            num_scalar_prefetch=1,
            grid=(rows // block,),
            in_specs=[
                spec,
                spec,
                fixed(w_all.shape),
                fixed((1, width)),
                fixed((1, width)),
            ],
            out_specs=[
                spec,
                spec,
                wide,
                wide,
                spec,
                spec,
                pl.BlockSpec((1, groups, width), lambda i, _: (i, 0, 0)),
            ],
        ),
        out_shape=[
            jax.ShapeDtypeStruct((rows, width), F32),
            jax.ShapeDtypeStruct((rows, width), BF),
            jax.ShapeDtypeStruct((rows, ff), BF),
            jax.ShapeDtypeStruct((rows, ff), BF),
            jax.ShapeDtypeStruct((rows, width), F32),
            jax.ShapeDtypeStruct((rows, width), BF),
            jax.ShapeDtypeStruct((rows // block, groups, width), F32),
        ],
        compiler_params=params(56),
        cost_estimate=cost(2 * rows * width * (width + 2 * ff), rows * width * 40),
        name="ffn_forward",
    )(glen, x, mixed, w_all, gain2, gain3)
    return *out[:6], out[6].reshape(rows // GROUP, width)


def norm_back(x, gain, grad):
    r = lax.rsqrt(jnp.mean(x * x, axis=-1, keepdims=True) + 1e-06)
    hat = x * r
    d_gain = jnp.sum(grad * hat, axis=0, keepdims=True)
    d_hat = grad * gain
    dx = r * (d_hat - hat * jnp.mean(d_hat * hat, axis=-1, keepdims=True))
    return dx, d_gain


def ffn_bwd_kernel(second):
    def kernel(*refs):
        (
            glen_ref,
            x2_ref,
            cot_ref,
            dpool_ref,
            x1_ref,
            a2_ref,
            mixed_ref,
            act_ref,
            slope_ref,
            w_ref,
            gain2_ref,
            gain3_ref,
        ) = refs[:12]
        rest = refs[12:]
        if second:
            before_ref, gproj_ref = rest[:2]
            rest = rest[2:]
        (
            g_ref,
            dx1_ref,
            dmixed_ref,
            ggain_ref,
            dx2_scr,
            dy2_scr,
            da2_scr,
            dpre_scr,
        ) = rest
        rows, width = x2_ref.shape
        step = pl.program_id(0)
        last = pl.num_programs(0) - 1
        block = 256
        left, right = slice(0, width), slice(width, 2 * width)

        def put(side, value):
            if second:
                value = value + before_ref[:, side]
            g_ref[:, side] = value.astype(g_ref.dtype)

        @pl.when(step == 0)
        def _():
            gain = jnp.zeros((1, width), F32)
            for b in range(rows // block):
                at = slice(b * block, (b + 1) * block)
                per = block // GROUP
                grad = jnp.concatenate(
                    [
                        jnp.broadcast_to(dpool_ref[b * per + g : b * per + g + 1, :], (GROUP, width))
                        for g in range(per)
                    ],
                    axis=0,
                )
                grad = jnp.where(usable_rows(glen_ref, b * per, block), grad, 0.0)
                dx, d_gain = norm_back(x2_ref[at, :], gain3_ref[...], grad)
                gain = gain + d_gain
                dx = dx + cot_ref[at, :].astype(F32)
                dx2_scr[at, :] = dx
                dy2_scr[at, :] = dx.astype(BF)
            ggain_ref[1:2, :] = gain
            da2_scr[...] = jnp.zeros_like(da2_scr)

        @pl.when(step < last)
        def _():
            dact = mm(dy2_scr[...], w_ref[:, right], NT)
            dpre_scr[...] = (dact * slope_ref[...].astype(F32)).astype(BF)
            put(right, mm(act_ref[...], dy2_scr[...], TN))
            put(left, mm(a2_ref[...], dpre_scr[...], TN))
            da2_scr[...] = da2_scr[...] + mm(dpre_scr[...], w_ref[:, left], NT)

        @pl.when(step == last)
        def _():
            gain = jnp.zeros((1, width), F32)
            for b in range(rows // block):
                at = slice(b * block, (b + 1) * block)
                dx, d_gain = norm_back(x1_ref[at, :], gain2_ref[...], da2_scr[at, :])
                gain = gain + d_gain
                dx = dx + dx2_scr[at, :]
                dx1_ref[at, :] = dx
                dy2_scr[at, :] = dx.astype(BF)
            ggain_ref[0:1, :] = gain
            put(left, mm(mixed_ref[...], dy2_scr[...], TN))
            if second:
                g_ref[:, right] = gproj_ref[...]
            dmixed_ref[...] = mm(dy2_scr[...], w_ref[:, left], NT).astype(BF)

    return kernel


def ffn_backward(
    glen, x2, cot, dpool, x1, a2, mixed, act, slope, w_all, gain2, gain3, before, gproj
):
    rows, width = x2.shape
    chunks = w_all.shape[1] // (2 * width) - 1
    ff = chunks * width
    second = before is not None
    side = pl.BlockSpec((rows, width), lambda i, _: (0, jnp.minimum(i, chunks - 1)))
    part = pl.BlockSpec((width, 2 * width), lambda i, _: (0, i))
    in_specs = [
        fixed((rows, width)),
        fixed((rows, width)),
        fixed(dpool.shape),
        fixed((rows, width)),
        fixed((rows, width)),
        fixed((rows, width)),
        side,
        side,
        part,
        fixed((1, width)),
        fixed((1, width)),
    ]
    operands = [x2, cot, dpool, x1, a2, mixed, act, slope, w_all, gain2, gain3]
    if second:
        in_specs += [part, fixed((width, width))]
        operands += [before, gproj]
    return pl.pallas_call(
        ffn_bwd_kernel(second),
        grid_spec=pltpu.PrefetchScalarGridSpec(
            num_scalar_prefetch=1,
            grid=(chunks + 1,),
            in_specs=in_specs,
            out_specs=[
                part,
                fixed((rows, width)),
                fixed((rows, width)),
                fixed((2, width)),
            ],
            scratch_shapes=[
                pltpu.VMEM((rows, width), F32),
                pltpu.VMEM((rows, width), BF),
                pltpu.VMEM((rows, width), F32),
                pltpu.VMEM((rows, width), BF),
            ],
        ),
        out_shape=[
            jax.ShapeDtypeStruct(w_all.shape, BF if second else F32),
            jax.ShapeDtypeStruct((rows, width), F32),
            jax.ShapeDtypeStruct((rows, width), BF),
            jax.ShapeDtypeStruct((2, width), F32),
        ],
        compiler_params=params(60),
        cost_estimate=cost(4 * rows * width * (width + 2 * ff), rows * width * 60),
        name="ffn_backward",
    )(glen, *operands)


def qkv_weight_kernel(a1_ref, d0_ref, d1_ref, w_ref, g_ref, gain_ref):
    rows, width = d0_ref.shape[1:]
    total = mm(a1_ref[0:rows, :], d0_ref[0], TN) + mm(a1_ref[rows:, :], d1_ref[0], TN)
    g_ref[...] = total.astype(BF)
    prod = total * w_ref[...].astype(F32)
    part = prod[:, 0:TILE]
    for lane in range(1, width // TILE):
        part = part + prod[:, lane * TILE : (lane + 1) * TILE]

    @pl.when(pl.program_id(0) == 0)
    def _():
        gain_ref[...] = part

    @pl.when(pl.program_id(0) > 0)
    def _():
        gain_ref[...] = gain_ref[...] + part


def qkv_weight_grads(a1, d0, d1, w):
    rows, width = a1.shape
    one = pl.BlockSpec((1, rows // 2, width), lambda i: (i, 0, 0))
    col = pl.BlockSpec((width, width), lambda i: (0, i))
    return pl.pallas_call(
        qkv_weight_kernel,
        grid=(3,),
        in_specs=[fixed((rows, width)), one, one, col],
        out_specs=[col, fixed((width, TILE))],
        out_shape=[
            jax.ShapeDtypeStruct((width, 3 * width), BF),
            jax.ShapeDtypeStruct((width, TILE), F32),
        ],
        compiler_params=params(48),
        cost_estimate=cost(6 * rows * width * width, rows * width * 10),
        name="qkv_weight_grads",
    )(a1, d0, d1, w)


def qkv_input_kernel(x_ref, gain_ref, w_ref, d_ref, dx1_ref, out_ref):
    width = x_ref.shape[1]
    grad = mm(d_ref[0], w_ref[:, 0:width], NT)
    grad = grad + mm(d_ref[1], w_ref[:, width : 2 * width], NT)
    grad = grad + mm(d_ref[2], w_ref[:, 2 * width : 3 * width], NT)
    x = x_ref[...].astype(F32)
    r = lax.rsqrt(jnp.mean(x * x, axis=-1, keepdims=True) + 1e-06)
    hat = x * r
    d_hat = grad * gain_ref[...]
    dx = r * (d_hat - hat * jnp.mean(d_hat * hat, axis=-1, keepdims=True))
    out_ref[0] = dx + dx1_ref[...]


def qkv_input_grad(x, gain, w, d, dx1, slab, before):
    slabs, rows, width = x.shape
    block = 256
    spec = pl.BlockSpec((block, width), lambda i: (i, 0))
    in_specs = [
        pl.BlockSpec((None, block, width), lambda i: (slab, i, 0)),
        fixed((1, width)),
        fixed(w.shape),
        pl.BlockSpec((3, block, width), lambda i: (0, i, 0)),
        spec,
    ]
    operands = [x, gain, w, d, dx1]
    kernel, aliases = qkv_input_kernel, {}
    if before is not None:
        in_specs.append(pl.BlockSpec(memory_space=pl.ANY))
        operands.append(before)
        aliases = {5: 0}

        def kernel(*refs):
            qkv_input_kernel(*refs[:5], refs[6])

    return pl.pallas_call(
        kernel,
        grid=(rows // block,),
        in_specs=in_specs,
        out_specs=pl.BlockSpec((1, block, width), lambda i: (slab, i, 0)),
        out_shape=jax.ShapeDtypeStruct((slabs, rows, width), F32),
        input_output_aliases=aliases,
        compiler_params=params(40),
        cost_estimate=cost(6 * rows * width * width, rows * width * 16),
        name="qkv_input_grad",
    )(*operands)


def near_offsets():
    key = jnp.arange(TILE, dtype=jnp.int32)[None, :, None]
    query = jnp.arange(TILE, dtype=jnp.int32)[None, None, :]
    delta = jnp.arange(-1, 2, dtype=jnp.int32)[:, None, None]
    return delta * TILE + key - query


def bias_tables(rel_bias, tiles):
    buckets, heads = rel_bias.shape
    onehot = (
        bucket_ids(near_offsets()).reshape(1, -1) == jnp.arange(buckets, dtype=jnp.int32)[:, None]
    )
    near = jnp.einsum(
        "bh,bn->hn", rel_bias, onehot.astype(F32), precision=lax.Precision.HIGHEST
    ).reshape(heads, 3, TILE, TILE)
    qb = jnp.arange(tiles)[:, None]
    kb = jnp.arange(tiles)[None, :]
    left = rel_bias[buckets // 2 - 1][:, None, None]
    right = rel_bias[buckets - 1][:, None, None]
    far = jnp.where(kb >= qb + 2, right, jnp.where(kb <= qb - 2, left, 0.0))
    high = far.astype(BF)
    rest = (far - high.astype(F32)).astype(BF)
    tags = jnp.concatenate(
        [
            jnp.ones((heads, tiles, 1), BF),
            high,
            rest,
            jnp.zeros((heads, tiles, TILE - 1 - 2 * tiles), BF),
        ],
        axis=2,
    )
    return near, tags


def bias_grad(near, far, buckets):
    heads = near.shape[0]
    tiles = far.shape[2]
    onehot = (
        bucket_ids(near_offsets()).reshape(-1, 1) == jnp.arange(buckets, dtype=jnp.int32)[None, :]
    )
    grad = jnp.einsum(
        "hn,nb->bh", near.reshape(heads, -1), onehot.astype(F32), precision=lax.Precision.HIGHEST
    )
    sums = jnp.sum(far.reshape(heads, tiles, tiles, TILE), axis=3)
    kb = jnp.arange(tiles)[:, None]
    qb = jnp.arange(tiles)[None, :]
    left = jnp.sum(jnp.where(kb <= qb - 2, sums, 0.0), axis=(1, 2))
    right = jnp.sum(jnp.where(kb >= qb + 2, sums, 0.0), axis=(1, 2))
    row = jnp.arange(buckets)[:, None]
    grad = grad + jnp.where(row == buckets // 2 - 1, left[None, :], 0.0)
    return grad + jnp.where(row == buckets - 1, right[None, :], 0.0)


def swap(x, axis):
    return lax.ppermute(x, axis, [(0, 1), (1, 0)])


def both_halves(x, axis):
    first = lax.axis_index(axis) == 0
    other = swap(x, axis)
    return jnp.stack([jnp.where(first, x, other), jnp.where(first, other, x)])


def ring_gather(x, axis):
    count = lax.axis_size(axis)
    if count > 4:
        return lax.all_gather(x, axis)
    me = lax.axis_index(axis)
    out = jnp.zeros((count,) + x.shape, x.dtype)
    out = lax.dynamic_update_index_in_dim(out, x, me, 0)
    for k in range(1, count):
        part = lax.ppermute(x, axis, [(j, (j + k) % count) for j in range(count)])
        out = lax.dynamic_update_index_in_dim(out, part, (me - k) % count, 0)
    return out


def quick_gather(x):
    rows, columns = x.shape
    half = columns // 2
    cut = half // 2 // TILE * TILE
    low = lax.axis_index("core") == 0
    pair = both_halves(x, "core")
    mine = jnp.where(low, pair[..., :half], pair[..., half:])
    line = ring_gather(mine, "z")
    one = both_halves(both_halves(line[..., :cut], "x"), "tower")
    two = both_halves(both_halves(line[..., cut:], "tower"), "x")
    full = jnp.concatenate([one, jnp.swapaxes(two, 0, 1)], axis=-1)
    full = both_halves(full, "core")
    full = jnp.concatenate([full[0], full[1]], axis=-1)
    return jnp.swapaxes(full, 1, 2).reshape(-1, columns)


def give_half(x, axis, dim):
    me = lax.axis_index(axis)
    keep = lax.dynamic_index_in_dim(x, me, dim, keepdims=False)
    got = swap(lax.dynamic_index_in_dim(x, 1 - me, dim, keepdims=False), axis)
    return (keep.astype(F32) + got.astype(F32)).astype(BF)


def ring_scatter(x, axis):
    count = lax.axis_size(axis)
    if count > 4:
        return lax.psum_scatter(x, axis, scatter_dimension=0, tiled=False).astype(F32)
    me = lax.axis_index(axis)
    total = lax.dynamic_index_in_dim(x, me, 0, keepdims=False).astype(F32)
    for k in range(1, count):
        part = lax.dynamic_index_in_dim(x, (me + k) % count, 0, keepdims=False)
        part = lax.ppermute(part, axis, [(j, (j + k) % count) for j in range(count)])
        total = total + part.astype(F32)
    return total


def by_device(x):
    sizes = tuple(lax.axis_size(a) for a in ("tower", "z", "x", "core"))
    return x.reshape(sizes + (-1, x.shape[-1]))


def quick_scatter(x):
    half = x.shape[-1] // 2
    x = give_half(by_device(x), "core", 3)
    one = give_half(give_half(x[..., :half], "tower", 0), "x", 1)
    two = give_half(give_half(x[..., half:], "x", 2), "tower", 0)
    return ring_scatter(jnp.concatenate([one, two], axis=-1), "z")


def big_scatter(x):
    x = give_half(by_device(x), "core", 3)
    columns = x.shape[-1]
    x = jnp.swapaxes(x, 1, 2).reshape(-1, columns)
    x = lax.psum_scatter(x, ("tower", "x"), scatter_dimension=0, tiled=True)
    return lax.psum_scatter(x, "z", scatter_dimension=0, tiled=True).astype(F32)


def sum_everywhere(x):
    for axis in ("core", "x", "tower", "z"):
        count, step = lax.axis_size(axis), 1
        while step < count:
            x = x + lax.ppermute(x, axis, [(j, j ^ step) for j in range(count)])
            step *= 2
    return x


AXES = ("tower", "z", "x", "core")


def per_device(
    hidden,
    lengths,
    pairs,
    out_grad,
    w_query,
    w_key,
    w_value,
    w_attn_out,
    w_in,
    w_out,
    w_proj,
    gain_attn,
    gain_ffn,
    gain_final,
    rel_bias,
):
    devices = lax.axis_size(AXES)
    dp_count = devices // lax.axis_size("tower")
    is_doc = lax.axis_index("tower") == 1
    query_side = jnp.where(is_doc, 0.0, 1.0).astype(F32)
    rows, width = hidden.shape[3:]
    slots = lengths.shape[3]
    buckets, heads = rel_bias.shape
    shard, ff = w_in.shape
    chunks = ff // width
    first_slot = (jnp.arange(slots) == 0)[:, None]
    gain1, gain2, gain3 = gain_attn[None], gain_ffn[None], gain_final[None]
    x_all = hidden[0, 0].reshape(MICRO * rows, width)

    w_in = w_in.reshape(shard, devices, chunks, shard).swapaxes(1, 2).reshape(shard, ff)
    pieces = []
    for c in range(chunks):
        pieces.append(w_in[:, c * width : (c + 1) * width])
        pieces.append(w_out[c * shard : (c + 1) * shard])
    wqkv = quick_gather(jnp.concatenate([w_query, w_key, w_value], axis=1))
    w_all = lax.all_gather(
        jnp.concatenate(pieces + [w_attn_out, w_proj], axis=1), AXES, axis=0, tiled=True
    )
    w_proj_all = w_all[:, -width:]

    near_bias, tags = bias_tables(rel_bias, rows // TILE)
    a1, qkv = project_qkv(x_all, gain1, wqkv)

    slabs = []
    for m in range(MICRO):
        at = slice(m * rows, (m + 1) * rows)
        lens = lengths[0, 0, m]
        per_group = jnp.clip(lens[0] - GROUP * jnp.arange(rows // GROUP), 0, GROUP)
        glen = jnp.where(is_doc, per_group, lens).astype(jnp.int32)
        info = jnp.concatenate([jnp.stack([is_doc.astype(jnp.int32), lens[0]]), glen])
        mixed, probs, linv = attention(info, qkv[at], tags, near_bias, heads)
        x1, a2, act, slope, x2, out, pool = ffn_forward(
            glen, hidden[0, 0, m], mixed, w_all, gain2, gain3
        )
        slabs.append((glen, info, lens, mixed, probs, linv, x1, a2, act, slope, x2, out, pool))

    pool = jnp.stack([slab[-1] for slab in slabs])
    counts = jnp.maximum(lengths[0, 0].astype(F32), 1.0)[..., None]
    doc_pool = jnp.where(first_slot, jnp.sum(pool, axis=1, keepdims=True), 0.0)
    pooled = (jnp.where(is_doc, doc_pool, pool) / counts).astype(BF)
    projected = jnp.dot(
        pooled.reshape(MICRO * slots, width), w_proj_all, preferred_element_type=F32
    ).reshape(MICRO, slots, width)
    unit_vec, unit_pull = jax.vjp(unit_norm, projected)
    unit_low = unit_vec.astype(BF)
    sent = jnp.broadcast_to(unit_low[None, :, 0], (devices, MICRO, width))
    docs = lax.all_to_all(sent, AXES, 0, 0, tiled=True)[dp_count:]
    logits = (
        jnp.einsum("msd,bmd->msb", unit_low, docs, preferred_element_type=F32) * logit_scale
    )
    row_max = jnp.max(logits, axis=-1, keepdims=True)
    log_total = row_max + jnp.log(jnp.sum(jnp.exp(logits - row_max), axis=-1, keepdims=True))
    chosen_mask = jnp.arange(dp_count, dtype=jnp.int32) == pairs[:, 0, :, None]
    chosen = jnp.sum(jnp.where(chosen_mask, logits, 0.0), axis=-1)
    loss_part = jnp.sum(log_total[..., 0] - chosen) * query_side
    logit_grad = (
        (jnp.exp(logits - log_total) - chosen_mask.astype(F32)) * query_side
    ).astype(BF)
    unit_grad = (
        jnp.einsum("msb,bmd->msd", logit_grad, docs, preferred_element_type=F32) * logit_scale
    )
    docs_grad = (
        jnp.einsum("msb,msd->bmd", logit_grad, unit_low, preferred_element_type=F32) * logit_scale
    )
    back = jnp.concatenate([jnp.zeros_like(docs_grad), docs_grad], axis=0)
    returned = jnp.sum(lax.all_to_all(back, AXES, 0, 0, tiled=True)[:dp_count], axis=0)
    unit_grad = unit_grad + jnp.where(first_slot & is_doc, returned[:, None], 0.0)
    proj_grad_in = unit_pull(unit_grad)[0].astype(BF)
    flat = proj_grad_in.reshape(MICRO * slots, width)
    grad_proj = mm(pooled.reshape(MICRO * slots, width), flat, TN).astype(BF)
    dpooled = jnp.dot(flat, w_proj_all.T, preferred_element_type=F32)
    dpooled = dpooled.reshape(MICRO, slots, width) / counts
    dpool = jnp.where(is_doc, jnp.broadcast_to(dpooled[:, 0:1], dpooled.shape), dpooled)

    grads, ggains, backs = None, 0.0, []
    for m in range(MICRO):
        glen, info, lens, mixed, probs, linv, x1, a2, act, slope, x2, out, _ = slabs[m]
        grads, dx1, d_mixed, ggain = ffn_backward(
            glen,
            x2,
            out_grad[0, 0, m],
            dpool[m],
            x1,
            a2,
            mixed,
            act,
            slope,
            w_all,
            gain2,
            gain3,
            grads,
            grad_proj,
        )
        backs.append((dx1, d_mixed))
        ggains = ggains + ggain
    grad_all = big_scatter(grads)
    grad_in = jnp.concatenate(
        [grad_all[:, 2 * c * width : (2 * c + 1) * width] for c in range(chunks)], axis=1
    )
    grad_in = grad_in.reshape(shard, chunks, devices, shard).swapaxes(1, 2).reshape(shard, ff)
    grad_out = jnp.concatenate(
        [grad_all[:, (2 * c + 1) * width : (2 * c + 2) * width] for c in range(chunks)], axis=0
    )
    grad_wo = grad_all[:, 2 * ff : 2 * ff + width]
    grad_proj = grad_all[:, 2 * ff + width :]

    dqkvs, near_sum, far_sum = [], 0.0, 0.0
    for m in range(MICRO):
        glen, info, lens, mixed, probs, linv = slabs[m][:6]
        at = slice(m * rows, (m + 1) * rows)
        dqkv, near, far = attention_back(info, qkv[at], mixed, backs[m][1], probs, linv)
        dqkvs.append(dqkv)
        near_sum = near_sum + near
        far_sum = far_sum + far
    grad_bias = bias_grad(near_sum, far_sum, buckets)

    grad_qkv, gain_part = qkv_weight_grads(a1, *dqkvs, wqkv)
    grad_qkv = quick_scatter(grad_qkv)
    ggain1 = jnp.sum(gain_part, axis=1) / gain_attn
    smalls = jnp.concatenate(
        [ggain1, ggains[0], ggains[1], grad_bias.reshape(-1), loss_part[None]]
    )
    pad = -smalls.shape[0] % (8 * TILE)
    totals = sum_everywhere(jnp.pad(smalls, (0, pad)).reshape(-1, TILE)).reshape(-1)
    input_grads = None
    for m in range(MICRO):
        input_grads = qkv_input_grad(
            hidden[0, 0], gain1, wqkv, dqkvs[m], backs[m][0], m, input_grads
        )

    outputs = jnp.stack([slab[-2] for slab in slabs])
    return (
        outputs[None, None],
        input_grads[None, None],
        totals[3 * width + buckets * heads] / (dp_count * slots * MICRO),
        grad_qkv[:, :width],
        grad_qkv[:, width : 2 * width],
        grad_qkv[:, 2 * width :],
        grad_wo,
        grad_in,
        grad_out,
        grad_proj,
        totals[:width],
        totals[width : 2 * width],
        totals[2 * width : 3 * width],
        totals[3 * width : 3 * width + buckets * heads].reshape(buckets, heads),
    )


def solution(mesh):
    towers, per_tower = mesh.devices.shape
    fine = Mesh(mesh.devices.reshape(towers, per_tower // 4, 2, 2), AXES)
    dp = AXES[1:]
    rows = P(AXES, None)
    slabs = P("tower", dp, None, None, None)
    return jax.shard_map(
        per_device,
        mesh=fine,
        in_specs=(slabs, P("tower", dp, None, None), P(None, dp, None), slabs)
        + (rows,) * 7
        + (P(),) * 4,
        out_specs=(slabs, slabs, P()) + (rows,) * 7 + (P(),) * 4,
        check_vma=False,
    )
```

```python
import jax
import jax.numpy as jnp
from jax import lax
from jax.experimental import pallas as pl
from jax.experimental.pallas import tpu as pltpu
from jax.sharding import Mesh, PartitionSpec as P

bucket_steps = (12, 16, 23, 32, 46, 64, 91)
score_scale = 0.125
logit_scale = 64.0
negative = -1e30
MICRO = 2
TILE = 128
WIDE = 256
GROUP = 64

BF = jnp.bfloat16
F32 = jnp.float32
NN = (((1,), (0,)), ((), ()))
NT = (((1,), (1,)), ((), ()))
TN = (((0,), (0,)), ((), ()))
GELU_A = 0.7978845608028654
GELU_B = 0.044715


def mm(a, b, dims=NN):
    return lax.dot_general(a, b, dims, preferred_element_type=F32)


def params(megabytes):
    return pltpu.CompilerParams(vmem_limit_bytes=megabytes << 20)


def fixed(shape):
    zeros = (0,) * len(shape)
    return pl.BlockSpec(shape, lambda *_: zeros, pipeline_mode=pl.Buffered(1))


def cost(flops, data):
    return pl.CostEstimate(flops=int(flops), bytes_accessed=int(data), transcendentals=0)


def unit_norm(vector):
    return vector * lax.rsqrt(jnp.sum(vector * vector, axis=-1, keepdims=True) + 1e-06)


def bucket_ids(offset):
    distance = jnp.abs(offset)
    far_bucket = jnp.full(offset.shape, 8, jnp.int32)
    for threshold in bucket_steps:
        far_bucket = far_bucket + (distance >= threshold).astype(jnp.int32)
    bucket = jnp.where(distance < 8, distance, far_bucket)
    return bucket + 16 * (offset > 0).astype(jnp.int32)


def qkv_kernel(x_ref, gain_ref, w_ref, a1_ref, qkv_ref, norm_ref):
    x = x_ref[...].astype(F32)
    r = lax.rsqrt(jnp.mean(x * x, axis=-1, keepdims=True) + 1e-06)
    a1 = (x * r * gain_ref[...]).astype(BF)
    a1_ref[...] = a1
    width = a1.shape[1]
    row = lax.broadcasted_iota(jnp.int32, (width, TILE), 0)
    col = lax.broadcasted_iota(jnp.int32, (width, TILE), 1)
    of_head = jnp.where(row // GROUP == col, 1.0, 0.0).astype(BF)
    norm_ref[...] = jnp.zeros(norm_ref.shape, F32)
    for part in range(3):
        out = mm(a1, w_ref[:, part * width : (part + 1) * width]).astype(BF)
        if part == 0:
            out = out * BF(score_scale)
        qkv_ref[:, part * width : (part + 1) * width] = out
        if part < 2:
            square = mm(out * out, of_head)
            norm_ref[0, part : part + 1, :] = jnp.max(square, axis=0, keepdims=True)


def project_qkv(x, gain, w):
    rows, width = x.shape
    block = 256
    return pl.pallas_call(
        qkv_kernel,
        grid=(rows // block,),
        in_specs=[
            pl.BlockSpec((block, width), lambda i: (i, 0)),
            fixed((1, width)),
            fixed(w.shape),
        ],
        out_specs=[
            pl.BlockSpec((block, width), lambda i: (i, 0)),
            pl.BlockSpec((block, 3 * width), lambda i: (i, 0)),
            pl.BlockSpec((1, 8, TILE), lambda i: (i, 0, 0)),
        ],
        out_shape=[
            jax.ShapeDtypeStruct((rows, width), BF),
            jax.ShapeDtypeStruct((rows, 3 * width), BF),
            jax.ShapeDtypeStruct((rows // block, 8, TILE), F32),
        ],
        compiler_params=params(40),
        cost_estimate=cost(6 * rows * width * width, rows * width * 10),
        name="norm_qkv",
    )(x, gain, w)


def lane_half(shape, head):
    lane = lax.broadcasted_iota(jnp.int32, shape, 1)
    return (lane // GROUP) == head


def key_extras(rows, length):
    row = lax.broadcasted_iota(jnp.int32, (rows, TILE), 0)
    col = lax.broadcasted_iota(jnp.int32, (rows, TILE), 1)
    block = row // TILE
    hit = (col - 1 == block) | (col - 1 - rows // TILE == block)
    ones = jnp.where(hit & (col > 0), 1.0, 0.0)
    return jnp.where(col == 0, jnp.where(row < length, 0.0, negative), ones).astype(BF)


def query_mask(info_ref, slab, tile):
    row = lax.broadcasted_iota(jnp.int32, (TILE, TILE), 0)
    col = lax.broadcasted_iota(jnp.int32, (TILE, TILE), 1)
    per = TILE // GROUP
    good = jnp.zeros((TILE, TILE), jnp.bool_)
    for s in range(per):
        low = s * GROUP
        inside = (row >= low) & (row < low + info_ref[slab, 3 + tile * per + s])
        good = good | (inside & (col >= low) & (col < low + GROUP))
    return good


def attn_fwd_kernel(
    info_ref, q_ref, k_ref, v_ref, eq_ref, t_ref, o_ref, p_ref, linv_ref, s_scr, ot_scr
):
    rows = q_ref.shape[0]
    tiles = rows // TILE
    per = WIDE // TILE
    vt = v_ref[...].T
    below = [
        jnp.concatenate([vt[h * GROUP : (h + 1) * GROUP, :], jnp.ones((16, rows), BF)], axis=0)
        for h in range(2)
    ]
    work = [(head, wide) for head in range(2) for wide in range(rows // WIDE)]

    def near(s, head, kb, qb):
        return s + t_ref[head, kb - qb + 1] if abs(kb - qb) <= 1 else s

    def tagged(n):
        head, wide = work[n]
        tags = [
            jnp.broadcast_to(eq_ref[head, qb : qb + 1, :], (TILE, TILE))
            for qb in range(wide * per, (wide + 1) * per)
        ]
        cols = slice(wide * WIDE, (wide + 1) * WIDE)
        masked = jnp.where(lane_half((WIDE, TILE), head), q_ref[cols, :], BF(0))
        return jnp.concatenate([masked, jnp.concatenate(tags, axis=0)], axis=1)

    def mix(n):
        head, wide = work[n]
        cols = slice(wide * WIDE, (wide + 1) * WIDE)
        out = mm(below[head], p_ref[head, :, cols])
        inv = 1.0 / out[GROUP : GROUP + 1, :]
        ot_scr[head * GROUP : (head + 1) * GROUP, cols] = out[:GROUP, :] * inv
        linv_ref[0, head : head + 1, cols] = inv

    slab = pl.program_id(0)
    is_doc = info_ref[slab, 0] == 1
    small = info_ref[slab, 2] == 1

    @pl.when(is_doc & small)
    def _():
        keys = jnp.concatenate([k_ref[...], key_extras(rows, info_ref[slab, 1])], axis=1)

        def weigh(n):
            head, wide = work[n]
            qa = tagged(n)
            for first in range(0, rows, WIDE):
                part = mm(keys[first : first + WIDE, :], qa, NT)
                for low in range(0, WIDE, TILE):
                    for sub in range(per):
                        kb, qb = (first + low) // TILE, wide * per + sub
                        s = part[low : low + TILE, sub * TILE : (sub + 1) * TILE]
                        p_ref[
                            head, kb * TILE : (kb + 1) * TILE, qb * TILE : (qb + 1) * TILE
                        ] = jnp.exp(near(s, head, kb, qb)).astype(BF)

        for n in range(len(work)):
            weigh(n)
            if n > 0:
                mix(n - 1)
        mix(len(work) - 1)

    @pl.when(is_doc & jnp.logical_not(small))
    def _():
        keys = jnp.concatenate([k_ref[...], key_extras(rows, info_ref[slab, 1])], axis=1)
        for n in range(len(work)):
            head, wide = work[n]
            part = mm(keys, tagged(n), NT)
            tops = [None] * per
            for kb in range(tiles):
                for sub in range(per):
                    at = (slice(kb * TILE, (kb + 1) * TILE), slice(sub * TILE, (sub + 1) * TILE))
                    s = near(part[at], head, kb, wide * per + sub)
                    s_scr[at] = s
                    tops[sub] = s if tops[sub] is None else jnp.maximum(tops[sub], s)
            top = jnp.concatenate([jnp.max(t, axis=0, keepdims=True) for t in tops], axis=1)
            for kb in range(tiles):
                at = slice(kb * TILE, (kb + 1) * TILE)
                p_ref[head, at, wide * WIDE : (wide + 1) * WIDE] = jnp.exp(
                    s_scr[at, :] - top
                ).astype(BF)
            mix(n)

    @pl.when(jnp.logical_not(is_doc))
    def _():
        spans = [slice(tile * TILE, (tile + 1) * TILE) for tile in range(tiles)]
        vo = jnp.concatenate([vt, jnp.ones((16, rows), BF)], axis=0)
        bias = jnp.concatenate([t_ref[0, 1], t_ref[1, 1]], axis=1)
        for at in spans:
            q = q_ref[at, :]
            both = [jnp.where(lane_half((TILE, TILE), head), q, BF(0)) for head in range(2)]
            s_scr[at, :] = mm(k_ref[at, :], jnp.concatenate(both, axis=0), NT)
        for tile, at in enumerate(spans):
            good = query_mask(info_ref, slab, tile)
            s = s_scr[at, :] + bias
            s = jnp.where(jnp.concatenate([good, good], axis=1), s, negative)
            p = jnp.exp(s - jnp.max(s, axis=0, keepdims=True)).astype(BF)
            p_ref[0, at, at] = p[:, :TILE]
            p_ref[1, at, at] = p[:, TILE:]
        for at in spans:
            out = mm(vo[:, at], jnp.concatenate([p_ref[0, at, at], p_ref[1, at, at]], axis=1))
            inv = 1.0 / out[TILE : TILE + 1, :]
            for head in range(2):
                lanes = slice(head * TILE, (head + 1) * TILE)
                mine = slice(head * GROUP, (head + 1) * GROUP)
                ot_scr[mine, at] = out[mine, lanes] * inv[:, lanes]
                linv_ref[0, head : head + 1, at] = inv[:, lanes]

    o_ref[...] = ot_scr[...].T.astype(BF)


def attention(info, qkv, tags, near, heads):
    slabs = info.shape[0]
    rows = qkv.shape[0] // slabs
    width = qkv.shape[1] // 3
    pairs = heads // 2
    return pl.pallas_call(
        attn_fwd_kernel,
        grid_spec=pltpu.PrefetchScalarGridSpec(
            num_scalar_prefetch=1,
            grid=(slabs, pairs),
            in_specs=[
                pl.BlockSpec((rows, TILE), lambda s, i, _: (s, i)),
                pl.BlockSpec((rows, TILE), lambda s, i, _: (s, pairs + i)),
                pl.BlockSpec((rows, TILE), lambda s, i, _: (s, 2 * pairs + i)),
                pl.BlockSpec((2,) + tags.shape[1:], lambda s, i, _: (i, 0, 0)),
                pl.BlockSpec((2,) + near.shape[1:], lambda s, i, _: (i, 0, 0, 0)),
            ],
            out_specs=[
                pl.BlockSpec((rows, TILE), lambda s, i, _: (s, i)),
                pl.BlockSpec((2, rows, rows), lambda s, i, _: (s * pairs + i, 0, 0)),
                pl.BlockSpec((1, 2, rows), lambda s, i, _: (s * pairs + i, 0, 0)),
            ],
            scratch_shapes=[pltpu.VMEM((rows, WIDE), F32), pltpu.VMEM((TILE, rows), F32)],
        ),
        out_shape=[
            jax.ShapeDtypeStruct((slabs * rows, width), BF),
            jax.ShapeDtypeStruct((slabs * heads, rows, rows), BF),
            jax.ShapeDtypeStruct((slabs * pairs, 2, rows), F32),
        ],
        compiler_params=params(48),
        cost_estimate=cost(slabs * heads * rows * rows * 512, slabs * heads * rows * rows * 2),
        name="attention_forward",
    )(info, qkv, qkv, qkv, tags, near)


def attn_bwd_kernel(
    info_ref,
    q_ref,
    k_ref,
    v_ref,
    o_ref,
    do_ref,
    p_ref,
    linv_ref,
    dqkv_ref,
    sums_ref,
    ds_scr,
    dqt_scr,
    far_scr,
):
    rows = q_ref.shape[0]
    tiles = rows // TILE
    square = (TILE, TILE)
    mirror = lax.broadcasted_iota(jnp.int32, square, 0) + lax.broadcasted_iota(jnp.int32, square, 1)
    mirror = jnp.where(mirror == TILE - 1, 1.0, 0.0)
    sums_ref[...] = jnp.zeros(sums_ref.shape, F32)

    def diagonals(x):
        x = lax.dot_general(
            x, mirror, NN, precision=lax.Precision.HIGHEST, preferred_element_type=F32
        )
        x = jnp.concatenate([x, jnp.zeros(square, F32)], axis=1)
        return jnp.sum(pltpu.roll(x, 0, 1, stride=1, stride_axis=0), axis=0, keepdims=True)

    col = lax.broadcasted_iota(jnp.int32, (rows, TILE), 1)
    kt = k_ref[...].T
    scale = jnp.concatenate([linv_ref[0], jnp.zeros((6, rows), F32)], axis=0).T
    d_out = do_ref[...].astype(F32)
    prod = d_out * o_ref[...].astype(F32)
    values = jnp.concatenate([v_ref[...], jnp.where(col < 2, 1.0, 0.0).astype(BF)], axis=1)

    def prepare(head):
        mine = lane_half((rows, TILE), head)
        inv = scale[:, head : head + 1]
        scaled = jnp.where(mine, d_out * inv, 0.0).astype(BF)
        shift = -jnp.sum(jnp.where(mine, prod, 0.0), axis=1, keepdims=True) * inv
        high = shift.astype(BF)
        rest = (shift - high.astype(F32)).astype(BF)
        extra = jnp.where(col == 0, high, jnp.where(col == 1, rest, BF(0)))
        masked = jnp.where(mine, q_ref[...], BF(0))
        return scaled, jnp.concatenate([scaled, extra], axis=1), masked

    @pl.when(info_ref[0, 0] == 1)
    def _():
        block = lax.broadcasted_iota(jnp.int32, (16, rows), 1) // TILE
        place = lax.broadcasted_iota(jnp.int32, (16, rows), 0)
        marks = jnp.where(block == place, 1.0, 0.0).astype(BF)
        ready = [prepare(head) for head in range(2)]
        ka = [
            jnp.concatenate([kt[head * GROUP : (head + 1) * GROUP, :], marks], axis=0)
            for head in range(2)
        ]
        work = [(head, wide) for head in range(2) for wide in range(rows // WIDE)]

        def slope(n):
            head, wide = work[n]
            cols = slice(wide * WIDE, (wide + 1) * WIDE)
            for first in range(0, rows, WIDE):
                at = slice(first, first + WIDE)
                dp = mm(values[at, :], ready[head][1][cols, :], NT)
                ds_scr[head, at, cols] = (p_ref[head, at, cols].astype(F32) * dp).astype(BF)

        def back(n):
            head, wide = work[n]
            cols = slice(wide * WIDE, (wide + 1) * WIDE)
            out = mm(ka[head], ds_scr[head, :, cols])
            dqt_scr[head * GROUP : (head + 1) * GROUP, cols] = out[:GROUP, :] * score_scale
            far_scr[head, :, cols] = out[GROUP : GROUP + tiles, :]

        for n in range(len(work)):
            slope(n)
            if n > 0:
                back(n - 1)
        back(len(work) - 1)
        dk = mm(ds_scr[0], ready[0][2]) + mm(ds_scr[1], ready[1][2])
        dv = mm(p_ref[0], ready[0][0]) + mm(p_ref[1], ready[1][0])
        for head in range(2):
            for delta in (-1, 0, 1):
                total = None
                for qb in range(tiles):
                    kb = qb + delta
                    if 0 <= kb < tiles:
                        part = ds_scr[
                            head, kb * TILE : (kb + 1) * TILE, qb * TILE : (qb + 1) * TILE
                        ].astype(F32)
                        total = part if total is None else total + part
                sums_ref[head, delta + 1 : delta + 2, :] = diagonals(total)
            kb = lax.broadcasted_iota(jnp.int32, (tiles, rows), 0)
            qb = lax.broadcasted_iota(jnp.int32, (tiles, rows), 1) // TILE
            for at, side in ((3, kb <= qb - 2), (4, kb >= qb + 2)):
                some = jnp.sum(jnp.where(side, far_scr[head], 0.0), axis=0, keepdims=True)
                sums_ref[head, at : at + 1, 0:TILE] = sum(
                    some[:, t * TILE : (t + 1) * TILE] for t in range(tiles)
                )
        dqkv_ref[1] = dk.astype(BF)
        dqkv_ref[2] = dv.astype(BF)

    @pl.when(info_ref[0, 0] == 0)
    def _():
        for head in range(2):
            scaled, outer, masked = prepare(head)
            total = None
            for tile in range(tiles):
                at = slice(tile * TILE, (tile + 1) * TILE)
                p = p_ref[head, at, at]
                dp = mm(values[at, :], outer[at, :], NT)
                part = p.astype(F32) * dp
                ds = part.astype(BF)
                total = part if total is None else total + part
                out = mm(kt[head * GROUP : (head + 1) * GROUP, at], ds)
                dqt_scr[head * GROUP : (head + 1) * GROUP, at] = out * score_scale
                dk = mm(ds, masked[at, :])
                dv = mm(p, scaled[at, :])
                if head == 0:
                    ds_scr[0, at, 0:TILE] = dk.astype(BF)
                    ds_scr[1, at, 0:TILE] = dv.astype(BF)
                else:
                    dqkv_ref[1, at, :] = ds_scr[0, at, 0:TILE] + dk.astype(BF)
                    dqkv_ref[2, at, :] = ds_scr[1, at, 0:TILE] + dv.astype(BF)
            sums_ref[head, 1:2, :] = diagonals(total)

    dqkv_ref[0] = dqt_scr[...].T.astype(BF)


def attention_back(info, qkv, mixed, d_mixed, probs, linv, slab, part, parts):
    slabs = info.shape[0]
    rows = qkv.shape[0] // slabs
    width = qkv.shape[1] // 3
    pairs = linv.shape[0] // slabs
    tiles = rows // TILE
    count = pairs // parts
    base = part * count
    heads = 2 * count
    return pl.pallas_call(
        attn_bwd_kernel,
        grid_spec=pltpu.PrefetchScalarGridSpec(
            num_scalar_prefetch=1,
            grid=(count,),
            in_specs=[
                pl.BlockSpec((rows, TILE), lambda i, _: (slab, base + i)),
                pl.BlockSpec((rows, TILE), lambda i, _: (slab, pairs + base + i)),
                pl.BlockSpec((rows, TILE), lambda i, _: (slab, 2 * pairs + base + i)),
                pl.BlockSpec((rows, TILE), lambda i, _: (slab, base + i)),
                pl.BlockSpec((rows, TILE), lambda i, _: (0, base + i)),
                pl.BlockSpec((2, rows, rows), lambda i, _: (slab * pairs + base + i, 0, 0)),
                pl.BlockSpec((1, 2, rows), lambda i, _: (slab * pairs + base + i, 0, 0)),
            ],
            out_specs=[
                pl.BlockSpec((3, rows, TILE), lambda i, _: (0, 0, i)),
                pl.BlockSpec((2, 8, 2 * TILE), lambda i, _: (i, 0, 0)),
            ],
            scratch_shapes=[
                pltpu.VMEM((2, rows, rows), BF),
                pltpu.VMEM((TILE, rows), F32),
                pltpu.VMEM((2, tiles, rows), F32),
            ],
        ),
        out_shape=[
            jax.ShapeDtypeStruct((3, rows, count * TILE), BF),
            jax.ShapeDtypeStruct((heads, 8, 2 * TILE), F32),
        ],
        compiler_params=params(56),
        cost_estimate=cost(heads * rows * rows * 1024, heads * rows * rows * 2),
        name="attention_backward",
    )(info, qkv, qkv, qkv, mixed, d_mixed, probs, linv)


def usable_rows(glen_ref, first, rows):
    row = lax.broadcasted_iota(jnp.int32, (rows, 1), 0)
    good = jnp.zeros((rows, 1), jnp.bool_)
    for g in range(rows // GROUP):
        low = g * GROUP
        good = good | ((row >= low) & (row < low + glen_ref[first + g]))
    return good


def ffn_fwd_kernel(
    glen_ref,
    x_ref,
    mixed_ref,
    w_ref,
    gain2_ref,
    gain3_ref,
    x1_ref,
    a2_ref,
    act_ref,
    slope_ref,
    x2_ref,
    out_ref,
    pool_ref,
):
    rows, width = x_ref.shape
    last = w_ref.shape[1] - 2 * width
    x1 = x_ref[...].astype(F32) + mm(mixed_ref[...], w_ref[:, last : last + width])
    x1_ref[...] = x1
    r = lax.rsqrt(jnp.mean(x1 * x1, axis=-1, keepdims=True) + 1e-06)
    a2 = (x1 * r * gain2_ref[...]).astype(BF)
    a2_ref[...] = a2
    total = x1
    for c in range(last // (2 * width)):
        at = slice(c * width, (c + 1) * width)
        into = 2 * c * width
        pre = mm(a2, w_ref[:, into : into + width])
        sq = pre * pre
        tanh = jnp.tanh(pre * (sq * (GELU_A * GELU_B) + GELU_A))
        half = 0.5 * tanh + 0.5
        act = pre * half
        slope = half + 2.0 * act * (1.0 - half) * (sq * (3 * GELU_A * GELU_B) + GELU_A)
        act = act.astype(BF)
        act_ref[:, at] = act
        slope_ref[:, at] = slope.astype(BF)
        total = total + mm(act, w_ref[:, into + width : into + 2 * width])
    x2_ref[...] = total
    out_ref[...] = total.astype(BF)
    r3 = lax.rsqrt(jnp.mean(total * total, axis=-1, keepdims=True) + 1e-06)
    a3 = total * r3 * gain3_ref[...]
    a3 = jnp.where(usable_rows(glen_ref, pl.program_id(0) * (rows // GROUP), rows), a3, 0.0)
    for g in range(rows // GROUP):
        pool_ref[0, g : g + 1, :] = jnp.sum(
            a3[g * GROUP : (g + 1) * GROUP, :], axis=0, keepdims=True
        )


def ffn_forward(glen, x, mixed, w_all, gain2, gain3):
    rows, width = x.shape
    ff = w_all.shape[1] // 2 - width
    block = 512
    groups = block // GROUP
    spec = pl.BlockSpec((block, width), lambda i, _: (i, 0))
    wide = pl.BlockSpec((block, ff), lambda i, _: (i, 0))
    out = pl.pallas_call(
        ffn_fwd_kernel,
        grid_spec=pltpu.PrefetchScalarGridSpec(
            num_scalar_prefetch=1,
            grid=(rows // block,),
            in_specs=[
                spec,
                spec,
                fixed(w_all.shape),
                fixed((1, width)),
                fixed((1, width)),
            ],
            out_specs=[
                spec,
                spec,
                wide,
                wide,
                spec,
                spec,
                pl.BlockSpec((1, groups, width), lambda i, _: (i, 0, 0)),
            ],
        ),
        out_shape=[
            jax.ShapeDtypeStruct((rows, width), F32),
            jax.ShapeDtypeStruct((rows, width), BF),
            jax.ShapeDtypeStruct((rows, ff), BF),
            jax.ShapeDtypeStruct((rows, ff), BF),
            jax.ShapeDtypeStruct((rows, width), F32),
            jax.ShapeDtypeStruct((rows, width), BF),
            jax.ShapeDtypeStruct((rows // block, groups, width), F32),
        ],
        compiler_params=params(56),
        cost_estimate=cost(2 * rows * width * (width + 2 * ff), rows * width * 40),
        name="ffn_forward",
    )(glen, x, mixed, w_all, gain2, gain3)
    return *out[:6], out[6].reshape(rows // GROUP, width)


def norm_back(x, gain, grad):
    r = lax.rsqrt(jnp.mean(x * x, axis=-1, keepdims=True) + 1e-06)
    hat = x * r
    d_gain = jnp.sum(grad * hat, axis=0, keepdims=True)
    d_hat = grad * gain
    dx = r * (d_hat - hat * jnp.mean(d_hat * hat, axis=-1, keepdims=True))
    return dx, d_gain


def ffn_bwd_kernel(slab, order):
    second = slab > 0

    def kernel(*refs):
        (
            glen_ref,
            x2_ref,
            cot_ref,
            dpool_ref,
            x1_ref,
            a2_ref,
            mixed_ref,
            act_ref,
            slope_ref,
            w_ref,
            gain2_ref,
            gain3_ref,
        ) = refs[:12]
        rest = refs[12:]
        if second:
            before_ref, gproj_ref = rest[:2]
            rest = rest[2:]
        (
            g_ref,
            dx1_ref,
            dmixed_ref,
            ggain_ref,
            dx2_scr,
            dy2_scr,
            da2_scr,
            dpre_scr,
        ) = rest
        rows, width = x2_ref.shape
        step = pl.program_id(0)
        last = pl.num_programs(0) - 1
        block = 256
        left, right = slice(0, width), slice(width, 2 * width)

        def put(side, value):
            if second:
                value = ordered(value + before_ref[:, side])
            g_ref[:, side] = value.astype(g_ref.dtype)

        def ordered(value):
            shard = value.shape[0] // len(order)
            return jnp.concatenate([value[d * shard : (d + 1) * shard, :] for d in order], axis=0)

        @pl.when(step == 0)
        def _():
            gain = jnp.zeros((1, width), F32)
            for b in range(rows // block):
                at = slice(b * block, (b + 1) * block)
                per = block // GROUP
                grad = jnp.concatenate(
                    [
                        jnp.broadcast_to(dpool_ref[b * per + g : b * per + g + 1, :], (GROUP, width))
                        for g in range(per)
                    ],
                    axis=0,
                )
                grad = jnp.where(usable_rows(glen_ref, slab * (rows // GROUP) + b * per, block), grad, 0.0)
                dx, d_gain = norm_back(x2_ref[at, :], gain3_ref[...], grad)
                gain = gain + d_gain
                dx = dx + cot_ref[at, :].astype(F32)
                dx2_scr[at, :] = dx
                dy2_scr[at, :] = dx.astype(BF)
            ggain_ref[1:2, :] = gain
            da2_scr[...] = jnp.zeros_like(da2_scr)

        @pl.when(step < last)
        def _():
            dact = mm(dy2_scr[...], w_ref[:, right], NT)
            dpre_scr[...] = (dact * slope_ref[...].astype(F32)).astype(BF)
            put(right, mm(act_ref[...], dy2_scr[...], TN))
            put(left, mm(a2_ref[...], dpre_scr[...], TN))
            da2_scr[...] = da2_scr[...] + mm(dpre_scr[...], w_ref[:, left], NT)

        @pl.when(step == last)
        def _():
            gain = jnp.zeros((1, width), F32)
            for b in range(rows // block):
                at = slice(b * block, (b + 1) * block)
                dx, d_gain = norm_back(x1_ref[at, :], gain2_ref[...], da2_scr[at, :])
                gain = gain + d_gain
                dx = dx + dx2_scr[at, :]
                dx1_ref[at, :] = dx
                dy2_scr[at, :] = dx.astype(BF)
            ggain_ref[0:1, :] = gain
            put(left, mm(mixed_ref[...], dy2_scr[...], TN))
            if second:
                g_ref[:, right] = ordered(gproj_ref[...]).astype(BF)
            dmixed_ref[...] = mm(dy2_scr[...], w_ref[:, left], NT).astype(BF)

    return kernel


def ffn_backward(
    slab, order, glen, x2, cot, dpool, x1, a2, mixed, act, slope, w_all, gain2, gain3, before, gproj
):
    rows, width = cot.shape[1:]
    chunks = w_all.shape[1] // (2 * width) - 1
    ff = chunks * width
    second = slab > 0
    side = pl.BlockSpec((rows, width), lambda i, _: (slab, jnp.minimum(i, chunks - 1)))
    once = pl.Buffered(1)
    mine = pl.BlockSpec((rows, width), lambda i, _: (slab, 0), pipeline_mode=once)
    part = pl.BlockSpec((width, 2 * width), lambda i, _: (0, i))
    in_specs = [
        mine,
        pl.BlockSpec((None, rows, width), lambda i, _: (slab, 0, 0), pipeline_mode=once),
        pl.BlockSpec((None,) + dpool.shape[1:], lambda i, _: (slab, 0, 0), pipeline_mode=once),
        mine,
        mine,
        mine,
        side,
        side,
        part,
        fixed((1, width)),
        fixed((1, width)),
    ]
    operands = [x2, cot, dpool, x1, a2, mixed, act, slope, w_all, gain2, gain3]
    if second:
        in_specs += [part, fixed((width, width))]
        operands += [before, gproj]
    return pl.pallas_call(
        ffn_bwd_kernel(slab, order),
        grid_spec=pltpu.PrefetchScalarGridSpec(
            num_scalar_prefetch=1,
            grid=(chunks + 1,),
            in_specs=in_specs,
            out_specs=[
                part,
                fixed((rows, width)),
                fixed((rows, width)),
                fixed((2, width)),
            ],
            scratch_shapes=[
                pltpu.VMEM((rows, width), F32),
                pltpu.VMEM((rows, width), BF),
                pltpu.VMEM((rows, width), F32),
                pltpu.VMEM((rows, width), BF),
            ],
        ),
        out_shape=[
            jax.ShapeDtypeStruct(w_all.shape, BF if second else F32),
            jax.ShapeDtypeStruct((rows, width), F32),
            jax.ShapeDtypeStruct((rows, width), BF),
            jax.ShapeDtypeStruct((2, width), F32),
        ],
        compiler_params=params(60),
        cost_estimate=cost(4 * rows * width * (width + 2 * ff), rows * width * 60),
        name="ffn_backward",
    )(glen, *operands)


def qkv_weight_kernel(a1_ref, d0_ref, d1_ref, w_ref, g_ref, gain_ref):
    rows, cols = d0_ref.shape[1:]
    total = mm(a1_ref[0:rows, :], d0_ref[0], TN) + mm(a1_ref[rows:, :], d1_ref[0], TN)
    g_ref[...] = total.astype(BF)
    prod = total * w_ref[...].astype(F32)
    part = prod[:, 0:TILE]
    for lane in range(1, cols // TILE):
        part = part + prod[:, lane * TILE : (lane + 1) * TILE]

    @pl.when(pl.program_id(0) == 0)
    def _():
        gain_ref[...] = part

    @pl.when(pl.program_id(0) > 0)
    def _():
        gain_ref[...] = gain_ref[...] + part


def qkv_weight_grads(a1, d, w, part, parts):
    rows, width = a1.shape
    cols = width // parts
    one = pl.BlockSpec((1, rows // 2, cols), lambda i: (i, 0, 0))
    return pl.pallas_call(
        qkv_weight_kernel,
        grid=(3,),
        in_specs=[
            fixed((rows, width)),
            one,
            one,
            pl.BlockSpec((width, cols), lambda i: (0, parts * i + part)),
        ],
        out_specs=[pl.BlockSpec((width, cols), lambda i: (0, i)), fixed((width, TILE))],
        out_shape=[
            jax.ShapeDtypeStruct((width, 3 * cols), BF),
            jax.ShapeDtypeStruct((width, TILE), F32),
        ],
        compiler_params=params(48),
        cost_estimate=cost(6 * rows * width * cols, rows * width * 10),
        name="qkv_weight_grads",
    )(a1, *d, w)


def qkv_input_kernel(x_ref, gain_ref, w_ref, dx1_ref, *refs):
    out_ref, parts = refs[-1], refs[:-1]
    width = x_ref.shape[1]
    grad = None
    for i in range(3):
        for part, d_ref in enumerate(parts):
            cols = d_ref.shape[2]
            at = i * width + part * cols
            term = mm(d_ref[i], w_ref[:, at : at + cols], NT)
            grad = term if grad is None else grad + term
    x = x_ref[...].astype(F32)
    r = lax.rsqrt(jnp.mean(x * x, axis=-1, keepdims=True) + 1e-06)
    hat = x * r
    d_hat = grad * gain_ref[...]
    dx = r * (d_hat - hat * jnp.mean(d_hat * hat, axis=-1, keepdims=True))
    out_ref[0] = dx + dx1_ref[...]


def qkv_input_grad(x, gain, w, d, dx1, slab, before):
    slabs, rows, width = x.shape
    block = 256
    spec = pl.BlockSpec((block, width), lambda i: (i, 0))
    in_specs = [
        pl.BlockSpec((None, block, width), lambda i: (slab, i, 0)),
        fixed((1, width)),
        fixed(w.shape),
        spec,
    ] + [pl.BlockSpec((3, block, part.shape[2]), lambda i: (0, i, 0)) for part in d]
    operands = [x, gain, w, dx1, *d]
    kernel, aliases = qkv_input_kernel, {}
    if before is not None:
        aliases = {len(operands): 0}
        in_specs.append(pl.BlockSpec(memory_space=pl.ANY))
        operands.append(before)

        def kernel(*refs):
            qkv_input_kernel(*refs[:-2], refs[-1])

    return pl.pallas_call(
        kernel,
        grid=(rows // block,),
        in_specs=in_specs,
        out_specs=pl.BlockSpec((1, block, width), lambda i: (slab, i, 0)),
        out_shape=jax.ShapeDtypeStruct((slabs, rows, width), F32),
        input_output_aliases=aliases,
        compiler_params=params(40),
        cost_estimate=cost(6 * rows * width * width, rows * width * 16),
        name="qkv_input_grad",
    )(*operands)


def bias_kernel(x_ref, near_ref):
    for delta in range(3):
        row = jnp.broadcast_to(x_ref[0, delta : delta + 1, :], (TILE, 2 * TILE))
        near_ref[0, delta] = pltpu.roll(row, 0, 1, stride=1, stride_axis=0)[:, :TILE]


def bias_tables(rel_bias, tiles):
    buckets, heads = rel_bias.shape
    lane = jnp.arange(2 * TILE, dtype=jnp.int32)
    back = jnp.where(lane < TILE, lane, lane - 2 * TILE)
    offsets = jnp.arange(-1, 2, dtype=jnp.int32)[:, None] * TILE - back[None, :]
    onehot = bucket_ids(offsets).reshape(1, -1) == jnp.arange(buckets, dtype=jnp.int32)[:, None]
    rows = jnp.einsum("bh,bn->hn", rel_bias, onehot.astype(F32), precision=lax.Precision.HIGHEST)
    near = pl.pallas_call(
        bias_kernel,
        grid=(heads,),
        in_specs=[pl.BlockSpec((1, 3, 2 * TILE), lambda i: (i, 0, 0))],
        out_specs=pl.BlockSpec((1, 3, TILE, TILE), lambda i: (i, 0, 0, 0)),
        out_shape=jax.ShapeDtypeStruct((heads, 3, TILE, TILE), F32),
        name="bias_tables",
    )(rows.reshape(heads, 3, 2 * TILE))
    qb = jnp.arange(tiles)[:, None]
    kb = jnp.arange(tiles)[None, :]
    left = rel_bias[buckets // 2 - 1][:, None, None]
    right = rel_bias[buckets - 1][:, None, None]
    far = jnp.where(kb >= qb + 2, right, jnp.where(kb <= qb - 2, left, 0.0))
    high = far.astype(BF)
    rest = (far - high.astype(F32)).astype(BF)
    tags = jnp.concatenate(
        [
            jnp.ones((heads, tiles, 1), BF),
            high,
            rest,
            jnp.zeros((heads, tiles, TILE - 1 - 2 * tiles), BF),
        ],
        axis=2,
    )
    return near, tags


def bias_grad(sums, buckets):
    heads = sums.shape[0]
    lane = jnp.arange(2 * TILE, dtype=jnp.int32)
    offsets = jnp.arange(-1, 2, dtype=jnp.int32)[:, None] * TILE + lane[None, :] - (TILE - 1)
    left = jnp.full((1, 2 * TILE), buckets // 2 - 1, jnp.int32)
    right = jnp.full((1, 2 * TILE), buckets - 1, jnp.int32)
    ids = jnp.concatenate([bucket_ids(offsets), left, right]).reshape(-1, 1)
    onehot = ids == jnp.arange(buckets, dtype=jnp.int32)[None, :]
    return jnp.einsum(
        "hn,nb->bh",
        sums[:, :5].reshape(heads, -1),
        onehot.astype(F32),
        precision=lax.Precision.HIGHEST,
    )


def swap(x, axis):
    return lax.ppermute(x, axis, [(0, 1), (1, 0)])


def both_halves(x, axis):
    first = lax.axis_index(axis) == 0
    other = swap(x, axis)
    return jnp.stack([jnp.where(first, x, other), jnp.where(first, other, x)])


def ring_gather(x, axis):
    count = lax.axis_size(axis)
    if count > 4:
        return lax.all_gather(x, axis)
    me = lax.axis_index(axis)
    out = jnp.zeros((count,) + x.shape, x.dtype)
    out = lax.dynamic_update_index_in_dim(out, x, me, 0)
    for k in range(1, count):
        part = lax.ppermute(x, axis, [(j, (j + k) % count) for j in range(count)])
        out = lax.dynamic_update_index_in_dim(out, part, (me - k) % count, 0)
    return out


def quick_gather(x):
    rows, columns = x.shape
    half = columns // 2
    cut = half // 2 // TILE * TILE
    low = lax.axis_index("core") == 0
    pair = both_halves(x, "core")
    mine = jnp.where(low, pair[..., :half], pair[..., half:])
    line = ring_gather(mine, "z")
    one = both_halves(both_halves(line[..., :cut], "x"), "tower")
    two = both_halves(both_halves(line[..., cut:], "tower"), "x")
    full = jnp.concatenate([one, jnp.swapaxes(two, 0, 1)], axis=-1)
    full = both_halves(full, "core")
    full = jnp.concatenate([full[0], full[1]], axis=-1)
    return jnp.swapaxes(full, 1, 2).reshape(-1, columns)


def after(x, *earlier):
    return lax.optimization_barrier((x,) + earlier)[0]


def send_half(x, axis, dim):
    me = lax.axis_index(axis)
    keep = lax.dynamic_index_in_dim(x, me, dim, keepdims=False)
    return keep, swap(lax.dynamic_index_in_dim(x, 1 - me, dim, keepdims=False), axis)


def join(keep, got):
    return (keep.astype(F32) + got.astype(F32)).astype(BF)


def by_device(x):
    sizes = tuple(lax.axis_size(a) for a in ("tower", "z", "x", "core"))
    return x.reshape(sizes + (-1, x.shape[-1]))


def scatter_order(shard):
    t, z, x, c = (lax.axis_size(a) for a in AXES)
    if shard % 8:
        return tuple(range(t * z * x * c))
    return tuple(
        ((i * z + j) * x + k) * c + n
        for i in range(t)
        for k in range(x)
        for n in range(c)
        for j in range(z)
    )


def quick_scatter(x):
    half = x.shape[-1] // 2 // TILE * TILE
    keep, got = send_half(by_device(x), "core", 3)
    x = join(keep, after(got, *(yield keep)))
    keep1, got1 = send_half(x[..., :half], "tower", 0)
    keep2, got2 = send_half(x[..., half:], "x", 2)
    earlier = yield x
    one, two = join(keep1, after(got1, *earlier)), join(keep2, after(got2, *earlier))
    keep1, got1 = send_half(one, "x", 1)
    keep2, got2 = send_half(two, "tower", 0)
    earlier = yield one, two
    one, two = join(keep1, after(got1, *earlier)), join(keep2, after(got2, *earlier))
    x = jnp.concatenate([one, two], axis=-1)
    count = lax.axis_size("z")
    if count > 4:
        yield x
        yield lax.psum_scatter(x, "z", scatter_dimension=0, tiled=False).astype(F32)
    me = lax.axis_index("z")
    total = lax.dynamic_index_in_dim(x, me, 0, keepdims=False).astype(F32)
    parts = []
    for k in range(1, count):
        part = lax.dynamic_index_in_dim(x, (me + k) % count, 0, keepdims=False)
        parts.append(lax.ppermute(part, "z", [(j, (j + k) % count) for j in range(count)]))
    earlier = yield x
    for part in parts:
        total = total + after(part, *earlier).astype(F32)
    yield total


def sum_everywhere(x):
    sent = jnp.broadcast_to(x[None], (lax.axis_size(AXES),) + x.shape)
    return jnp.sum(lax.all_to_all(sent, AXES, 0, 0, tiled=True), axis=0)


AXES = ("tower", "z", "x", "core")


def per_device(
    hidden,
    lengths,
    pairs,
    out_grad,
    w_query,
    w_key,
    w_value,
    w_attn_out,
    w_in,
    w_out,
    w_proj,
    gain_attn,
    gain_ffn,
    gain_final,
    rel_bias,
):
    devices = lax.axis_size(AXES)
    dp_count = devices // lax.axis_size("tower")
    is_doc = lax.axis_index("tower") == 1
    query_side = jnp.where(is_doc, 0.0, 1.0).astype(F32)
    rows, width = hidden.shape[3:]
    slots = lengths.shape[3]
    buckets, heads = rel_bias.shape
    shard, ff = w_in.shape
    chunks = ff // width
    first_slot = (jnp.arange(slots) == 0)[:, None]
    gain1, gain2, gain3 = gain_attn[None], gain_ffn[None], gain_final[None]
    x_all = hidden[0, 0].reshape(MICRO * rows, width)

    w_in = w_in.reshape(shard, devices, chunks, shard).swapaxes(1, 2).reshape(shard, ff)
    pieces = []
    for c in range(chunks):
        pieces.append(w_in[:, c * width : (c + 1) * width])
        pieces.append(w_out[c * shard : (c + 1) * shard])
    wqkv = quick_gather(jnp.concatenate([w_query, w_key, w_value], axis=1))
    w_all = lax.all_gather(
        jnp.concatenate(pieces + [w_attn_out, w_proj], axis=1), AXES, axis=0, tiled=True
    )
    w_proj_all = w_all[:, -width:]

    near_bias, tags = bias_tables(rel_bias, rows // TILE)
    a1, qkv, norms = project_qkv(x_all, gain1, wqkv)

    room = jnp.maximum(60.0 - jnp.max(jnp.abs(rel_bias)), 0.0)
    norms = jnp.max(norms, axis=0)
    small = jnp.all(norms[0] * norms[1] * 1.05 <= room * room).astype(jnp.int32)
    lens = lengths[0, 0]
    groups = jnp.arange(rows // GROUP, dtype=jnp.int32)
    per_group = jnp.clip(lens[:, 0:1] - GROUP * groups[None], 0, GROUP)
    glen = jnp.where(is_doc, per_group, lens).astype(jnp.int32)
    flags = jnp.broadcast_to(jnp.stack([is_doc.astype(jnp.int32), small]), (MICRO, 2))
    info = jnp.concatenate([flags[:, 0:1], lens[:, 0:1], flags[:, 1:2], glen], axis=1)
    glen = glen.reshape(-1)
    mixed, probs, linv = attention(info, qkv, tags, near_bias, heads)
    x1, a2, act, slope, x2, out, pool = ffn_forward(
        glen, x_all, mixed, w_all, gain2, gain3
    )
    pool = pool.reshape(MICRO, rows // GROUP, width)
    counts = jnp.maximum(lengths[0, 0].astype(F32), 1.0)[..., None]
    doc_pool = jnp.where(first_slot, jnp.sum(pool, axis=1, keepdims=True), 0.0)
    pooled = (jnp.where(is_doc, doc_pool, pool) / counts).astype(BF)
    projected = jnp.dot(
        pooled.reshape(MICRO * slots, width), w_proj_all, preferred_element_type=F32
    ).reshape(MICRO, slots, width)
    unit_vec, unit_pull = jax.vjp(unit_norm, projected)
    unit_low = unit_vec.astype(BF)
    sent = jnp.broadcast_to(unit_low[:, 0].reshape(1, -1, TILE), (devices, MICRO * width // TILE, TILE))
    docs = lax.all_to_all(sent, AXES, 0, 0, tiled=True)[dp_count:].reshape(-1, MICRO, width)
    logits = (
        jnp.einsum("msd,bmd->msb", unit_low, docs, preferred_element_type=F32) * logit_scale
    )
    row_max = jnp.max(logits, axis=-1, keepdims=True)
    log_total = row_max + jnp.log(jnp.sum(jnp.exp(logits - row_max), axis=-1, keepdims=True))
    chosen_mask = jnp.arange(dp_count, dtype=jnp.int32) == pairs[:, 0, :, None]
    chosen = jnp.sum(jnp.where(chosen_mask, logits, 0.0), axis=-1)
    loss_part = jnp.sum(log_total[..., 0] - chosen) * query_side
    logit_grad = (
        (jnp.exp(logits - log_total) - chosen_mask.astype(F32)) * query_side
    ).astype(BF)
    unit_grad = (
        jnp.einsum("msb,bmd->msd", logit_grad, docs, preferred_element_type=F32) * logit_scale
    )
    docs_grad = (
        jnp.einsum("msb,msd->bmd", logit_grad, unit_low, preferred_element_type=F32) * logit_scale
    )
    back = jnp.concatenate([jnp.zeros_like(docs_grad), docs_grad], axis=0)
    returned = jnp.sum(lax.all_to_all(back, AXES, 0, 0, tiled=True)[:dp_count], axis=0)
    unit_grad = unit_grad + jnp.where(first_slot & is_doc, returned[:, None], 0.0)
    proj_grad_in = unit_pull(unit_grad)[0].astype(BF)
    flat = proj_grad_in.reshape(MICRO * slots, width)
    grad_proj = mm(pooled.reshape(MICRO * slots, width), flat, TN)
    dpooled = jnp.dot(flat, w_proj_all.T, preferred_element_type=F32)
    dpooled = dpooled.reshape(MICRO, slots, width) / counts
    dpool = jnp.where(is_doc, jnp.broadcast_to(dpooled[:, 0:1], dpooled.shape), dpooled)

    order = scatter_order(shard)
    grads, ggains, backs = None, 0.0, []
    for m in range(MICRO):
        grads, dx1, d_mixed, ggain = ffn_backward(
            m,
            order,
            glen,
            x2,
            out_grad[0, 0],
            dpool,
            x1,
            a2,
            mixed,
            act,
            slope,
            w_all,
            gain2,
            gain3,
            grads,
            grad_proj,
        )
        backs.append((dx1, d_mixed))
        ggains = ggains + ggain

    if shard % 8:
        grad_all = lax.psum_scatter(grads, AXES, scatter_dimension=0, tiled=True).astype(F32)
    else:
        inner = lax.psum_scatter(grads, ("tower", "x", "core"), scatter_dimension=0, tiled=True)
    dqkvs, bias_sums = [], []
    for m in range(MICRO):
        dqkv, sums = attention_back(info, qkv, mixed, backs[m][1], probs, linv, m, 0, 1)
        dqkvs.append(dqkv)
        bias_sums.append(sums)
    piece, gain_part = qkv_weight_grads(a1, dqkvs, wqkv, 0, 1)
    flow = quick_scatter(piece)
    sent = next(flow)
    ggain1 = jnp.sum(gain_part, axis=1) / gain_attn
    bias_part = bias_grad(bias_sums[0] + bias_sums[1], buckets)
    smalls = jnp.concatenate(
        [ggain1, ggains[0], ggains[1], bias_part.reshape(-1), loss_part[None]]
    )
    pad = -smalls.shape[0] % (8 * TILE)
    smalls = jnp.pad(smalls, (0, pad)).reshape(-1, TILE)
    if shard % 8 == 0:
        sent = after(sent, inner)
        grad_all = lax.psum_scatter(inner, "z", scatter_dimension=0, tiled=True).astype(F32)
    input_grads = qkv_input_grad(
        hidden[0, 0], gain1, wqkv, dqkvs[:1], after(backs[0][0], sent), 0, None
    )
    sent = flow.send((input_grads,))
    input_grads = qkv_input_grad(
        hidden[0, 0], gain1, wqkv, dqkvs[1:], after(backs[1][0], sent), 1, input_grads
    )
    flow.send((input_grads,))
    totals = sum_everywhere(smalls).reshape(-1)
    flow.send(())
    grad_qkv = flow.send(()).reshape(shard, 3, width)
    grad_in = jnp.concatenate(
        [grad_all[:, 2 * c * width : (2 * c + 1) * width] for c in range(chunks)], axis=1
    )
    grad_in = grad_in.reshape(shard, chunks, devices, shard).swapaxes(1, 2).reshape(shard, ff)
    grad_out = jnp.concatenate(
        [grad_all[:, (2 * c + 1) * width : (2 * c + 2) * width] for c in range(chunks)], axis=0
    )
    grad_wo = grad_all[:, 2 * ff : 2 * ff + width]
    grad_proj = grad_all[:, 2 * ff + width :]

    return (
        out.reshape(hidden.shape),
        input_grads[None, None],
        totals[3 * width + buckets * heads] / (dp_count * slots * MICRO),
        grad_qkv[:, 0],
        grad_qkv[:, 1],
        grad_qkv[:, 2],
        grad_wo,
        grad_in,
        grad_out,
        grad_proj,
        totals[:width],
        totals[width : 2 * width],
        totals[2 * width : 3 * width],
        totals[3 * width : 3 * width + buckets * heads].reshape(buckets, heads),
    )


def solution(mesh):
    towers, per_tower = mesh.devices.shape
    fine = Mesh(mesh.devices.reshape(towers, per_tower // 4, 2, 2), AXES)
    dp = AXES[1:]
    rows = P(AXES, None)
    slabs = P("tower", dp, None, None, None)
    return jax.shard_map(
        per_device,
        mesh=fine,
        in_specs=(slabs, P("tower", dp, None, None), P(None, dp, None), slabs)
        + (rows,) * 7
        + (P(),) * 4,
        out_specs=(slabs, slabs, P()) + (rows,) * 7 + (P(),) * 4,
        check_vma=False,
    )
```

```python
import jax
import jax.numpy as jnp
from jax import lax
from jax.experimental import pallas as pl
from jax.experimental.pallas import tpu as pltpu
from jax.sharding import Mesh, PartitionSpec as P

bucket_steps = (12, 16, 23, 32, 46, 64, 91)
score_scale = 0.125
logit_scale = 64.0
negative = -1e30
MICRO = 2
TILE = 128
WIDE = 256
GROUP = 64

BF = jnp.bfloat16
F32 = jnp.float32
NN = (((1,), (0,)), ((), ()))
NT = (((1,), (1,)), ((), ()))
TN = (((0,), (0,)), ((), ()))
GELU_A = 0.7978845608028654
GELU_B = 0.044715


def mm(a, b, dims=NN):
    return lax.dot_general(a, b, dims, preferred_element_type=F32)


def params(megabytes):
    return pltpu.CompilerParams(vmem_limit_bytes=megabytes << 20)


def fixed(shape):
    zeros = (0,) * len(shape)
    return pl.BlockSpec(shape, lambda *_: zeros, pipeline_mode=pl.Buffered(1))


def cost(flops, data):
    return pl.CostEstimate(flops=int(flops), bytes_accessed=int(data), transcendentals=0)


def unit_norm(vector):
    return vector * lax.rsqrt(jnp.sum(vector * vector, axis=-1, keepdims=True) + 1e-06)


def bucket_ids(offset):
    distance = jnp.abs(offset)
    far_bucket = jnp.full(offset.shape, 8, jnp.int32)
    for threshold in bucket_steps:
        far_bucket = far_bucket + (distance >= threshold).astype(jnp.int32)
    bucket = jnp.where(distance < 8, distance, far_bucket)
    return bucket + 16 * (offset > 0).astype(jnp.int32)


def qkv_kernel(room_ref, x_ref, gain_ref, w_ref, a1_ref, qkv_ref, small_ref, norm_scr):
    x = x_ref[...].astype(F32)
    r = lax.rsqrt(jnp.mean(x * x, axis=-1, keepdims=True) + 1e-06)
    a1 = (x * r * gain_ref[...]).astype(BF)
    a1_ref[...] = a1
    width = a1.shape[1]
    row = lax.broadcasted_iota(jnp.int32, (width, TILE), 0)
    col = lax.broadcasted_iota(jnp.int32, (width, TILE), 1)
    of_head = jnp.where(row // GROUP == col, 1.0, 0.0).astype(BF)

    @pl.when(pl.program_id(0) == 0)
    def _():
        norm_scr[...] = jnp.zeros(norm_scr.shape, F32)

    for part in range(3):
        out = mm(a1, w_ref[:, part * width : (part + 1) * width]).astype(BF)
        if part == 0:
            out = out * BF(score_scale)
        qkv_ref[:, part * width : (part + 1) * width] = out
        if part < 2:
            square = mm(out * out, of_head)
            at = slice(part, part + 1)
            norm_scr[at, :] = jnp.maximum(
                norm_scr[at, :], jnp.max(square, axis=0, keepdims=True)
            )

    @pl.when(pl.program_id(0) == pl.num_programs(0) - 1)
    def _():
        reach = jnp.max(norm_scr[0:1, :] * norm_scr[1:2, :]) * 1.05
        room = room_ref[0, 0]
        small_ref[0, 0] = (reach <= room * room).astype(jnp.int32)


def project_qkv(room, x, gain, w):
    rows, width = x.shape
    block = 512
    return pl.pallas_call(
        qkv_kernel,
        grid=(rows // block,),
        in_specs=[
            pl.BlockSpec((1, 1), lambda i: (0, 0), memory_space=pltpu.SMEM),
            pl.BlockSpec((block, width), lambda i: (i, 0)),
            fixed((1, width)),
            fixed(w.shape),
        ],
        out_specs=[
            pl.BlockSpec((block, width), lambda i: (i, 0)),
            pl.BlockSpec((block, 3 * width), lambda i: (i, 0)),
            pl.BlockSpec((1, 1), lambda i: (0, 0), memory_space=pltpu.SMEM),
        ],
        out_shape=[
            jax.ShapeDtypeStruct((rows, width), BF),
            jax.ShapeDtypeStruct((rows, 3 * width), BF),
            jax.ShapeDtypeStruct((1, 1), jnp.int32),
        ],
        scratch_shapes=[pltpu.VMEM((8, TILE), F32)],
        compiler_params=params(60),
        cost_estimate=cost(6 * rows * width * width, rows * width * 10),
        name="norm_qkv",
    )(room, x, gain, w)


def lane_half(shape, head):
    lane = lax.broadcasted_iota(jnp.int32, shape, 1)
    return (lane // GROUP) == head


def key_extras(rows, length):
    row = lax.broadcasted_iota(jnp.int32, (rows, TILE), 0)
    col = lax.broadcasted_iota(jnp.int32, (rows, TILE), 1)
    block = row // TILE
    hit = (col - 1 == block) | (col - 1 - rows // TILE == block)
    ones = jnp.where(hit & (col > 0), 1.0, 0.0)
    return jnp.where(col == 0, jnp.where(row < length, 0.0, negative), ones).astype(BF)


def query_mask(info_ref, slab, tile):
    row = lax.broadcasted_iota(jnp.int32, (TILE, TILE), 0)
    col = lax.broadcasted_iota(jnp.int32, (TILE, TILE), 1)
    per = TILE // GROUP
    good = jnp.zeros((TILE, TILE), jnp.bool_)
    for s in range(per):
        low = s * GROUP
        inside = (row >= low) & (row < low + info_ref[slab, 2 + tile * per + s])
        good = good | (inside & (col >= low) & (col < low + GROUP))
    return good


def attn_fwd_kernel(
    info_ref, small_ref, q_ref, k_ref, v_ref, eq_ref, t_ref, o_ref, p_ref, linv_ref, s_scr, ot_scr
):
    rows = q_ref.shape[0]
    tiles = rows // TILE
    per = WIDE // TILE
    vt = v_ref[...].T
    below = [
        jnp.concatenate([vt[h * GROUP : (h + 1) * GROUP, :], jnp.ones((16, rows), BF)], axis=0)
        for h in range(2)
    ]
    work = [(head, wide) for head in range(2) for wide in range(rows // WIDE)]

    def near(s, head, kb, qb):
        return s + t_ref[head, kb - qb + 1] if abs(kb - qb) <= 1 else s

    def tagged(n):
        head, wide = work[n]
        tags = [
            jnp.broadcast_to(eq_ref[head, qb : qb + 1, :], (TILE, TILE))
            for qb in range(wide * per, (wide + 1) * per)
        ]
        cols = slice(wide * WIDE, (wide + 1) * WIDE)
        masked = jnp.where(lane_half((WIDE, TILE), head), q_ref[cols, :], BF(0))
        return jnp.concatenate([masked, jnp.concatenate(tags, axis=0)], axis=1)

    def mix(n):
        head, wide = work[n]
        cols = slice(wide * WIDE, (wide + 1) * WIDE)
        out = mm(below[head], p_ref[head, :, cols])
        inv = 1.0 / out[GROUP : GROUP + 1, :]
        ot_scr[head * GROUP : (head + 1) * GROUP, cols] = out[:GROUP, :] * inv
        linv_ref[0, head : head + 1, cols] = inv

    slab = pl.program_id(0)
    is_doc = info_ref[slab, 0] == 1
    small = small_ref[0, 0] == 1

    @pl.when(is_doc & small)
    def _():
        keys = jnp.concatenate([k_ref[...], key_extras(rows, info_ref[slab, 1])], axis=1)

        def weigh(n):
            head, wide = work[n]
            qa = tagged(n)
            for first in range(0, rows, WIDE):
                part = mm(keys[first : first + WIDE, :], qa, NT)
                for low in range(0, WIDE, TILE):
                    for sub in range(per):
                        kb, qb = (first + low) // TILE, wide * per + sub
                        s = part[low : low + TILE, sub * TILE : (sub + 1) * TILE]
                        p_ref[
                            head, kb * TILE : (kb + 1) * TILE, qb * TILE : (qb + 1) * TILE
                        ] = jnp.exp(near(s, head, kb, qb)).astype(BF)

        for n in range(len(work)):
            weigh(n)
            if n > 0:
                mix(n - 1)
        mix(len(work) - 1)

    @pl.when(is_doc & jnp.logical_not(small))
    def _():
        keys = jnp.concatenate([k_ref[...], key_extras(rows, info_ref[slab, 1])], axis=1)
        for n in range(len(work)):
            head, wide = work[n]
            part = mm(keys, tagged(n), NT)
            tops = [None] * per
            for kb in range(tiles):
                for sub in range(per):
                    at = (slice(kb * TILE, (kb + 1) * TILE), slice(sub * TILE, (sub + 1) * TILE))
                    s = near(part[at], head, kb, wide * per + sub)
                    s_scr[at] = s
                    tops[sub] = s if tops[sub] is None else jnp.maximum(tops[sub], s)
            top = jnp.concatenate([jnp.max(t, axis=0, keepdims=True) for t in tops], axis=1)
            for kb in range(tiles):
                at = slice(kb * TILE, (kb + 1) * TILE)
                p_ref[head, at, wide * WIDE : (wide + 1) * WIDE] = jnp.exp(
                    s_scr[at, :] - top
                ).astype(BF)
            mix(n)

    @pl.when(jnp.logical_not(is_doc))
    def _():
        spans = [slice(tile * TILE, (tile + 1) * TILE) for tile in range(tiles)]
        vo = jnp.concatenate([vt, jnp.ones((16, rows), BF)], axis=0)
        bias = jnp.concatenate([t_ref[0, 1], t_ref[1, 1]], axis=1)
        for at in spans:
            q = q_ref[at, :]
            both = [jnp.where(lane_half((TILE, TILE), head), q, BF(0)) for head in range(2)]
            s_scr[at, :] = mm(k_ref[at, :], jnp.concatenate(both, axis=0), NT)
        for tile, at in enumerate(spans):
            good = query_mask(info_ref, slab, tile)
            s = s_scr[at, :] + bias
            s = jnp.where(jnp.concatenate([good, good], axis=1), s, negative)
            p = jnp.exp(s - jnp.max(s, axis=0, keepdims=True)).astype(BF)
            p_ref[0, at, at] = p[:, :TILE]
            p_ref[1, at, at] = p[:, TILE:]
        for at in spans:
            out = mm(vo[:, at], jnp.concatenate([p_ref[0, at, at], p_ref[1, at, at]], axis=1))
            inv = 1.0 / out[TILE : TILE + 1, :]
            for head in range(2):
                lanes = slice(head * TILE, (head + 1) * TILE)
                mine = slice(head * GROUP, (head + 1) * GROUP)
                ot_scr[mine, at] = out[mine, lanes] * inv[:, lanes]
                linv_ref[0, head : head + 1, at] = inv[:, lanes]

    o_ref[...] = ot_scr[...].T.astype(BF)


def attention(info, small, qkv, tags, near, heads):
    slabs = info.shape[0]
    rows = qkv.shape[0] // slabs
    width = qkv.shape[1] // 3
    pairs = heads // 2
    return pl.pallas_call(
        attn_fwd_kernel,
        grid_spec=pltpu.PrefetchScalarGridSpec(
            num_scalar_prefetch=2,
            grid=(slabs, pairs),
            in_specs=[
                pl.BlockSpec((rows, TILE), lambda s, i, *_: (s, i)),
                pl.BlockSpec((rows, TILE), lambda s, i, *_: (s, pairs + i)),
                pl.BlockSpec((rows, TILE), lambda s, i, *_: (s, 2 * pairs + i)),
                pl.BlockSpec((2,) + tags.shape[1:], lambda s, i, *_: (i, 0, 0)),
                pl.BlockSpec((2,) + near.shape[1:], lambda s, i, *_: (i, 0, 0, 0)),
            ],
            out_specs=[
                pl.BlockSpec((rows, TILE), lambda s, i, *_: (s, i)),
                pl.BlockSpec((2, rows, rows), lambda s, i, *_: (s * pairs + i, 0, 0)),
                pl.BlockSpec((1, 2, rows), lambda s, i, *_: (s * pairs + i, 0, 0)),
            ],
            scratch_shapes=[pltpu.VMEM((rows, WIDE), F32), pltpu.VMEM((TILE, rows), F32)],
        ),
        out_shape=[
            jax.ShapeDtypeStruct((slabs * rows, width), BF),
            jax.ShapeDtypeStruct((slabs * heads, rows, rows), BF),
            jax.ShapeDtypeStruct((slabs * pairs, 2, rows), F32),
        ],
        compiler_params=params(60),
        cost_estimate=cost(slabs * heads * rows * rows * 512, slabs * heads * rows * rows * 2),
        name="attention_forward",
    )(info, small, qkv, qkv, qkv, tags, near)


def attn_bwd_kernel(
    info_ref,
    q_ref,
    k_ref,
    v_ref,
    o_ref,
    do_ref,
    p_ref,
    linv_ref,
    dqkv_ref,
    sums_ref,
    ds_scr,
    dqt_scr,
    far_scr,
):
    rows = q_ref.shape[0]
    tiles = rows // TILE
    square = (TILE, TILE)
    mirror = lax.broadcasted_iota(jnp.int32, square, 0) + lax.broadcasted_iota(jnp.int32, square, 1)
    mirror = jnp.where(mirror == TILE - 1, 1.0, 0.0)
    sums_ref[...] = jnp.zeros(sums_ref.shape, F32)

    def diagonals(x):
        x = lax.dot_general(
            x, mirror, NN, precision=lax.Precision.HIGHEST, preferred_element_type=F32
        )
        x = jnp.concatenate([x, jnp.zeros(square, F32)], axis=1)
        return jnp.sum(pltpu.roll(x, 0, 1, stride=1, stride_axis=0), axis=0, keepdims=True)

    col = lax.broadcasted_iota(jnp.int32, (rows, TILE), 1)
    kt = k_ref[...].T
    scale = jnp.concatenate([linv_ref[0], jnp.zeros((6, rows), F32)], axis=0).T
    d_out = do_ref[...].astype(F32)
    prod = d_out * o_ref[...].astype(F32)
    values = jnp.concatenate([v_ref[...], jnp.where(col < 2, 1.0, 0.0).astype(BF)], axis=1)

    def prepare(head):
        mine = lane_half((rows, TILE), head)
        inv = scale[:, head : head + 1]
        scaled = jnp.where(mine, d_out * inv, 0.0).astype(BF)
        shift = -jnp.sum(jnp.where(mine, prod, 0.0), axis=1, keepdims=True) * inv
        high = shift.astype(BF)
        rest = (shift - high.astype(F32)).astype(BF)
        extra = jnp.where(col == 0, high, jnp.where(col == 1, rest, BF(0)))
        masked = jnp.where(mine, q_ref[...], BF(0))
        return scaled, jnp.concatenate([scaled, extra], axis=1), masked

    @pl.when(info_ref[0, 0] == 1)
    def _():
        block = lax.broadcasted_iota(jnp.int32, (16, rows), 1) // TILE
        place = lax.broadcasted_iota(jnp.int32, (16, rows), 0)
        marks = jnp.where(block == place, 1.0, 0.0).astype(BF)
        ready = [prepare(head) for head in range(2)]
        ka = [
            jnp.concatenate([kt[head * GROUP : (head + 1) * GROUP, :], marks], axis=0)
            for head in range(2)
        ]
        work = [(head, wide) for head in range(2) for wide in range(rows // WIDE)]

        def slope(n):
            head, wide = work[n]
            cols = slice(wide * WIDE, (wide + 1) * WIDE)
            for first in range(0, rows, WIDE):
                at = slice(first, first + WIDE)
                dp = mm(values[at, :], ready[head][1][cols, :], NT)
                ds_scr[head, at, cols] = (p_ref[head, at, cols].astype(F32) * dp).astype(BF)

        def back(n):
            head, wide = work[n]
            cols = slice(wide * WIDE, (wide + 1) * WIDE)
            out = mm(ka[head], ds_scr[head, :, cols])
            dqt_scr[head * GROUP : (head + 1) * GROUP, cols] = out[:GROUP, :] * score_scale
            far_scr[head, :, cols] = out[GROUP : GROUP + tiles, :]

        for n in range(len(work)):
            slope(n)
            if n > 0:
                back(n - 1)
        back(len(work) - 1)
        dk = mm(ds_scr[0], ready[0][2]) + mm(ds_scr[1], ready[1][2])
        dv = mm(p_ref[0], ready[0][0]) + mm(p_ref[1], ready[1][0])
        for head in range(2):
            for delta in (-1, 0, 1):
                total = None
                for qb in range(tiles):
                    kb = qb + delta
                    if 0 <= kb < tiles:
                        part = ds_scr[
                            head, kb * TILE : (kb + 1) * TILE, qb * TILE : (qb + 1) * TILE
                        ].astype(F32)
                        total = part if total is None else total + part
                sums_ref[head, delta + 1 : delta + 2, :] = diagonals(total)
            kb = lax.broadcasted_iota(jnp.int32, (tiles, rows), 0)
            qb = lax.broadcasted_iota(jnp.int32, (tiles, rows), 1) // TILE
            for at, side in ((3, kb <= qb - 2), (4, kb >= qb + 2)):
                some = jnp.sum(jnp.where(side, far_scr[head], 0.0), axis=0, keepdims=True)
                sums_ref[head, at : at + 1, 0:TILE] = sum(
                    some[:, t * TILE : (t + 1) * TILE] for t in range(tiles)
                )
        dqkv_ref[1] = dk.astype(BF)
        dqkv_ref[2] = dv.astype(BF)

    @pl.when(info_ref[0, 0] == 0)
    def _():
        for head in range(2):
            scaled, outer, masked = prepare(head)
            total = None
            for tile in range(tiles):
                at = slice(tile * TILE, (tile + 1) * TILE)
                p = p_ref[head, at, at]
                dp = mm(values[at, :], outer[at, :], NT)
                part = p.astype(F32) * dp
                ds = part.astype(BF)
                total = part if total is None else total + part
                out = mm(kt[head * GROUP : (head + 1) * GROUP, at], ds)
                dqt_scr[head * GROUP : (head + 1) * GROUP, at] = out * score_scale
                dk = mm(ds, masked[at, :])
                dv = mm(p, scaled[at, :])
                if head == 0:
                    ds_scr[0, at, 0:TILE] = dk.astype(BF)
                    ds_scr[1, at, 0:TILE] = dv.astype(BF)
                else:
                    dqkv_ref[1, at, :] = ds_scr[0, at, 0:TILE] + dk.astype(BF)
                    dqkv_ref[2, at, :] = ds_scr[1, at, 0:TILE] + dv.astype(BF)
            sums_ref[head, 1:2, :] = diagonals(total)

    dqkv_ref[0] = dqt_scr[...].T.astype(BF)


def attention_back(info, qkv, mixed, d_mixed, probs, linv, slab, part, parts):
    slabs = info.shape[0]
    rows = qkv.shape[0] // slabs
    width = qkv.shape[1] // 3
    pairs = linv.shape[0] // slabs
    tiles = rows // TILE
    count = pairs // parts
    base = part * count
    heads = 2 * count
    return pl.pallas_call(
        attn_bwd_kernel,
        grid_spec=pltpu.PrefetchScalarGridSpec(
            num_scalar_prefetch=1,
            grid=(count,),
            in_specs=[
                pl.BlockSpec((rows, TILE), lambda i, _: (slab, base + i)),
                pl.BlockSpec((rows, TILE), lambda i, _: (slab, pairs + base + i)),
                pl.BlockSpec((rows, TILE), lambda i, _: (slab, 2 * pairs + base + i)),
                pl.BlockSpec((rows, TILE), lambda i, _: (slab, base + i)),
                pl.BlockSpec((rows, TILE), lambda i, _: (0, base + i)),
                pl.BlockSpec((2, rows, rows), lambda i, _: (slab * pairs + base + i, 0, 0)),
                pl.BlockSpec((1, 2, rows), lambda i, _: (slab * pairs + base + i, 0, 0)),
            ],
            out_specs=[
                pl.BlockSpec((3, rows, TILE), lambda i, _: (0, 0, i)),
                pl.BlockSpec((2, 8, 2 * TILE), lambda i, _: (i, 0, 0)),
            ],
            scratch_shapes=[
                pltpu.VMEM((2, rows, rows), BF),
                pltpu.VMEM((TILE, rows), F32),
                pltpu.VMEM((2, tiles, rows), F32),
            ],
        ),
        out_shape=[
            jax.ShapeDtypeStruct((3, rows, count * TILE), BF),
            jax.ShapeDtypeStruct((heads, 8, 2 * TILE), F32),
        ],
        compiler_params=params(60),
        cost_estimate=cost(heads * rows * rows * 1024, heads * rows * rows * 2),
        name="attention_backward",
    )(info, qkv, qkv, qkv, mixed, d_mixed, probs, linv)


def usable_rows(glen_ref, first, rows):
    row = lax.broadcasted_iota(jnp.int32, (rows, 1), 0)
    good = jnp.zeros((rows, 1), jnp.bool_)
    for g in range(rows // GROUP):
        low = g * GROUP
        good = good | ((row >= low) & (row < low + glen_ref[first + g]))
    return good


def ffn_fwd_kernel(
    glen_ref,
    x_ref,
    mixed_ref,
    w_ref,
    gain2_ref,
    gain3_ref,
    x1_ref,
    a2_ref,
    act_ref,
    slope_ref,
    x2_ref,
    out_ref,
    pool_ref,
):
    rows, width = x_ref.shape
    last = w_ref.shape[1] - 2 * width
    x1 = x_ref[...].astype(F32) + mm(mixed_ref[...], w_ref[:, last : last + width])
    x1_ref[...] = x1
    r = lax.rsqrt(jnp.mean(x1 * x1, axis=-1, keepdims=True) + 1e-06)
    a2 = (x1 * r * gain2_ref[...]).astype(BF)
    a2_ref[...] = a2
    total = x1
    for c in range(last // (2 * width)):
        at = slice(c * width, (c + 1) * width)
        into = 2 * c * width
        pre = mm(a2, w_ref[:, into : into + width])
        sq = pre * pre
        tanh = jnp.tanh(pre * (sq * (GELU_A * GELU_B) + GELU_A))
        half = 0.5 * tanh + 0.5
        act = pre * half
        slope = half + 2.0 * act * (1.0 - half) * (sq * (3 * GELU_A * GELU_B) + GELU_A)
        act = act.astype(BF)
        act_ref[:, at] = act
        slope_ref[:, at] = slope.astype(BF)
        total = total + mm(act, w_ref[:, into + width : into + 2 * width])
    x2_ref[...] = total
    out_ref[...] = total.astype(BF)
    r3 = lax.rsqrt(jnp.mean(total * total, axis=-1, keepdims=True) + 1e-06)
    a3 = total * r3 * gain3_ref[...]
    a3 = jnp.where(usable_rows(glen_ref, pl.program_id(0) * (rows // GROUP), rows), a3, 0.0)
    for g in range(rows // GROUP):
        pool_ref[0, g : g + 1, :] = jnp.sum(
            a3[g * GROUP : (g + 1) * GROUP, :], axis=0, keepdims=True
        )


def ffn_forward(glen, x, mixed, w_all, gain2, gain3):
    rows, width = x.shape
    ff = w_all.shape[1] // 2 - width
    block = 512
    groups = block // GROUP
    spec = pl.BlockSpec((block, width), lambda i, _: (i, 0))
    wide = pl.BlockSpec((block, ff), lambda i, _: (i, 0))
    out = pl.pallas_call(
        ffn_fwd_kernel,
        grid_spec=pltpu.PrefetchScalarGridSpec(
            num_scalar_prefetch=1,
            grid=(rows // block,),
            in_specs=[
                spec,
                spec,
                fixed(w_all.shape),
                fixed((1, width)),
                fixed((1, width)),
            ],
            out_specs=[
                spec,
                spec,
                wide,
                wide,
                spec,
                spec,
                pl.BlockSpec((1, groups, width), lambda i, _: (i, 0, 0)),
            ],
        ),
        out_shape=[
            jax.ShapeDtypeStruct((rows, width), F32),
            jax.ShapeDtypeStruct((rows, width), BF),
            jax.ShapeDtypeStruct((rows, ff), BF),
            jax.ShapeDtypeStruct((rows, ff), BF),
            jax.ShapeDtypeStruct((rows, width), F32),
            jax.ShapeDtypeStruct((rows, width), BF),
            jax.ShapeDtypeStruct((rows // block, groups, width), F32),
        ],
        compiler_params=params(60),
        cost_estimate=cost(2 * rows * width * (width + 2 * ff), rows * width * 40),
        name="ffn_forward",
    )(glen, x, mixed, w_all, gain2, gain3)
    return *out[:6], out[6].reshape(rows // GROUP, width)


def norm_back(x, gain, grad):
    r = lax.rsqrt(jnp.mean(x * x, axis=-1, keepdims=True) + 1e-06)
    hat = x * r
    d_gain = jnp.sum(grad * hat, axis=0, keepdims=True)
    d_hat = grad * gain
    dx = r * (d_hat - hat * jnp.mean(d_hat * hat, axis=-1, keepdims=True))
    return dx, d_gain


def ffn_bwd_kernel(slab, order):
    second = slab > 0

    def kernel(*refs):
        (
            glen_ref,
            x2_ref,
            cot_ref,
            dpool_ref,
            x1_ref,
            a2_ref,
            mixed_ref,
            act_ref,
            slope_ref,
            w_ref,
            gain2_ref,
            gain3_ref,
        ) = refs[:12]
        rest = refs[12:]
        if second:
            before_ref, gproj_ref = rest[:2]
            rest = rest[2:]
        (
            g_ref,
            dx1_ref,
            dmixed_ref,
            ggain_ref,
            dx2_scr,
            dy2_scr,
            da2_scr,
            dpre_scr,
            x1_scr,
            a2_scr,
            mixed_scr,
            sems,
        ) = rest
        rows, width = x2_ref.shape
        mine = pl.ds(slab * rows, rows)
        later = [
            pltpu.make_async_copy(hbm.at[mine], scr, sems.at[n])
            for n, (hbm, scr) in enumerate(
                ((a2_ref, a2_scr), (x1_ref, x1_scr), (mixed_ref, mixed_scr))
            )
        ]
        step = pl.program_id(0)
        last = pl.num_programs(0) - 1
        block = 256
        left, right = slice(0, width), slice(width, 2 * width)

        def put(side, value):
            if second:
                value = ordered(value + before_ref[:, side])
            g_ref[:, side] = value.astype(g_ref.dtype)

        def ordered(value):
            shard = value.shape[0] // len(order)
            return jnp.concatenate([value[d * shard : (d + 1) * shard, :] for d in order], axis=0)

        @pl.when(step == 0)
        def _():
            for copy in later:
                copy.start()
            gain = jnp.zeros((1, width), F32)
            for b in range(rows // block):
                at = slice(b * block, (b + 1) * block)
                per = block // GROUP
                grad = jnp.concatenate(
                    [
                        jnp.broadcast_to(dpool_ref[b * per + g : b * per + g + 1, :], (GROUP, width))
                        for g in range(per)
                    ],
                    axis=0,
                )
                grad = jnp.where(usable_rows(glen_ref, slab * (rows // GROUP) + b * per, block), grad, 0.0)
                dx, d_gain = norm_back(x2_ref[at, :], gain3_ref[...], grad)
                gain = gain + d_gain
                dx = dx + cot_ref[at, :].astype(F32)
                dx2_scr[at, :] = dx
                dy2_scr[at, :] = dx.astype(BF)
            ggain_ref[1:2, :] = gain
            da2_scr[...] = jnp.zeros_like(da2_scr)
            later[0].wait()

        @pl.when(step < last)
        def _():
            dact = mm(dy2_scr[...], w_ref[:, right], NT)
            dpre_scr[...] = (dact * slope_ref[...].astype(F32)).astype(BF)
            put(right, mm(act_ref[...], dy2_scr[...], TN))
            put(left, mm(a2_scr[...], dpre_scr[...], TN))
            da2_scr[...] = da2_scr[...] + mm(dpre_scr[...], w_ref[:, left], NT)

        @pl.when(step == last)
        def _():
            later[1].wait()
            later[2].wait()
            gain = jnp.zeros((1, width), F32)
            for b in range(rows // block):
                at = slice(b * block, (b + 1) * block)
                dx, d_gain = norm_back(x1_scr[at, :], gain2_ref[...], da2_scr[at, :])
                gain = gain + d_gain
                dx = dx + dx2_scr[at, :]
                dx1_ref[at, :] = dx
                dy2_scr[at, :] = dx.astype(BF)
            ggain_ref[0:1, :] = gain
            put(left, mm(mixed_scr[...], dy2_scr[...], TN))
            if second:
                g_ref[:, right] = ordered(gproj_ref[...]).astype(BF)
            dmixed_ref[...] = mm(dy2_scr[...], w_ref[:, left], NT).astype(BF)

    return kernel


def ffn_backward(
    slab, order, glen, x2, cot, dpool, x1, a2, mixed, act, slope, w_all, gain2, gain3, before, gproj
):
    rows, width = cot.shape[1:]
    chunks = w_all.shape[1] // (2 * width) - 1
    ff = chunks * width
    second = slab > 0
    side = pl.BlockSpec((rows, width), lambda i, _: (slab, jnp.minimum(i, chunks - 1)))
    once = pl.Buffered(1)
    mine = pl.BlockSpec((rows, width), lambda i, _: (slab, 0), pipeline_mode=once)
    part = pl.BlockSpec((width, 2 * width), lambda i, _: (0, i))
    in_specs = [
        mine,
        pl.BlockSpec((None, rows, width), lambda i, _: (slab, 0, 0), pipeline_mode=once),
        pl.BlockSpec((None,) + dpool.shape[1:], lambda i, _: (slab, 0, 0), pipeline_mode=once),
        pl.BlockSpec(memory_space=pl.ANY),
        pl.BlockSpec(memory_space=pl.ANY),
        pl.BlockSpec(memory_space=pl.ANY),
        side,
        side,
        part,
        fixed((1, width)),
        fixed((1, width)),
    ]
    operands = [x2, cot, dpool, x1, a2, mixed, act, slope, w_all, gain2, gain3]
    if second:
        in_specs += [part, fixed((width, width))]
        operands += [before, gproj]
    return pl.pallas_call(
        ffn_bwd_kernel(slab, order),
        grid_spec=pltpu.PrefetchScalarGridSpec(
            num_scalar_prefetch=1,
            grid=(chunks + 1,),
            in_specs=in_specs,
            out_specs=[
                part,
                fixed((rows, width)),
                fixed((rows, width)),
                fixed((2, width)),
            ],
            scratch_shapes=[
                pltpu.VMEM((rows, width), F32),
                pltpu.VMEM((rows, width), BF),
                pltpu.VMEM((rows, width), F32),
                pltpu.VMEM((rows, width), BF),
                pltpu.VMEM((rows, width), F32),
                pltpu.VMEM((rows, width), BF),
                pltpu.VMEM((rows, width), BF),
                pltpu.SemaphoreType.DMA((3,)),
            ],
        ),
        out_shape=[
            jax.ShapeDtypeStruct(w_all.shape, BF if second else F32),
            jax.ShapeDtypeStruct((rows, width), F32),
            jax.ShapeDtypeStruct((rows, width), BF),
            jax.ShapeDtypeStruct((2, width), F32),
        ],
        compiler_params=params(60),
        cost_estimate=cost(4 * rows * width * (width + 2 * ff), rows * width * 60),
        name="ffn_backward",
    )(glen, *operands)


def qkv_weight_kernel(a1_ref, d0_ref, d1_ref, w_ref, g_ref, gain_ref):
    rows, cols = d0_ref.shape[1:]
    total = mm(a1_ref[0:rows, :], d0_ref[0], TN) + mm(a1_ref[rows:, :], d1_ref[0], TN)
    g_ref[...] = total.astype(BF)
    prod = total * w_ref[...].astype(F32)
    part = prod[:, 0:TILE]
    for lane in range(1, cols // TILE):
        part = part + prod[:, lane * TILE : (lane + 1) * TILE]

    @pl.when(pl.program_id(0) == 0)
    def _():
        gain_ref[...] = part

    @pl.when(pl.program_id(0) > 0)
    def _():
        gain_ref[...] = gain_ref[...] + part


def qkv_weight_grads(a1, d, w, part, parts):
    rows, width = a1.shape
    cols = width // parts
    one = pl.BlockSpec((1, rows // 2, cols), lambda i: (i, 0, 0))
    return pl.pallas_call(
        qkv_weight_kernel,
        grid=(3,),
        in_specs=[
            fixed((rows, width)),
            one,
            one,
            pl.BlockSpec((width, cols), lambda i: (0, parts * i + part)),
        ],
        out_specs=[pl.BlockSpec((width, cols), lambda i: (0, i)), fixed((width, TILE))],
        out_shape=[
            jax.ShapeDtypeStruct((width, 3 * cols), BF),
            jax.ShapeDtypeStruct((width, TILE), F32),
        ],
        compiler_params=params(60),
        cost_estimate=cost(6 * rows * width * cols, rows * width * 10),
        name="qkv_weight_grads",
    )(a1, *d, w)


def qkv_input_kernel(x_ref, gain_ref, w_ref, dx1_ref, *refs):
    out_ref, parts = refs[-1], refs[:-1]
    width = x_ref.shape[1]
    grad = None
    for i in range(3):
        for part, d_ref in enumerate(parts):
            cols = d_ref.shape[2]
            at = i * width + part * cols
            term = mm(d_ref[i], w_ref[:, at : at + cols], NT)
            grad = term if grad is None else grad + term
    x = x_ref[...].astype(F32)
    r = lax.rsqrt(jnp.mean(x * x, axis=-1, keepdims=True) + 1e-06)
    hat = x * r
    d_hat = grad * gain_ref[...]
    dx = r * (d_hat - hat * jnp.mean(d_hat * hat, axis=-1, keepdims=True))
    out_ref[0] = dx + dx1_ref[...]


def qkv_input_grad(x, gain, w, d, dx1, slab, before):
    slabs, rows, width = x.shape
    block = 256
    spec = pl.BlockSpec((block, width), lambda i: (i, 0))
    in_specs = [
        pl.BlockSpec((None, block, width), lambda i: (slab, i, 0)),
        fixed((1, width)),
        fixed(w.shape),
        spec,
    ] + [pl.BlockSpec((3, block, part.shape[2]), lambda i: (0, i, 0)) for part in d]
    operands = [x, gain, w, dx1, *d]
    kernel, aliases = qkv_input_kernel, {}
    if before is not None:
        aliases = {len(operands): 0}
        in_specs.append(pl.BlockSpec(memory_space=pl.ANY))
        operands.append(before)

        def kernel(*refs):
            qkv_input_kernel(*refs[:-2], refs[-1])

    return pl.pallas_call(
        kernel,
        grid=(rows // block,),
        in_specs=in_specs,
        out_specs=pl.BlockSpec((1, block, width), lambda i: (slab, i, 0)),
        out_shape=jax.ShapeDtypeStruct((slabs, rows, width), F32),
        input_output_aliases=aliases,
        compiler_params=params(60),
        cost_estimate=cost(6 * rows * width * width, rows * width * 16),
        name="qkv_input_grad",
    )(*operands)


def bias_kernel(x_ref, near_ref):
    for head in range(x_ref.shape[0]):
        for delta in range(3):
            row = jnp.broadcast_to(x_ref[head, delta : delta + 1, :], (TILE, 2 * TILE))
            near_ref[head, delta] = pltpu.roll(row, 0, 1, stride=1, stride_axis=0)[:, :TILE]


def bias_tables(rel_bias, tiles):
    buckets, heads = rel_bias.shape
    lane = jnp.arange(2 * TILE, dtype=jnp.int32)
    back = jnp.where(lane < TILE, lane, lane - 2 * TILE)
    offsets = jnp.arange(-1, 2, dtype=jnp.int32)[:, None] * TILE - back[None, :]
    onehot = bucket_ids(offsets).reshape(1, -1) == jnp.arange(buckets, dtype=jnp.int32)[:, None]
    rows = jnp.einsum("bh,bn->hn", rel_bias, onehot.astype(F32), precision=lax.Precision.HIGHEST)
    near = pl.pallas_call(
        bias_kernel,
        grid=(2,),
        in_specs=[pl.BlockSpec((heads // 2, 3, 2 * TILE), lambda i: (i, 0, 0))],
        out_specs=pl.BlockSpec((heads // 2, 3, TILE, TILE), lambda i: (i, 0, 0, 0)),
        out_shape=jax.ShapeDtypeStruct((heads, 3, TILE, TILE), F32),
        name="bias_tables",
    )(rows.reshape(heads, 3, 2 * TILE))
    qb = jnp.arange(tiles)[:, None]
    kb = jnp.arange(tiles)[None, :]
    left = rel_bias[buckets // 2 - 1][:, None, None]
    right = rel_bias[buckets - 1][:, None, None]
    far = jnp.where(kb >= qb + 2, right, jnp.where(kb <= qb - 2, left, 0.0))
    high = far.astype(BF)
    rest = (far - high.astype(F32)).astype(BF)
    tags = jnp.concatenate(
        [
            jnp.ones((heads, tiles, 1), BF),
            high,
            rest,
            jnp.zeros((heads, tiles, TILE - 1 - 2 * tiles), BF),
        ],
        axis=2,
    )
    return near, tags


def bias_grad(sums, buckets):
    heads = sums.shape[0]
    lane = jnp.arange(2 * TILE, dtype=jnp.int32)
    offsets = jnp.arange(-1, 2, dtype=jnp.int32)[:, None] * TILE + lane[None, :] - (TILE - 1)
    left = jnp.full((1, 2 * TILE), buckets // 2 - 1, jnp.int32)
    right = jnp.full((1, 2 * TILE), buckets - 1, jnp.int32)
    ids = jnp.concatenate([bucket_ids(offsets), left, right]).reshape(-1, 1)
    onehot = ids == jnp.arange(buckets, dtype=jnp.int32)[None, :]
    return jnp.einsum(
        "hn,nb->bh",
        sums[:, :5].reshape(heads, -1),
        onehot.astype(F32),
        precision=lax.Precision.HIGHEST,
    )


def swap(x, axis):
    return lax.ppermute(x, axis, [(0, 1), (1, 0)])


def both_halves(x, axis):
    first = lax.axis_index(axis) == 0
    other = swap(x, axis)
    return jnp.stack([jnp.where(first, x, other), jnp.where(first, other, x)])


def ring_gather(x, axis):
    count = lax.axis_size(axis)
    if count > 4:
        return lax.all_gather(x, axis)
    me = lax.axis_index(axis)
    out = jnp.zeros((count,) + x.shape, x.dtype)
    out = lax.dynamic_update_index_in_dim(out, x, me, 0)
    for k in range(1, count):
        part = lax.ppermute(x, axis, [(j, (j + k) % count) for j in range(count)])
        out = lax.dynamic_update_index_in_dim(out, part, (me - k) % count, 0)
    return out


def quick_gather(x):
    columns = x.shape[-1]
    cut = columns // 2 // TILE * TILE
    line = ring_gather(x, "z")
    one = both_halves(both_halves(line[..., :cut], "x"), "tower")
    two = both_halves(both_halves(line[..., cut:], "tower"), "x")
    full = jnp.concatenate([one, jnp.swapaxes(two, 0, 1)], axis=-1)
    full = both_halves(full, "core")
    return jnp.transpose(full, (1, 3, 2, 0, 4, 5)).reshape(-1, columns)


def after(x, *earlier):
    return lax.optimization_barrier((x,) + earlier)[0]


def send_half(x, axis, dim):
    me = lax.axis_index(axis)
    keep = lax.dynamic_index_in_dim(x, me, dim, keepdims=False)
    return keep, swap(lax.dynamic_index_in_dim(x, 1 - me, dim, keepdims=False), axis)


def join(keep, got):
    return (keep.astype(F32) + got.astype(F32)).astype(BF)


def by_device(x):
    sizes = tuple(lax.axis_size(a) for a in ("tower", "z", "x", "core"))
    return x.reshape(sizes + (-1, x.shape[-1]))


def scatter_order(shard):
    t, z, x, c = (lax.axis_size(a) for a in AXES)
    if shard % 8:
        return tuple(range(t * z * x * c))
    return tuple(
        ((i * z + j) * x + k) * c + n
        for i in range(t)
        for k in range(x)
        for n in range(c)
        for j in range(z)
    )


def quick_scatter(x):
    half = x.shape[-1] // 2 // TILE * TILE
    keep, got = send_half(by_device(x), "core", 3)
    x = join(keep, after(got, *(yield keep)))
    keep1, got1 = send_half(x[..., :half], "tower", 0)
    keep2, got2 = send_half(x[..., half:], "x", 2)
    earlier = yield x
    one, two = join(keep1, after(got1, *earlier)), join(keep2, after(got2, *earlier))
    keep1, got1 = send_half(one, "x", 1)
    keep2, got2 = send_half(two, "tower", 0)
    earlier = yield one, two
    one, two = join(keep1, after(got1, *earlier)), join(keep2, after(got2, *earlier))
    x = jnp.concatenate([one, two], axis=-1)
    count = lax.axis_size("z")
    if count > 4:
        yield x
        yield lax.psum_scatter(x, "z", scatter_dimension=0, tiled=False).astype(F32)
    me = lax.axis_index("z")
    total = lax.dynamic_index_in_dim(x, me, 0, keepdims=False).astype(F32)
    parts = []
    for k in range(1, count):
        part = lax.dynamic_index_in_dim(x, (me + k) % count, 0, keepdims=False)
        parts.append(lax.ppermute(part, "z", [(j, (j + k) % count) for j in range(count)]))
    earlier = yield x
    for part in parts:
        total = total + after(part, *earlier).astype(F32)
    yield total


def broadcast(x):
    sent = jnp.broadcast_to(x[None], (lax.axis_size(AXES),) + x.shape)
    return lax.all_to_all(sent, AXES, 0, 0, tiled=True)


AXES = ("tower", "z", "x", "core")


def per_device(
    hidden,
    lengths,
    pairs,
    out_grad,
    w_query,
    w_key,
    w_value,
    w_attn_out,
    w_in,
    w_out,
    w_proj,
    gain_attn,
    gain_ffn,
    gain_final,
    rel_bias,
):
    devices = lax.axis_size(AXES)
    dp_count = devices // lax.axis_size("tower")
    is_doc = lax.axis_index("tower") == 1
    query_side = jnp.where(is_doc, 0.0, 1.0).astype(F32)
    rows, width = hidden.shape[3:]
    slots = lengths.shape[3]
    buckets, heads = rel_bias.shape
    shard, ff = w_in.shape
    chunks = ff // width
    first_slot = (jnp.arange(slots) == 0)[:, None]
    gain1, gain2, gain3 = gain_attn[None], gain_ffn[None], gain_final[None]
    x_all = hidden[0, 0].reshape(MICRO * rows, width)

    w_in = w_in.reshape(shard, devices, chunks, shard).swapaxes(1, 2).reshape(shard, ff)
    pieces = []
    for c in range(chunks):
        pieces.append(w_in[:, c * width : (c + 1) * width])
        pieces.append(w_out[c * shard : (c + 1) * shard])
    wqkv = quick_gather(jnp.concatenate([w_query, w_key, w_value], axis=1))
    w_all = lax.all_gather(
        jnp.concatenate(pieces + [w_attn_out, w_proj], axis=1), AXES, axis=0, tiled=True
    )
    w_proj_all = w_all[:, -width:]

    near_bias, tags = bias_tables(rel_bias, rows // TILE)
    room = jnp.maximum(60.0 - jnp.max(jnp.abs(rel_bias)), 0.0).reshape(1, 1)
    a1, qkv, small = project_qkv(room, x_all, gain1, wqkv)
    lens = lengths[0, 0]
    groups = jnp.arange(rows // GROUP, dtype=jnp.int32)
    per_group = jnp.clip(lens[:, 0:1] - GROUP * groups[None], 0, GROUP)
    glen = jnp.where(is_doc, per_group, lens).astype(jnp.int32)
    flag = jnp.broadcast_to(is_doc.astype(jnp.int32), (MICRO, 1))
    info = jnp.concatenate([flag, lens[:, 0:1], glen], axis=1)
    glen = glen.reshape(-1)
    mixed, probs, linv = attention(info, small, qkv, tags, near_bias, heads)
    x1, a2, act, slope, x2, out, pool = ffn_forward(
        glen, x_all, mixed, w_all, gain2, gain3
    )
    pool = pool.reshape(MICRO, rows // GROUP, width)
    counts = jnp.maximum(lengths[0, 0].astype(F32), 1.0)[..., None]
    doc_pool = jnp.where(first_slot, jnp.sum(pool, axis=1, keepdims=True), 0.0)
    pooled = (jnp.where(is_doc, doc_pool, pool) / counts).astype(BF)
    projected = jnp.dot(
        pooled.reshape(MICRO * slots, width), w_proj_all, preferred_element_type=F32
    ).reshape(MICRO, slots, width)
    unit_vec, unit_pull = jax.vjp(unit_norm, projected)
    unit_low = unit_vec.astype(BF)
    sent = jnp.broadcast_to(unit_low[None, :, 0].astype(F32), (devices, MICRO, width))
    docs = lax.optimization_barrier(lax.all_to_all(sent, AXES, 0, 0, tiled=True))
    docs = docs[dp_count:].astype(BF)
    logits = (
        jnp.einsum("msd,bmd->msb", unit_low, docs, preferred_element_type=F32) * logit_scale
    )
    row_max = jnp.max(logits, axis=-1, keepdims=True)
    log_total = row_max + jnp.log(jnp.sum(jnp.exp(logits - row_max), axis=-1, keepdims=True))
    chosen_mask = jnp.arange(dp_count, dtype=jnp.int32) == pairs[:, 0, :, None]
    chosen = jnp.sum(jnp.where(chosen_mask, logits, 0.0), axis=-1)
    loss_part = jnp.sum(log_total[..., 0] - chosen) * query_side
    logit_grad = (
        (jnp.exp(logits - log_total) - chosen_mask.astype(F32)) * query_side
    ).astype(BF)
    unit_grad = (
        jnp.einsum("msb,bmd->msd", logit_grad, docs, preferred_element_type=F32) * logit_scale
    )
    docs_grad = (
        jnp.einsum("msb,msd->bmd", logit_grad, unit_low, preferred_element_type=F32) * logit_scale
    )
    back = jnp.concatenate([jnp.zeros_like(docs_grad), docs_grad], axis=0)
    returned = jnp.sum(lax.all_to_all(back, AXES, 0, 0, tiled=True)[:dp_count], axis=0)
    unit_grad = unit_grad + jnp.where(first_slot & is_doc, returned[:, None], 0.0)
    proj_grad_in = unit_pull(unit_grad)[0].astype(BF)
    flat = proj_grad_in.reshape(MICRO * slots, width)
    grad_proj = mm(pooled.reshape(MICRO * slots, width), flat, TN)
    dpooled = jnp.dot(flat, w_proj_all.T, preferred_element_type=F32)
    dpooled = dpooled.reshape(MICRO, slots, width) / counts
    dpool = jnp.where(is_doc, jnp.broadcast_to(dpooled[:, 0:1], dpooled.shape), dpooled)

    order = scatter_order(shard)
    grads, ggains, backs = None, 0.0, []
    for m in range(MICRO):
        grads, dx1, d_mixed, ggain = ffn_backward(
            m,
            order,
            glen,
            x2,
            out_grad[0, 0],
            dpool,
            x1,
            a2,
            mixed,
            act,
            slope,
            w_all,
            gain2,
            gain3,
            grads,
            grad_proj,
        )
        backs.append((dx1, d_mixed))
        ggains = ggains + ggain

    if shard % 8:
        grad_all = lax.psum_scatter(grads, AXES, scatter_dimension=0, tiled=True).astype(F32)
    else:
        inner = lax.psum_scatter(grads, ("tower", "x", "core"), scatter_dimension=0, tiled=True)
    dqkvs, bias_sums = [], []
    for m in range(MICRO):
        dqkv, sums = attention_back(info, qkv, mixed, backs[m][1], probs, linv, m, 0, 1)
        dqkvs.append(dqkv)
        bias_sums.append(sums)
    piece, gain_part = qkv_weight_grads(a1, dqkvs, wqkv, 0, 1)
    if shard % 8 == 0:
        piece = after(piece, inner)
        grad_all = lax.psum_scatter(inner, "z", scatter_dimension=0, tiled=True).astype(F32)
    flow = quick_scatter(piece)
    sent = next(flow)
    ggain1 = jnp.sum(gain_part, axis=1) / gain_attn
    bias_part = bias_grad(bias_sums[0] + bias_sums[1], buckets)
    row = lax.broadcasted_iota(jnp.int32, (4, width), 0)
    lane = lax.broadcasted_iota(jnp.int32, (4, width), 1)
    used = buckets * heads
    bias_row = jnp.pad(bias_part.reshape(1, -1), ((0, 0), (0, width - used)))
    smalls = jnp.where(lane == used, loss_part, bias_row)
    for at, part in enumerate((ggain1[None], ggains[0:1], ggains[1:2])):
        smalls = jnp.where(row == at, part, smalls)
    everywhere = broadcast(smalls)
    input_grads = qkv_input_grad(
        hidden[0, 0], gain1, wqkv, dqkvs[:1], after(backs[0][0], sent), 0, None
    )
    sent = flow.send((input_grads,))
    input_grads = qkv_input_grad(
        hidden[0, 0], gain1, wqkv, dqkvs[1:], after(backs[1][0], sent), 1, input_grads
    )
    flow.send((input_grads,))
    flow.send(())
    totals = jnp.sum(everywhere, axis=0)
    grad_in = jnp.concatenate(
        [grad_all[:, 2 * c * width : (2 * c + 1) * width] for c in range(chunks)], axis=1
    )
    grad_in = grad_in.reshape(shard, chunks, devices, shard).swapaxes(1, 2).reshape(shard, ff)
    grad_out = jnp.concatenate(
        [grad_all[:, (2 * c + 1) * width : (2 * c + 2) * width] for c in range(chunks)], axis=0
    )
    grad_wo = grad_all[:, 2 * ff : 2 * ff + width]
    grad_proj = grad_all[:, 2 * ff + width :]

    grad_qkv = flow.send((grad_in,)).reshape(shard, 3, width)
    return (
        out.reshape(hidden.shape),
        input_grads[None, None],
        totals[3, used] / (dp_count * slots * MICRO),
        grad_qkv[:, 0],
        grad_qkv[:, 1],
        grad_qkv[:, 2],
        grad_wo,
        grad_in,
        grad_out,
        grad_proj,
        totals[0],
        totals[1],
        totals[2],
        totals[3, :used].reshape(buckets, heads),
    )


def solution(mesh):
    towers, per_tower = mesh.devices.shape
    fine = Mesh(mesh.devices.reshape(towers, per_tower // 4, 2, 2), AXES)
    dp = AXES[1:]
    rows = P(AXES, None)
    slabs = P("tower", dp, None, None, None)
    return jax.shard_map(
        per_device,
        mesh=fine,
        in_specs=(slabs, P("tower", dp, None, None), P(None, dp, None), slabs)
        + (rows,) * 7
        + (P(),) * 4,
        out_specs=(slabs, slabs, P()) + (rows,) * 7 + (P(),) * 4,
        check_vma=False,
    )
```

```python
import jax
import jax.numpy as jnp
from jax import lax
from jax.experimental import pallas as pl
from jax.experimental.pallas import tpu as pltpu
from jax.sharding import Mesh, PartitionSpec as P

bucket_steps = (12, 16, 23, 32, 46, 64, 91)
score_scale = 0.125
logit_scale = 64.0
negative = -1e30
MICRO = 2
TILE = 128
WIDE = 256
GROUP = 64

BF = jnp.bfloat16
F32 = jnp.float32
NN = (((1,), (0,)), ((), ()))
NT = (((1,), (1,)), ((), ()))
TN = (((0,), (0,)), ((), ()))
GELU_A = 0.7978845608028654
GELU_B = 0.044715


def mm(a, b, dims=NN):
    return lax.dot_general(a, b, dims, preferred_element_type=F32)


def params(megabytes):
    return pltpu.CompilerParams(vmem_limit_bytes=megabytes << 20)


def fixed(shape):
    zeros = (0,) * len(shape)
    return pl.BlockSpec(shape, lambda *_: zeros, pipeline_mode=pl.Buffered(1))


def cost(flops, data):
    return pl.CostEstimate(flops=int(flops), bytes_accessed=int(data), transcendentals=0)


def unit_norm(vector):
    return vector * lax.rsqrt(jnp.sum(vector * vector, axis=-1, keepdims=True) + 1e-06)


def bucket_ids(offset):
    distance = jnp.abs(offset)
    far_bucket = jnp.full(offset.shape, 8, jnp.int32)
    for threshold in bucket_steps:
        far_bucket = far_bucket + (distance >= threshold).astype(jnp.int32)
    bucket = jnp.where(distance < 8, distance, far_bucket)
    return bucket + 16 * (offset > 0).astype(jnp.int32)


def qkv_kernel(room_ref, x_ref, gain_ref, w_ref, a1_ref, qkv_ref, small_ref, norm_scr):
    x = x_ref[...].astype(F32)
    r = lax.rsqrt(jnp.mean(x * x, axis=-1, keepdims=True) + 1e-06)
    a1 = (x * r * gain_ref[...]).astype(BF)
    a1_ref[...] = a1
    width = a1.shape[1]
    row = lax.broadcasted_iota(jnp.int32, (width, TILE), 0)
    col = lax.broadcasted_iota(jnp.int32, (width, TILE), 1)
    of_head = jnp.where(row // GROUP == col, 1.0, 0.0).astype(BF)

    @pl.when(pl.program_id(0) == 0)
    def _():
        norm_scr[...] = jnp.zeros(norm_scr.shape, F32)

    for part in range(3):
        out = mm(a1, w_ref[:, part * width : (part + 1) * width]).astype(BF)
        if part == 0:
            out = out * BF(score_scale)
        qkv_ref[:, part * width : (part + 1) * width] = out
        if part < 2:
            square = mm(out * out, of_head)
            at = slice(part, part + 1)
            norm_scr[at, :] = jnp.maximum(
                norm_scr[at, :], jnp.max(square, axis=0, keepdims=True)
            )

    @pl.when(pl.program_id(0) == pl.num_programs(0) - 1)
    def _():
        reach = jnp.max(norm_scr[0:1, :] * norm_scr[1:2, :]) * 1.05
        room = room_ref[0, 0]
        small_ref[0, 0] = (reach <= room * room).astype(jnp.int32)


def project_qkv(room, x, gain, w):
    rows, width = x.shape
    block = 512
    return pl.pallas_call(
        qkv_kernel,
        grid=(rows // block,),
        in_specs=[
            pl.BlockSpec((1, 1), lambda i: (0, 0), memory_space=pltpu.SMEM),
            pl.BlockSpec((block, width), lambda i: (i, 0)),
            fixed((1, width)),
            fixed(w.shape),
        ],
        out_specs=[
            pl.BlockSpec((block, width), lambda i: (i, 0)),
            pl.BlockSpec((block, 3 * width), lambda i: (i, 0)),
            pl.BlockSpec((1, 1), lambda i: (0, 0), memory_space=pltpu.SMEM),
        ],
        out_shape=[
            jax.ShapeDtypeStruct((rows, width), BF),
            jax.ShapeDtypeStruct((rows, 3 * width), BF),
            jax.ShapeDtypeStruct((1, 1), jnp.int32),
        ],
        scratch_shapes=[pltpu.VMEM((8, TILE), F32)],
        compiler_params=params(60),
        cost_estimate=cost(6 * rows * width * width, rows * width * 10),
        name="norm_qkv",
    )(room, x, gain, w)


def lane_half(shape, head):
    lane = lax.broadcasted_iota(jnp.int32, shape, 1)
    return (lane // GROUP) == head


def key_extras(rows, length):
    row = lax.broadcasted_iota(jnp.int32, (rows, TILE), 0)
    col = lax.broadcasted_iota(jnp.int32, (rows, TILE), 1)
    block = row // TILE
    hit = (col - 1 == block) | (col - 1 - rows // TILE == block)
    ones = jnp.where(hit & (col > 0), 1.0, 0.0)
    return jnp.where(col == 0, jnp.where(row < length, 0.0, negative), ones).astype(BF)


def query_mask(info_ref, slab, tile):
    row = lax.broadcasted_iota(jnp.int32, (TILE, TILE), 0)
    col = lax.broadcasted_iota(jnp.int32, (TILE, TILE), 1)
    per = TILE // GROUP
    good = jnp.zeros((TILE, TILE), jnp.bool_)
    for s in range(per):
        low = s * GROUP
        inside = (row >= low) & (row < low + info_ref[slab, 2 + tile * per + s])
        good = good | (inside & (col >= low) & (col < low + GROUP))
    return good


def attn_fwd_kernel(
    info_ref, small_ref, q_ref, k_ref, v_ref, eq_ref, t_ref, o_ref, p_ref, linv_ref, s_scr, ot_scr
):
    rows = q_ref.shape[0]
    tiles = rows // TILE
    per = WIDE // TILE
    vt = v_ref[...].T
    below = [
        jnp.concatenate([vt[h * GROUP : (h + 1) * GROUP, :], jnp.ones((16, rows), BF)], axis=0)
        for h in range(2)
    ]
    work = [(head, wide) for head in range(2) for wide in range(rows // WIDE)]

    def near(s, head, kb, qb):
        return s + t_ref[head, kb - qb + 1] if abs(kb - qb) <= 1 else s

    def tagged(n):
        head, wide = work[n]
        tags = [
            jnp.broadcast_to(eq_ref[head, qb : qb + 1, :], (TILE, TILE))
            for qb in range(wide * per, (wide + 1) * per)
        ]
        cols = slice(wide * WIDE, (wide + 1) * WIDE)
        masked = jnp.where(lane_half((WIDE, TILE), head), q_ref[cols, :], BF(0))
        return jnp.concatenate([masked, jnp.concatenate(tags, axis=0)], axis=1)

    def mix(n):
        head, wide = work[n]
        cols = slice(wide * WIDE, (wide + 1) * WIDE)
        out = mm(below[head], p_ref[head, :, cols])
        inv = 1.0 / out[GROUP : GROUP + 1, :]
        ot_scr[head * GROUP : (head + 1) * GROUP, cols] = out[:GROUP, :] * inv
        linv_ref[0, head : head + 1, cols] = inv

    slab = pl.program_id(0)
    is_doc = info_ref[slab, 0] == 1
    small = small_ref[0, 0] == 1

    @pl.when(is_doc & small)
    def _():
        keys = jnp.concatenate([k_ref[...], key_extras(rows, info_ref[slab, 1])], axis=1)

        def weigh(n):
            head, wide = work[n]
            qa = tagged(n)
            for first in range(0, rows, WIDE):
                part = mm(keys[first : first + WIDE, :], qa, NT)
                for low in range(0, WIDE, TILE):
                    for sub in range(per):
                        kb, qb = (first + low) // TILE, wide * per + sub
                        s = part[low : low + TILE, sub * TILE : (sub + 1) * TILE]
                        p_ref[
                            head, kb * TILE : (kb + 1) * TILE, qb * TILE : (qb + 1) * TILE
                        ] = jnp.exp(near(s, head, kb, qb)).astype(BF)

        for n in range(len(work)):
            weigh(n)
            if n > 0:
                mix(n - 1)
        mix(len(work) - 1)

    @pl.when(is_doc & jnp.logical_not(small))
    def _():
        keys = jnp.concatenate([k_ref[...], key_extras(rows, info_ref[slab, 1])], axis=1)
        for n in range(len(work)):
            head, wide = work[n]
            part = mm(keys, tagged(n), NT)
            tops = [None] * per
            for kb in range(tiles):
                for sub in range(per):
                    at = (slice(kb * TILE, (kb + 1) * TILE), slice(sub * TILE, (sub + 1) * TILE))
                    s = near(part[at], head, kb, wide * per + sub)
                    s_scr[at] = s
                    tops[sub] = s if tops[sub] is None else jnp.maximum(tops[sub], s)
            top = jnp.concatenate([jnp.max(t, axis=0, keepdims=True) for t in tops], axis=1)
            for kb in range(tiles):
                at = slice(kb * TILE, (kb + 1) * TILE)
                p_ref[head, at, wide * WIDE : (wide + 1) * WIDE] = jnp.exp(
                    s_scr[at, :] - top
                ).astype(BF)
            mix(n)

    @pl.when(jnp.logical_not(is_doc))
    def _():
        spans = [slice(tile * TILE, (tile + 1) * TILE) for tile in range(tiles)]
        vo = jnp.concatenate([vt, jnp.ones((16, rows), BF)], axis=0)
        bias = jnp.concatenate([t_ref[0, 1], t_ref[1, 1]], axis=1)
        for at in spans:
            q = q_ref[at, :]
            both = [jnp.where(lane_half((TILE, TILE), head), q, BF(0)) for head in range(2)]
            s_scr[at, :] = mm(k_ref[at, :], jnp.concatenate(both, axis=0), NT)
        for tile, at in enumerate(spans):
            good = query_mask(info_ref, slab, tile)
            s = s_scr[at, :] + bias
            s = jnp.where(jnp.concatenate([good, good], axis=1), s, negative)
            p = jnp.exp(s - jnp.max(s, axis=0, keepdims=True)).astype(BF)
            p_ref[0, at, at] = p[:, :TILE]
            p_ref[1, at, at] = p[:, TILE:]
        for at in spans:
            out = mm(vo[:, at], jnp.concatenate([p_ref[0, at, at], p_ref[1, at, at]], axis=1))
            inv = 1.0 / out[TILE : TILE + 1, :]
            for head in range(2):
                lanes = slice(head * TILE, (head + 1) * TILE)
                mine = slice(head * GROUP, (head + 1) * GROUP)
                ot_scr[mine, at] = out[mine, lanes] * inv[:, lanes]
                linv_ref[0, head : head + 1, at] = inv[:, lanes]

    o_ref[...] = ot_scr[...].T.astype(BF)


def attention(info, small, qkv, tags, near, heads):
    slabs = info.shape[0]
    rows = qkv.shape[0] // slabs
    width = qkv.shape[1] // 3
    pairs = heads // 2
    return pl.pallas_call(
        attn_fwd_kernel,
        grid_spec=pltpu.PrefetchScalarGridSpec(
            num_scalar_prefetch=2,
            grid=(slabs, pairs),
            in_specs=[
                pl.BlockSpec((rows, TILE), lambda s, i, *_: (s, i)),
                pl.BlockSpec((rows, TILE), lambda s, i, *_: (s, pairs + i)),
                pl.BlockSpec((rows, TILE), lambda s, i, *_: (s, 2 * pairs + i)),
                pl.BlockSpec((2,) + tags.shape[1:], lambda s, i, *_: (i, 0, 0)),
                pl.BlockSpec((2,) + near.shape[1:], lambda s, i, *_: (i, 0, 0, 0)),
            ],
            out_specs=[
                pl.BlockSpec((rows, TILE), lambda s, i, *_: (s, i)),
                pl.BlockSpec((2, rows, rows), lambda s, i, *_: (s * pairs + i, 0, 0)),
                pl.BlockSpec((1, 2, rows), lambda s, i, *_: (s * pairs + i, 0, 0)),
            ],
            scratch_shapes=[pltpu.VMEM((rows, WIDE), F32), pltpu.VMEM((TILE, rows), F32)],
        ),
        out_shape=[
            jax.ShapeDtypeStruct((slabs * rows, width), BF),
            jax.ShapeDtypeStruct((slabs * heads, rows, rows), BF),
            jax.ShapeDtypeStruct((slabs * pairs, 2, rows), F32),
        ],
        compiler_params=params(60),
        cost_estimate=cost(slabs * heads * rows * rows * 512, slabs * heads * rows * rows * 2),
        name="attention_forward",
    )(info, small, qkv, qkv, qkv, tags, near)


def attn_bwd_kernel(
    info_ref,
    q_ref,
    k_ref,
    v_ref,
    o_ref,
    do_ref,
    p_ref,
    linv_ref,
    dqkv_ref,
    sums_ref,
    ds_scr,
    dqt_scr,
    far_scr,
):
    rows = q_ref.shape[0]
    tiles = rows // TILE
    square = (TILE, TILE)
    mirror = lax.broadcasted_iota(jnp.int32, square, 0) + lax.broadcasted_iota(jnp.int32, square, 1)
    mirror = jnp.where(mirror == TILE - 1, 1.0, 0.0)
    sums_ref[...] = jnp.zeros(sums_ref.shape, F32)

    def diagonals(x):
        x = lax.dot_general(
            x, mirror, NN, precision=lax.Precision.HIGHEST, preferred_element_type=F32
        )
        x = jnp.concatenate([x, jnp.zeros(square, F32)], axis=1)
        return jnp.sum(pltpu.roll(x, 0, 1, stride=1, stride_axis=0), axis=0, keepdims=True)

    col = lax.broadcasted_iota(jnp.int32, (rows, TILE), 1)
    kt = k_ref[...].T
    scale = jnp.concatenate([linv_ref[0], jnp.zeros((6, rows), F32)], axis=0).T
    d_out = do_ref[...].astype(F32)
    prod = d_out * o_ref[...].astype(F32)
    values = jnp.concatenate([v_ref[...], jnp.where(col < 2, 1.0, 0.0).astype(BF)], axis=1)

    def prepare(head):
        mine = lane_half((rows, TILE), head)
        inv = scale[:, head : head + 1]
        scaled = jnp.where(mine, d_out * inv, 0.0).astype(BF)
        shift = -jnp.sum(jnp.where(mine, prod, 0.0), axis=1, keepdims=True) * inv
        high = shift.astype(BF)
        rest = (shift - high.astype(F32)).astype(BF)
        extra = jnp.where(col == 0, high, jnp.where(col == 1, rest, BF(0)))
        masked = jnp.where(mine, q_ref[...], BF(0))
        return scaled, jnp.concatenate([scaled, extra], axis=1), masked

    is_doc = info_ref[0, 0] == 1

    @pl.when(is_doc)
    def _():
        block = lax.broadcasted_iota(jnp.int32, (16, rows), 1) // TILE
        place = lax.broadcasted_iota(jnp.int32, (16, rows), 0)
        marks = jnp.where(block == place, 1.0, 0.0).astype(BF)
        ready = [prepare(head) for head in range(2)]
        ka = [
            jnp.concatenate([kt[head * GROUP : (head + 1) * GROUP, :], marks], axis=0)
            for head in range(2)
        ]
        work = [(head, wide) for head in range(2) for wide in range(rows // WIDE)]

        def slope(n):
            head, wide = work[n]
            cols = slice(wide * WIDE, (wide + 1) * WIDE)
            for first in range(0, rows, WIDE):
                at = slice(first, first + WIDE)
                dp = mm(values[at, :], ready[head][1][cols, :], NT)
                ds_scr[head, at, cols] = (p_ref[head, at, cols].astype(F32) * dp).astype(BF)

        def back(n):
            head, wide = work[n]
            cols = slice(wide * WIDE, (wide + 1) * WIDE)
            out = mm(ka[head], ds_scr[head, :, cols])
            dqt_scr[head * GROUP : (head + 1) * GROUP, cols] = out[:GROUP, :] * score_scale
            far_scr[head, :, cols] = out[GROUP : GROUP + tiles, :]

        for n in range(len(work)):
            slope(n)
            if n > 0:
                back(n - 1)
        back(len(work) - 1)
        dk = mm(ds_scr[0], ready[0][2]) + mm(ds_scr[1], ready[1][2])
        dv = mm(p_ref[0], ready[0][0]) + mm(p_ref[1], ready[1][0])
        for head in range(2):
            for delta in (-1, 0, 1):
                total = None
                for qb in range(tiles):
                    kb = qb + delta
                    if 0 <= kb < tiles:
                        part = ds_scr[
                            head, kb * TILE : (kb + 1) * TILE, qb * TILE : (qb + 1) * TILE
                        ].astype(F32)
                        total = part if total is None else total + part
                sums_ref[head, delta + 1 : delta + 2, :] = diagonals(total)
            kb = lax.broadcasted_iota(jnp.int32, (tiles, rows), 0)
            qb = lax.broadcasted_iota(jnp.int32, (tiles, rows), 1) // TILE
            for at, side in ((3, kb <= qb - 2), (4, kb >= qb + 2)):
                some = jnp.sum(jnp.where(side, far_scr[head], 0.0), axis=0, keepdims=True)
                sums_ref[head, at : at + 1, 0:TILE] = sum(
                    some[:, t * TILE : (t + 1) * TILE] for t in range(tiles)
                )
        dqkv_ref[1] = dk.astype(BF)
        dqkv_ref[2] = dv.astype(BF)

    @pl.when(jnp.logical_not(is_doc))
    def _():
        for head in range(2):
            scaled, outer, masked = prepare(head)
            total = None
            for tile in range(tiles):
                at = slice(tile * TILE, (tile + 1) * TILE)
                p = p_ref[head, at, at]
                dp = mm(values[at, :], outer[at, :], NT)
                part = p.astype(F32) * dp
                ds = part.astype(BF)
                total = part if total is None else total + part
                out = mm(kt[head * GROUP : (head + 1) * GROUP, at], ds)
                dqt_scr[head * GROUP : (head + 1) * GROUP, at] = out * score_scale
                dk = mm(ds, masked[at, :])
                dv = mm(p, scaled[at, :])
                if head == 0:
                    ds_scr[0, at, 0:TILE] = dk.astype(BF)
                    ds_scr[1, at, 0:TILE] = dv.astype(BF)
                else:
                    dqkv_ref[1, at, :] = ds_scr[0, at, 0:TILE] + dk.astype(BF)
                    dqkv_ref[2, at, :] = ds_scr[1, at, 0:TILE] + dv.astype(BF)
            sums_ref[head, 1:2, :] = diagonals(total)

    dqkv_ref[0] = dqt_scr[...].T.astype(BF)


def attention_back(info, qkv, mixed, d_mixed, probs, linv):
    slabs = info.shape[0]
    rows = qkv.shape[0] // slabs
    width = qkv.shape[1] // 3
    pairs = linv.shape[0] // slabs
    tiles = rows // TILE
    heads = 2 * pairs
    return pl.pallas_call(
        attn_bwd_kernel,
        grid_spec=pltpu.PrefetchScalarGridSpec(
            num_scalar_prefetch=1,
            grid=(slabs, pairs),
            in_specs=[
                pl.BlockSpec((rows, TILE), lambda s, i, _: (s, i)),
                pl.BlockSpec((rows, TILE), lambda s, i, _: (s, pairs + i)),
                pl.BlockSpec((rows, TILE), lambda s, i, _: (s, 2 * pairs + i)),
                pl.BlockSpec((rows, TILE), lambda s, i, _: (s, i)),
                pl.BlockSpec((rows, TILE), lambda s, i, _: (s, i)),
                pl.BlockSpec((2, rows, rows), lambda s, i, _: (s * pairs + i, 0, 0)),
                pl.BlockSpec((1, 2, rows), lambda s, i, _: (s * pairs + i, 0, 0)),
            ],
            out_specs=[
                pl.BlockSpec((3, rows, TILE), lambda s, i, _: (0, s, i)),
                pl.BlockSpec((2, 8, 2 * TILE), lambda s, i, _: (s * pairs + i, 0, 0)),
            ],
            scratch_shapes=[
                pltpu.VMEM((2, rows, rows), BF),
                pltpu.VMEM((TILE, rows), F32),
                pltpu.VMEM((2, tiles, rows), F32),
            ],
        ),
        out_shape=[
            jax.ShapeDtypeStruct((3, slabs * rows, width), BF),
            jax.ShapeDtypeStruct((slabs * heads, 8, 2 * TILE), F32),
        ],
        compiler_params=params(60),
        cost_estimate=cost(slabs * heads * rows * rows * 1024, slabs * heads * rows * rows * 2),
        name="attention_backward",
    )(info, qkv, qkv, qkv, mixed, d_mixed, probs, linv)


def usable_rows(glen_ref, first, rows):
    row = lax.broadcasted_iota(jnp.int32, (rows, 1), 0)
    good = jnp.zeros((rows, 1), jnp.bool_)
    for g in range(rows // GROUP):
        low = g * GROUP
        good = good | ((row >= low) & (row < low + glen_ref[first + g]))
    return good


def ffn_fwd_kernel(
    glen_ref,
    x_ref,
    mixed_ref,
    w_ref,
    gain2_ref,
    gain3_ref,
    x1_ref,
    a2_ref,
    act_ref,
    slope_ref,
    x2_ref,
    out_ref,
    pool_ref,
):
    rows, width = x_ref.shape
    last = w_ref.shape[1] - 2 * width
    x1 = x_ref[...].astype(F32) + mm(mixed_ref[...], w_ref[:, last : last + width])
    x1_ref[...] = x1
    r = lax.rsqrt(jnp.mean(x1 * x1, axis=-1, keepdims=True) + 1e-06)
    a2 = (x1 * r * gain2_ref[...]).astype(BF)
    a2_ref[...] = a2
    total = x1
    for c in range(last // (2 * width)):
        at = slice(c * width, (c + 1) * width)
        into = 2 * c * width
        pre = mm(a2, w_ref[:, into : into + width])
        sq = pre * pre
        tanh = jnp.tanh(pre * (sq * (GELU_A * GELU_B) + GELU_A))
        half = 0.5 * tanh + 0.5
        act = pre * half
        slope = half + 2.0 * act * (1.0 - half) * (sq * (3 * GELU_A * GELU_B) + GELU_A)
        act = act.astype(BF)
        act_ref[:, at] = act
        slope_ref[:, at] = slope.astype(BF)
        total = total + mm(act, w_ref[:, into + width : into + 2 * width])
    x2_ref[...] = total
    out_ref[...] = total.astype(BF)
    r3 = lax.rsqrt(jnp.mean(total * total, axis=-1, keepdims=True) + 1e-06)
    a3 = total * r3 * gain3_ref[...]
    a3 = jnp.where(usable_rows(glen_ref, pl.program_id(0) * (rows // GROUP), rows), a3, 0.0)
    for g in range(rows // GROUP):
        pool_ref[0, g : g + 1, :] = jnp.sum(
            a3[g * GROUP : (g + 1) * GROUP, :], axis=0, keepdims=True
        )


def ffn_forward(glen, x, mixed, w_all, gain2, gain3):
    rows, width = x.shape
    ff = w_all.shape[1] // 2 - width
    block = 512
    groups = block // GROUP
    spec = pl.BlockSpec((block, width), lambda i, _: (i, 0))
    wide = pl.BlockSpec((block, ff), lambda i, _: (i, 0))
    out = pl.pallas_call(
        ffn_fwd_kernel,
        grid_spec=pltpu.PrefetchScalarGridSpec(
            num_scalar_prefetch=1,
            grid=(rows // block,),
            in_specs=[
                spec,
                spec,
                fixed(w_all.shape),
                fixed((1, width)),
                fixed((1, width)),
            ],
            out_specs=[
                spec,
                spec,
                wide,
                wide,
                spec,
                spec,
                pl.BlockSpec((1, groups, width), lambda i, _: (i, 0, 0)),
            ],
        ),
        out_shape=[
            jax.ShapeDtypeStruct((rows, width), F32),
            jax.ShapeDtypeStruct((rows, width), BF),
            jax.ShapeDtypeStruct((rows, ff), BF),
            jax.ShapeDtypeStruct((rows, ff), BF),
            jax.ShapeDtypeStruct((rows, width), F32),
            jax.ShapeDtypeStruct((rows, width), BF),
            jax.ShapeDtypeStruct((rows // block, groups, width), F32),
        ],
        compiler_params=params(60),
        cost_estimate=cost(2 * rows * width * (width + 2 * ff), rows * width * 40),
        name="ffn_forward",
    )(glen, x, mixed, w_all, gain2, gain3)
    return *out[:6], out[6].reshape(rows // GROUP, width)


def norm_back(x, gain, grad):
    r = lax.rsqrt(jnp.mean(x * x, axis=-1, keepdims=True) + 1e-06)
    hat = x * r
    d_gain = jnp.sum(grad * hat, axis=0, keepdims=True)
    d_hat = grad * gain
    dx = r * (d_hat - hat * jnp.mean(d_hat * hat, axis=-1, keepdims=True))
    return dx, d_gain


def ffn_bwd_kernel(slab, order):
    second = slab > 0

    def kernel(*refs):
        (
            glen_ref,
            x2_ref,
            cot_ref,
            dpool_ref,
            x1_ref,
            a2_ref,
            mixed_ref,
            act_ref,
            slope_ref,
            w_ref,
            gain2_ref,
            gain3_ref,
        ) = refs[:12]
        rest = refs[12:]
        if second:
            before_ref, gproj_ref = rest[:2]
            rest = rest[4:]
        (
            g_ref,
            dx1_ref,
            dmixed_ref,
            ggain_ref,
            dx2_scr,
            dy2_scr,
            da2_scr,
            dpre_scr,
            x1_scr,
            a2_scr,
            mixed_scr,
            sems,
        ) = rest
        rows, width = x2_ref.shape
        mine = pl.ds(slab * rows, rows)
        later = [
            pltpu.make_async_copy(hbm.at[mine], scr, sems.at[n])
            for n, (hbm, scr) in enumerate(
                ((a2_ref, a2_scr), (x1_ref, x1_scr), (mixed_ref, mixed_scr))
            )
        ]
        step = pl.program_id(0)
        last = pl.num_programs(0) - 1
        block = 256
        left, right = slice(0, width), slice(width, 2 * width)

        def put(side, value):
            if second:
                value = ordered(value + before_ref[:, side])
            g_ref[:, side] = value.astype(g_ref.dtype)

        def ordered(value):
            shard = value.shape[0] // len(order)
            return jnp.concatenate([value[d * shard : (d + 1) * shard, :] for d in order], axis=0)

        @pl.when(step == 0)
        def _():
            for copy in later:
                copy.start()
            gain = jnp.zeros((1, width), F32)
            for b in range(rows // block):
                at = slice(b * block, (b + 1) * block)
                per = block // GROUP
                grad = jnp.concatenate(
                    [
                        jnp.broadcast_to(dpool_ref[b * per + g : b * per + g + 1, :], (GROUP, width))
                        for g in range(per)
                    ],
                    axis=0,
                )
                grad = jnp.where(usable_rows(glen_ref, slab * (rows // GROUP) + b * per, block), grad, 0.0)
                dx, d_gain = norm_back(x2_ref[at, :], gain3_ref[...], grad)
                gain = gain + d_gain
                dx = dx + cot_ref[at, :].astype(F32)
                dx2_scr[at, :] = dx
                dy2_scr[at, :] = dx.astype(BF)
            ggain_ref[1:2, :] = gain
            da2_scr[...] = jnp.zeros_like(da2_scr)
            later[0].wait()

        @pl.when(step < last)
        def _():
            dact = mm(dy2_scr[...], w_ref[:, right], NT)
            dpre_scr[...] = (dact * slope_ref[...].astype(F32)).astype(BF)
            put(right, mm(act_ref[...], dy2_scr[...], TN))
            put(left, mm(a2_scr[...], dpre_scr[...], TN))
            da2_scr[...] = da2_scr[...] + mm(dpre_scr[...], w_ref[:, left], NT)

        @pl.when(step == last)
        def _():
            later[1].wait()
            later[2].wait()
            gain = jnp.zeros((1, width), F32)
            for b in range(rows // block):
                at = slice(b * block, (b + 1) * block)
                dx, d_gain = norm_back(x1_scr[at, :], gain2_ref[...], da2_scr[at, :])
                gain = gain + d_gain
                dx = dx + dx2_scr[at, :]
                dx1_ref[at, :] = dx
                dy2_scr[at, :] = dx.astype(BF)
            ggain_ref[0:1, :] = gain
            put(left, mm(mixed_scr[...], dy2_scr[...], TN))
            if second:
                g_ref[:, right] = ordered(gproj_ref[...]).astype(BF)
            dmixed_ref[...] = mm(dy2_scr[...], w_ref[:, left], NT).astype(BF)

    return kernel


def ffn_backward(
    slab, order, glen, x2, cot, dpool, x1, a2, mixed, act, slope, w_all, gain2, gain3, before, gproj
):
    rows, width = cot.shape[1:]
    chunks = w_all.shape[1] // (2 * width) - 1
    ff = chunks * width
    second = slab > 0
    side = pl.BlockSpec((rows, width), lambda i, _: (slab, jnp.minimum(i, chunks - 1)))
    once = pl.Buffered(1)
    mine = pl.BlockSpec((rows, width), lambda i, _: (slab, 0), pipeline_mode=once)
    part = pl.BlockSpec((width, 2 * width), lambda i, _: (0, i))
    in_specs = [
        mine,
        pl.BlockSpec((None, rows, width), lambda i, _: (slab, 0, 0), pipeline_mode=once),
        pl.BlockSpec((None,) + dpool.shape[1:], lambda i, _: (slab, 0, 0), pipeline_mode=once),
        pl.BlockSpec(memory_space=pl.ANY),
        pl.BlockSpec(memory_space=pl.ANY),
        pl.BlockSpec(memory_space=pl.ANY),
        side,
        side,
        part,
        fixed((1, width)),
        fixed((1, width)),
    ]
    operands = [x2, cot, dpool, x1, a2, mixed, act, slope, w_all, gain2, gain3]
    aliases = {}
    if second:
        in_specs += [part, fixed((width, width))] + [pl.BlockSpec(memory_space=pl.ANY)] * 2
        aliases = {len(operands) + 3: 1, len(operands) + 4: 2}
        operands += [before[0], gproj, before[1], before[2]]
    return pl.pallas_call(
        ffn_bwd_kernel(slab, order),
        grid_spec=pltpu.PrefetchScalarGridSpec(
            num_scalar_prefetch=1,
            grid=(chunks + 1,),
            in_specs=in_specs,
            out_specs=[
                part,
                mine,
                mine,
                fixed((2, width)),
            ],
            scratch_shapes=[
                pltpu.VMEM((rows, width), F32),
                pltpu.VMEM((rows, width), BF),
                pltpu.VMEM((rows, width), F32),
                pltpu.VMEM((rows, width), BF),
                pltpu.VMEM((rows, width), F32),
                pltpu.VMEM((rows, width), BF),
                pltpu.VMEM((rows, width), BF),
                pltpu.SemaphoreType.DMA((3,)),
            ],
        ),
        out_shape=[
            jax.ShapeDtypeStruct(w_all.shape, BF if second else F32),
            jax.ShapeDtypeStruct(x2.shape, F32),
            jax.ShapeDtypeStruct(x2.shape, BF),
            jax.ShapeDtypeStruct((2, width), F32),
        ],
        input_output_aliases=aliases,
        compiler_params=params(60),
        cost_estimate=cost(4 * rows * width * (width + 2 * ff), rows * width * 60),
        name="ffn_backward",
    )(glen, *operands)


def qkv_weight_kernel(a1_ref, d_ref, w_ref, g_ref, gain_ref):
    cols = d_ref.shape[2]
    total = mm(a1_ref[...], d_ref[0], TN)
    g_ref[...] = total.astype(BF)
    prod = total * w_ref[...].astype(F32)
    part = prod[:, 0:TILE]
    for lane in range(1, cols // TILE):
        part = part + prod[:, lane * TILE : (lane + 1) * TILE]

    @pl.when(pl.program_id(0) == 0)
    def _():
        gain_ref[...] = part

    @pl.when(pl.program_id(0) > 0)
    def _():
        gain_ref[...] = gain_ref[...] + part


def qkv_weight_grads(a1, d, w):
    rows, width = a1.shape
    col = pl.BlockSpec((width, width), lambda i: (0, i))
    return pl.pallas_call(
        qkv_weight_kernel,
        grid=(3,),
        in_specs=[
            fixed((rows, width)),
            pl.BlockSpec((1, rows, width), lambda i: (i, 0, 0)),
            col,
        ],
        out_specs=[col, fixed((width, TILE))],
        out_shape=[
            jax.ShapeDtypeStruct((width, 3 * width), BF),
            jax.ShapeDtypeStruct((width, TILE), F32),
        ],
        compiler_params=params(60),
        cost_estimate=cost(6 * rows * width * width, rows * width * 10),
        name="qkv_weight_grads",
    )(a1, d, w)


def qkv_input_kernel(x_ref, gain_ref, w_ref, dx1_ref, d_ref, out_ref):
    width = x_ref.shape[1]
    grad = mm(d_ref[0], w_ref[:, 0:width], NT)
    for i in (1, 2):
        grad = grad + mm(d_ref[i], w_ref[:, i * width : (i + 1) * width], NT)
    x = x_ref[...].astype(F32)
    r = lax.rsqrt(jnp.mean(x * x, axis=-1, keepdims=True) + 1e-06)
    hat = x * r
    d_hat = grad * gain_ref[...]
    dx = r * (d_hat - hat * jnp.mean(d_hat * hat, axis=-1, keepdims=True))
    out_ref[...] = dx + dx1_ref[...]


def qkv_input_grad(x, gain, w, d, dx1, slab, before):
    rows, width = x.shape
    block = 256
    steps = rows // MICRO // block
    first = slab * steps
    spec = pl.BlockSpec((block, width), lambda i: (first + i, 0))
    in_specs = [
        spec,
        fixed((1, width)),
        fixed(w.shape),
        spec,
        pl.BlockSpec((3, block, width), lambda i: (0, first + i, 0)),
    ]
    operands = [x, gain, w, dx1, d]
    kernel, aliases = qkv_input_kernel, {}
    if before is not None:
        aliases = {len(operands): 0}
        in_specs.append(pl.BlockSpec(memory_space=pl.ANY))
        operands.append(before)

        def kernel(*refs):
            qkv_input_kernel(*refs[:-2], refs[-1])

    return pl.pallas_call(
        kernel,
        grid=(steps,),
        in_specs=in_specs,
        out_specs=spec,
        out_shape=jax.ShapeDtypeStruct((rows, width), F32),
        input_output_aliases=aliases,
        compiler_params=params(60),
        cost_estimate=cost(6 * rows * width * width // MICRO, rows * width * 8),
        name="qkv_input_grad",
    )(*operands)


def bias_kernel(x_ref, near_ref):
    for head in range(x_ref.shape[0]):
        for delta in range(3):
            row = jnp.broadcast_to(x_ref[head, delta : delta + 1, :], (TILE, 2 * TILE))
            near_ref[head, delta] = pltpu.roll(row, 0, 1, stride=1, stride_axis=0)[:, :TILE]


def bias_tables(rel_bias, tiles):
    buckets, heads = rel_bias.shape
    lane = jnp.arange(2 * TILE, dtype=jnp.int32)
    back = jnp.where(lane < TILE, lane, lane - 2 * TILE)
    offsets = jnp.arange(-1, 2, dtype=jnp.int32)[:, None] * TILE - back[None, :]
    onehot = bucket_ids(offsets).reshape(1, -1) == jnp.arange(buckets, dtype=jnp.int32)[:, None]
    rows = jnp.einsum("bh,bn->hn", rel_bias, onehot.astype(F32), precision=lax.Precision.HIGHEST)
    near = pl.pallas_call(
        bias_kernel,
        grid=(2,),
        in_specs=[pl.BlockSpec((heads // 2, 3, 2 * TILE), lambda i: (i, 0, 0))],
        out_specs=pl.BlockSpec((heads // 2, 3, TILE, TILE), lambda i: (i, 0, 0, 0)),
        out_shape=jax.ShapeDtypeStruct((heads, 3, TILE, TILE), F32),
        name="bias_tables",
    )(rows.reshape(heads, 3, 2 * TILE))
    qb = jnp.arange(tiles)[:, None]
    kb = jnp.arange(tiles)[None, :]
    left = rel_bias[buckets // 2 - 1][:, None, None]
    right = rel_bias[buckets - 1][:, None, None]
    far = jnp.where(kb >= qb + 2, right, jnp.where(kb <= qb - 2, left, 0.0))
    high = far.astype(BF)
    rest = (far - high.astype(F32)).astype(BF)
    tags = jnp.concatenate(
        [
            jnp.ones((heads, tiles, 1), BF),
            high,
            rest,
            jnp.zeros((heads, tiles, TILE - 1 - 2 * tiles), BF),
        ],
        axis=2,
    )
    return near, tags


def bias_grad(sums, buckets):
    heads = sums.shape[0]
    lane = jnp.arange(2 * TILE, dtype=jnp.int32)
    offsets = jnp.arange(-1, 2, dtype=jnp.int32)[:, None] * TILE + lane[None, :] - (TILE - 1)
    left = jnp.full((1, 2 * TILE), buckets // 2 - 1, jnp.int32)
    right = jnp.full((1, 2 * TILE), buckets - 1, jnp.int32)
    ids = jnp.concatenate([bucket_ids(offsets), left, right]).reshape(-1, 1)
    onehot = ids == jnp.arange(buckets, dtype=jnp.int32)[None, :]
    return jnp.einsum(
        "hn,nb->bh",
        sums[:, :5].reshape(heads, -1),
        onehot.astype(F32),
        precision=lax.Precision.HIGHEST,
    )


def swap(x, axis):
    return lax.ppermute(x, axis, [(0, 1), (1, 0)])


def both_halves(x, axis):
    first = lax.axis_index(axis) == 0
    other = swap(x, axis)
    return jnp.stack([jnp.where(first, x, other), jnp.where(first, other, x)])


def ring_gather(x, axis):
    count = lax.axis_size(axis)
    if count > 4:
        return lax.all_gather(x, axis)
    me = lax.axis_index(axis)
    out = jnp.zeros((count,) + x.shape, x.dtype)
    out = lax.dynamic_update_index_in_dim(out, x, me, 0)
    for k in range(1, count):
        part = lax.ppermute(x, axis, [(j, (j + k) % count) for j in range(count)])
        out = lax.dynamic_update_index_in_dim(out, part, (me - k) % count, 0)
    return out


def quick_gather(x):
    columns = x.shape[-1]
    cut = columns // 2 // TILE * TILE
    line = ring_gather(x, "z")
    one = both_halves(both_halves(line[..., :cut], "x"), "tower")
    two = both_halves(both_halves(line[..., cut:], "tower"), "x")
    full = jnp.concatenate([one, jnp.swapaxes(two, 0, 1)], axis=-1)
    full = both_halves(full, "core")
    return jnp.transpose(full, (1, 3, 2, 0, 4, 5)).reshape(-1, columns)


def after(x, *earlier):
    return lax.optimization_barrier((x,) + earlier)[0]


def send_half(x, axis, dim):
    me = lax.axis_index(axis)
    keep = lax.dynamic_index_in_dim(x, me, dim, keepdims=False)
    return keep, swap(lax.dynamic_index_in_dim(x, 1 - me, dim, keepdims=False), axis)


def join(keep, got):
    return (keep.astype(F32) + got.astype(F32)).astype(BF)


def by_device(x):
    sizes = tuple(lax.axis_size(a) for a in ("tower", "z", "x", "core"))
    return x.reshape(sizes + (-1, x.shape[-1]))


def scatter_order(shard):
    t, z, x, c = (lax.axis_size(a) for a in AXES)
    if shard % 8:
        return tuple(range(t * z * x * c))
    return tuple(
        ((i * z + j) * x + k) * c + n
        for i in range(t)
        for k in range(x)
        for n in range(c)
        for j in range(z)
    )


def quick_scatter(x):
    half = x.shape[-1] // 2 // TILE * TILE
    keep, got = send_half(by_device(x), "core", 3)
    x = join(keep, after(got, *(yield keep)))
    keep1, got1 = send_half(x[..., :half], "tower", 0)
    keep2, got2 = send_half(x[..., half:], "x", 2)
    earlier = yield x
    one, two = join(keep1, after(got1, *earlier)), join(keep2, after(got2, *earlier))
    keep1, got1 = send_half(one, "x", 1)
    keep2, got2 = send_half(two, "tower", 0)
    earlier = yield one, two
    one, two = join(keep1, after(got1, *earlier)), join(keep2, after(got2, *earlier))
    x = jnp.concatenate([one, two], axis=-1)
    count = lax.axis_size("z")
    if count > 4:
        yield x
        yield lax.psum_scatter(x, "z", scatter_dimension=0, tiled=False).astype(F32)
    me = lax.axis_index("z")
    total = lax.dynamic_index_in_dim(x, me, 0, keepdims=False).astype(F32)
    parts = []
    for k in range(1, count):
        part = lax.dynamic_index_in_dim(x, (me + k) % count, 0, keepdims=False)
        parts.append(lax.ppermute(part, "z", [(j, (j + k) % count) for j in range(count)]))
    earlier = yield x
    for part in parts:
        total = total + after(part, *earlier).astype(F32)
    yield total


def broadcast(x):
    sent = jnp.broadcast_to(x[None], (lax.axis_size(AXES),) + x.shape)
    return lax.all_to_all(sent, AXES, 0, 0, tiled=True)


AXES = ("tower", "z", "x", "core")


def per_device(
    hidden,
    lengths,
    pairs,
    out_grad,
    w_query,
    w_key,
    w_value,
    w_attn_out,
    w_in,
    w_out,
    w_proj,
    gain_attn,
    gain_ffn,
    gain_final,
    rel_bias,
):
    devices = lax.axis_size(AXES)
    dp_count = devices // lax.axis_size("tower")
    is_doc = lax.axis_index("tower") == 1
    query_side = jnp.where(is_doc, 0.0, 1.0).astype(F32)
    rows, width = hidden.shape[3:]
    slots = lengths.shape[3]
    buckets, heads = rel_bias.shape
    shard, ff = w_in.shape
    chunks = ff // width
    first_slot = (jnp.arange(slots) == 0)[:, None]
    gain1, gain2, gain3 = gain_attn[None], gain_ffn[None], gain_final[None]
    x_all = hidden[0, 0].reshape(MICRO * rows, width)

    w_in = w_in.reshape(shard, devices, chunks, shard).swapaxes(1, 2).reshape(shard, ff)
    pieces = []
    for c in range(chunks):
        pieces.append(w_in[:, c * width : (c + 1) * width])
        pieces.append(w_out[c * shard : (c + 1) * shard])
    wqkv = quick_gather(jnp.concatenate([w_query, w_key, w_value], axis=1))
    w_all = lax.all_gather(
        jnp.concatenate(pieces + [w_attn_out, w_proj], axis=1), AXES, axis=0, tiled=True
    )
    w_proj_all = w_all[:, -width:]

    near_bias, tags = bias_tables(rel_bias, rows // TILE)
    room = jnp.maximum(60.0 - jnp.max(jnp.abs(rel_bias)), 0.0).reshape(1, 1)
    a1, qkv, small = project_qkv(room, x_all, gain1, wqkv)
    lens = lengths[0, 0]
    groups = jnp.arange(rows // GROUP, dtype=jnp.int32)
    per_group = jnp.clip(lens[:, 0:1] - GROUP * groups[None], 0, GROUP)
    glen = jnp.where(is_doc, per_group, lens).astype(jnp.int32)
    flag = jnp.broadcast_to(is_doc.astype(jnp.int32), (MICRO, 1))
    info = jnp.concatenate([flag, lens[:, 0:1], glen], axis=1)
    glen = glen.reshape(-1)
    mixed, probs, linv = attention(info, small, qkv, tags, near_bias, heads)
    x1, a2, act, slope, x2, out, pool = ffn_forward(
        glen, x_all, mixed, w_all, gain2, gain3
    )
    pool = pool.reshape(MICRO, rows // GROUP, width)
    counts = jnp.maximum(lengths[0, 0].astype(F32), 1.0)[..., None]
    doc_pool = jnp.where(first_slot, jnp.sum(pool, axis=1, keepdims=True), 0.0)
    pooled = (jnp.where(is_doc, doc_pool, pool) / counts).astype(BF)
    projected = jnp.dot(
        pooled.reshape(MICRO * slots, width), w_proj_all, preferred_element_type=F32
    ).reshape(MICRO, slots, width)
    unit_vec, unit_pull = jax.vjp(unit_norm, projected)
    unit_low = unit_vec.astype(BF)
    sent = jnp.broadcast_to(unit_low[None, :, 0].astype(F32), (devices, MICRO, width))
    docs = lax.optimization_barrier(lax.all_to_all(sent, AXES, 0, 0, tiled=True))
    docs = docs[dp_count:].astype(BF)
    logits = (
        jnp.einsum("msd,bmd->msb", unit_low, docs, preferred_element_type=F32) * logit_scale
    )
    row_max = jnp.max(logits, axis=-1, keepdims=True)
    log_total = row_max + jnp.log(jnp.sum(jnp.exp(logits - row_max), axis=-1, keepdims=True))
    chosen_mask = jnp.arange(dp_count, dtype=jnp.int32) == pairs[:, 0, :, None]
    chosen = jnp.sum(jnp.where(chosen_mask, logits, 0.0), axis=-1)
    loss_part = jnp.sum(log_total[..., 0] - chosen) * query_side
    logit_grad = (
        (jnp.exp(logits - log_total) - chosen_mask.astype(F32)) * query_side
    ).astype(BF)
    unit_grad = (
        jnp.einsum("msb,bmd->msd", logit_grad, docs, preferred_element_type=F32) * logit_scale
    )
    docs_grad = (
        jnp.einsum("msb,msd->bmd", logit_grad, unit_low, preferred_element_type=F32) * logit_scale
    )
    back = jnp.concatenate([jnp.zeros_like(docs_grad), docs_grad], axis=0)
    returned = jnp.sum(lax.all_to_all(back, AXES, 0, 0, tiled=True)[:dp_count], axis=0)
    unit_grad = unit_grad + jnp.where(first_slot & is_doc, returned[:, None], 0.0)
    proj_grad_in = unit_pull(unit_grad)[0].astype(BF)
    flat = proj_grad_in.reshape(MICRO * slots, width)
    grad_proj = mm(pooled.reshape(MICRO * slots, width), flat, TN)
    dpooled = jnp.dot(flat, w_proj_all.T, preferred_element_type=F32)
    dpooled = dpooled.reshape(MICRO, slots, width) / counts
    dpool = jnp.where(is_doc, jnp.broadcast_to(dpooled[:, 0:1], dpooled.shape), dpooled)

    order = scatter_order(shard)
    backs, ggains = None, 0.0
    for m in range(MICRO):
        *backs, ggain = ffn_backward(
            m,
            order,
            glen,
            x2,
            out_grad[0, 0],
            dpool,
            x1,
            a2,
            mixed,
            act,
            slope,
            w_all,
            gain2,
            gain3,
            backs,
            grad_proj,
        )
        ggains = ggains + ggain
    grads, dx1, d_mixed = backs

    if shard % 8:
        grad_all = lax.psum_scatter(grads, AXES, scatter_dimension=0, tiled=True).astype(F32)
    else:
        inner = lax.psum_scatter(grads, ("tower", "x", "core"), scatter_dimension=0, tiled=True)
    dqkv, bias_sums = attention_back(info, qkv, mixed, d_mixed, probs, linv)
    bias_sums = jnp.sum(bias_sums.reshape((MICRO, heads) + bias_sums.shape[1:]), axis=0)
    bias_part = bias_grad(bias_sums, buckets)
    piece, gain_part = qkv_weight_grads(a1, after(dqkv, bias_part), wqkv)
    if shard % 8 == 0:
        piece = after(piece, inner)
        grad_all = lax.psum_scatter(inner, "z", scatter_dimension=0, tiled=True).astype(F32)
    flow = quick_scatter(piece)
    sent = next(flow)
    ggain1 = jnp.sum(gain_part, axis=1) / gain_attn
    row = lax.broadcasted_iota(jnp.int32, (4, width), 0)
    lane = lax.broadcasted_iota(jnp.int32, (4, width), 1)
    used = buckets * heads
    bias_row = jnp.pad(bias_part.reshape(1, -1), ((0, 0), (0, width - used)))
    smalls = jnp.where(lane == used, loss_part, bias_row)
    for at, part in enumerate((ggain1[None], ggains[0:1], ggains[1:2])):
        smalls = jnp.where(row == at, part, smalls)
    everywhere = broadcast(smalls)
    totals = jnp.sum(everywhere, axis=0)
    sent = flow.send((totals,))
    input_grads = qkv_input_grad(x_all, gain1, wqkv, dqkv, after(dx1, sent), 0, None)
    sent = flow.send((input_grads,))
    input_grads = qkv_input_grad(x_all, gain1, wqkv, dqkv, after(dx1, *sent), 1, input_grads)
    flow.send((input_grads,))
    grad_in = jnp.concatenate(
        [grad_all[:, 2 * c * width : (2 * c + 1) * width] for c in range(chunks)], axis=1
    )
    grad_in = grad_in.reshape(shard, chunks, devices, shard).swapaxes(1, 2).reshape(shard, ff)
    grad_out = jnp.concatenate(
        [grad_all[:, (2 * c + 1) * width : (2 * c + 2) * width] for c in range(chunks)], axis=0
    )
    grad_wo = grad_all[:, 2 * ff : 2 * ff + width]
    grad_proj = grad_all[:, 2 * ff + width :]

    grad_qkv = flow.send((grad_in,)).reshape(shard, 3, width)
    return (
        out.reshape(hidden.shape),
        input_grads.reshape(hidden.shape),
        totals[3, used] / (dp_count * slots * MICRO),
        grad_qkv[:, 0],
        grad_qkv[:, 1],
        grad_qkv[:, 2],
        grad_wo,
        grad_in,
        grad_out,
        grad_proj,
        totals[0],
        totals[1],
        totals[2],
        totals[3, :used].reshape(buckets, heads),
    )


def solution(mesh):
    towers, per_tower = mesh.devices.shape
    fine = Mesh(mesh.devices.reshape(towers, per_tower // 4, 2, 2), AXES)
    dp = AXES[1:]
    rows = P(AXES, None)
    slabs = P("tower", dp, None, None, None)
    return jax.shard_map(
        per_device,
        mesh=fine,
        in_specs=(slabs, P("tower", dp, None, None), P(None, dp, None), slabs)
        + (rows,) * 7
        + (P(),) * 4,
        out_specs=(slabs, slabs, P()) + (rows,) * 7 + (P(),) * 4,
        check_vma=False,
    )
```
